128 devices in a mesh: pipe: 4 (over y_lo, core), dp: 32 (over y_hi, z, x).
Axes of the slice: x: 4, y: 4 (y_hi: 2, y_lo: 2; y = y_hi * 2 + y_lo), z: 4, core: 2. Of those that a mesh axis runs over, the one named last changes fastest.
Arguments:
- enc_in: bfloat16 [64, 128, 2048], P('dp'), may hold values from -6 to 6
- dec_in: bfloat16 [64, 32, 2048], P('dp'), may hold values from -6 to 6
- out_grad: bfloat16 [64, 32, 2048], P('dp'), may hold values from -6 to 6
- enc_weight: bfloat16 [4, 2048, 2048], P('pipe'), may hold values from -0.125 to 0.125
- dec_weight: bfloat16 [4, 2048, 2048], P('pipe'), may hold values from -0.125 to 0.125
- enc_gain: float32 [4, 2048], P('pipe'), may hold values from 0.25 to 1.75
- dec_gain: float32 [4, 2048], P('pipe'), may hold values from 0.25 to 1.75
- mem_gain: float32 [2048], replicated, may hold values from 0.1 to 1.9
Outputs:
- enc_weight_grad: float32 [4, 2048, 2048], P('pipe', 'dp')
- dec_weight_grad: float32 [4, 2048, 2048], P('pipe', 'dp')
- enc_gain_grad: float32 [4, 2048], P('pipe', 'dp')
- dec_gain_grad: float32 [4, 2048], P('pipe', 'dp')
The draws below stay inside these ranges and needn't reach their ends.
All inputs are finite; a program needn't handle non-finite values.
Results may differ from the reference program's by a relative error of at most 0.034.
Values may be sent and summed in bfloat16 or wider, within the bound.
No kernel may reach another device: no remote copies, remote signals or barrier semaphores. Data moves between devices by JAX's collectives and lax.ppermute only.
A program may use at most 128 MiB of HBM per device.

```python
import jax
import jax.numpy as jnp
from jax import lax

D = 2048
HEAD_DIM = 256
HEADS = 8
MICRO = 2
ENC_LEN = 128
DEC_LEN = 32
SECTIONS = 4
BATCH = 64
N_DP = 32


def with_spikes(values, own_key, source, target, parts, factor):
    owner, partner = [(jnp.arange(values.shape[dim]) // (values.shape[dim] // parts)).reshape([-1 if axis == dim else 1 for axis in range(values.ndim)]) for dim in (source, target)]
    chosen = jax.random.permutation(own_key, parts)[partner]
    strong = (owner == chosen) | (owner == (partner + parts // 2) % parts)
    return jnp.where(strong, factor * values, values)


def level_of(own_key, extent, shards, low, high):
    loudness, own = 1.0, jax.random.fold_in(own_key, 6)
    for position, parts in shards:
        heights = jnp.exp(jax.random.uniform(jax.random.fold_in(own, position), (parts,), jnp.float32, low / len(shards), high / len(shards)))
        loudness = loudness * jnp.repeat(heights, extent[position] // parts).reshape([-1 if axis == position else 1 for axis in range(len(extent))])
    return loudness


def normal_values(key, dims, scale, bound, cuts=(), kind=jnp.bfloat16):
    drawn = scale * jax.random.normal(key, dims, jnp.float32)
    if cuts:
        drawn = drawn * level_of(key, dims, cuts, -0.22, 0.18)
    return jnp.clip(drawn, -bound, bound).astype(kind)


def noise_with(rng, shape, spread, limit, split, heavy, kind=jnp.bfloat16):
    entries = spread * jax.random.normal(rng, shape, jnp.float32)
    if split:
        entries = entries * level_of(rng, shape, split, -0.22, 0.18)
    return jnp.clip(with_spikes(entries, jax.random.fold_in(rng, 3), *heavy), -limit, limit).astype(kind)


def setup_inputs(seed: int = 0) -> dict:
    splits = jax.random.split(jax.random.key(seed), 9)
    return {
        "enc_in": noise_with(splits[0], (BATCH, ENC_LEN, D), 1.0, 6.0, ((0, 32),), (0, 2, 32, 2.75)),
        "dec_in": noise_with(splits[1], (BATCH, DEC_LEN, D), 1.0, 6.0, ((0, 32),), (0, 2, 32, 2.75)),
        "out_grad": normal_values(splits[2], (BATCH, DEC_LEN, D), 1.0, 6.0, ((0, 32),)),
        "enc_weight": normal_values(splits[3], (SECTIONS, D, D), D ** -0.5, 0.125, ((0, 4),)),
        "dec_weight": normal_values(splits[4], (SECTIONS, D, D), D ** -0.5, 0.125, ((0, 4),)),
        "enc_gain": jnp.clip(1.0 + 0.15 * jax.random.normal(splits[5], (SECTIONS, D), jnp.float32), 0.25, 1.75),
        "dec_gain": jnp.clip(1.0 + 0.15 * jax.random.normal(splits[6], (SECTIONS, D), jnp.float32), 0.25, 1.75),
        "mem_gain": jnp.clip(1.0 + 0.18 * jax.random.normal(splits[7], (D,), jnp.float32), 0.1, 1.9),
    }


EPSILON = 1e-06
QUERY_SCALE = 0.0625

def product(form, left_side, right_side):
    return jnp.einsum(form, left_side.astype(jnp.float32), right_side.astype(jnp.float32), precision=lax.Precision.HIGHEST)

def row_scale(values):
    return lax.rsqrt(lax.optimization_barrier(jnp.mean(values * values, axis=-1, keepdims=True)) + EPSILON)

def to_heads(values):
    return values.reshape(values.shape[0], HEADS, HEAD_DIM)

def attend(hidden, norm_gain, weight, memory):
    hidden_float = hidden.astype(jnp.float32)
    row_scales = row_scale(hidden_float)
    normed = (hidden_float * row_scales * norm_gain).astype(jnp.bfloat16)
    source = normed if memory is None else memory
    queries = (jnp.dot(normed, weight, preferred_element_type=jnp.float32) * QUERY_SCALE).astype(jnp.bfloat16)
    scores = product('lhd,shd->hls', to_heads(queries), to_heads(source))
    raised = jnp.exp(scores)
    weights_float = raised / lax.optimization_barrier(jnp.sum(raised, axis=-1, keepdims=True))
    return (hidden_float, row_scales, normed, source, queries, weights_float, weights_float.astype(jnp.bfloat16))

def forward(hidden, norm_gain, weight, memory):
    hidden_float, row_scales, normed, source, queries, weights_float, weights_low = attend(hidden, norm_gain, weight, memory)
    mixture = product('hls,shd->lhd', weights_low, to_heads(source)).reshape(hidden.shape)
    return (hidden_float + mixture).astype(jnp.bfloat16)

def backward(hidden, norm_gain, weight, memory, upstream):
    hidden_float, row_scales, normed, source, queries, weights_float, weights_low = attend(hidden, norm_gain, weight, memory)
    up_heads = to_heads(upstream)
    source_heads = to_heads(source)
    grad_probs = product('lhd,shd->hls', up_heads, source_heads)
    grad_values = product('hls,lhd->shd', weights_low, up_heads)
    grad_scores = (weights_float * (grad_probs - lax.optimization_barrier(jnp.sum(grad_probs * weights_float, axis=-1, keepdims=True)))).astype(jnp.bfloat16)
    grad_query = product('hls,shd->lhd', grad_scores, source_heads).reshape(queries.shape)
    grad_query = (grad_query * QUERY_SCALE).astype(jnp.bfloat16)
    grad_keys = product('hls,lhd->shd', grad_scores, to_heads(queries))
    grad_source = (grad_keys + grad_values).reshape(source.shape)
    grad_normed = jnp.dot(grad_query, weight.T, preferred_element_type=jnp.float32)
    if memory is None:
        grad_normed = grad_normed + grad_source
    scaled = norm_gain * grad_normed
    grad_input = upstream.astype(jnp.float32) + row_scales * scaled - hidden_float * row_scales ** 3 * lax.optimization_barrier(jnp.mean(scaled * hidden_float, axis=-1, keepdims=True))
    gain_term = lax.optimization_barrier(jnp.sum(grad_normed * hidden_float * row_scales, axis=0))
    return (grad_input.astype(jnp.bfloat16), normed, grad_query, gain_term, grad_source)

def memory_of(hidden, norm_gain):
    hidden_float = hidden.astype(jnp.float32)
    return (hidden_float * row_scale(hidden_float) * norm_gain).astype(jnp.bfloat16)

def memory_back(hidden, norm_gain, grad_memory):
    hidden_float = hidden.astype(jnp.float32)
    row_scales = row_scale(hidden_float)
    scaled = norm_gain * grad_memory
    result = row_scales * scaled - hidden_float * row_scales ** 3 * lax.optimization_barrier(jnp.mean(scaled * hidden_float, axis=-1, keepdims=True))
    return result.astype(jnp.bfloat16)

def reference(enc_in, dec_in, out_grad, enc_weight, dec_weight, enc_gain, dec_gain, mem_gain):

    def one_shard(totals, shard_index):
        first_row = shard_index * MICRO
        enc_rows = lax.dynamic_slice_in_dim(enc_in, first_row, MICRO, 0)
        dec_rows = lax.dynamic_slice_in_dim(dec_in, first_row, MICRO, 0)
        grad_rows = lax.dynamic_slice_in_dim(out_grad, first_row, MICRO, 0)
        enc_w_terms = [jnp.zeros((D, D), jnp.float32) for layer_index in range(SECTIONS)]
        dec_w_terms = [jnp.zeros((D, D), jnp.float32) for layer_index in range(SECTIONS)]
        enc_g_terms = [jnp.zeros((D,), jnp.float32) for layer_index in range(SECTIONS)]
        dec_g_terms = [jnp.zeros((D,), jnp.float32) for layer_index in range(SECTIONS)]
        for sequence in range(MICRO):
            hidden = enc_rows[sequence]
            enc_inputs = []
            for layer_index in range(SECTIONS):
                enc_inputs.append(hidden)
                hidden = forward(hidden, enc_gain[layer_index], enc_weight[layer_index], None)
            memory = memory_of(hidden, mem_gain)
            target = dec_rows[sequence]
            dec_inputs = []
            for layer_index in range(SECTIONS):
                dec_inputs.append(target)
                target = forward(target, dec_gain[layer_index], dec_weight[layer_index], memory)
            upstream = grad_rows[sequence]
            memory_grad = jnp.zeros(memory.shape, jnp.float32)
            for layer_index in reversed(range(SECTIONS)):
                upstream, normed, grad_query, gain_term, grad_source = backward(dec_inputs[layer_index], dec_gain[layer_index], dec_weight[layer_index], memory, upstream)
                dec_w_terms[layer_index] = dec_w_terms[layer_index] + jnp.dot(normed.T, grad_query, preferred_element_type=jnp.float32)
                dec_g_terms[layer_index] = dec_g_terms[layer_index] + gain_term
                memory_grad = memory_grad + grad_source
            upstream = memory_back(hidden, mem_gain, memory_grad)
            for layer_index in reversed(range(SECTIONS)):
                upstream, normed, grad_query, gain_term, grad_source = backward(enc_inputs[layer_index], enc_gain[layer_index], enc_weight[layer_index], None, upstream)
                enc_w_terms[layer_index] = enc_w_terms[layer_index] + jnp.dot(normed.T, grad_query, preferred_element_type=jnp.float32)
                enc_g_terms[layer_index] = enc_g_terms[layer_index] + gain_term
        partials = (jnp.stack(enc_w_terms), jnp.stack(dec_w_terms), jnp.stack(enc_g_terms), jnp.stack(dec_g_terms))
        updated = tuple((total + lax.optimization_barrier(partial_sum.astype(jnp.bfloat16)).astype(jnp.float32) for total, partial_sum in zip(totals, partials)))
        return (updated, None)
    initial = (jnp.zeros((SECTIONS, D, D), jnp.float32), jnp.zeros((SECTIONS, D, D), jnp.float32), jnp.zeros((SECTIONS, D), jnp.float32), jnp.zeros((SECTIONS, D), jnp.float32))
    totals, unused = lax.scan(one_shard, initial, jnp.arange(N_DP, dtype=jnp.int32))
    return (totals[0], totals[1], totals[2], totals[3])
```

```python
import functools

import jax
import jax.numpy as jnp
from jax import lax
from jax.experimental import pallas as pl
from jax.experimental.pallas import tpu as pltpu
from jax.sharding import PartitionSpec as P

HEAD_DIM = 256
EPSILON = 1e-06
QUERY_SCALE = 0.0625
EXTRA_ROWS = 16
GAIN_LANES = 128

BF16 = jnp.bfloat16
F32 = jnp.float32
ANY = pl.BlockSpec(memory_space=pl.ANY)
SMEM = pl.BlockSpec(memory_space=pltpu.SMEM)
VMEM = pl.BlockSpec(memory_space=pltpu.VMEM)
PARAMS = pltpu.CompilerParams(vmem_limit_bytes=48 * 2**20)


def dot(left, right):
    return jnp.dot(left, right, preferred_element_type=F32)


def dot_nt(left, right):
    return lax.dot_general(left, right, (((1,), (1,)), ((), ())), preferred_element_type=F32)


def dot_tn(left, right):
    return lax.dot_general(left, right, (((0,), (0,)), ((), ())), preferred_element_type=F32)


def row_scale(values):
    return lax.rsqrt(jnp.mean(values * values, axis=-1, keepdims=True) + EPSILON)


def head(index):
    return slice(index * HEAD_DIM, (index + 1) * HEAD_DIM)


def weight_copy(source, buffer, sems, slot, part, by_rows):
    where = (head(part), slice(None)) if by_rows else (slice(None), head(part))
    return pltpu.make_async_copy(source.at[where], buffer.at[(slot,) + where], sems.at[slot, part])


def start_weights(core, own, other, buffer, sems, slots, by_rows):
    parts = own.shape[0] // HEAD_DIM
    for mine in (0, 1):

        @pl.when(core == mine)
        def _():
            for slot in slots:
                for part in range(parts):
                    weight_copy(own if slot == mine else other, buffer, sems, slot, part, by_rows).start()


def waiter(own, buffer, sems, slot, by_rows):
    return lambda part: weight_copy(own, buffer, sems, slot, part, by_rows).wait()


def sub_forward(x, gain, weight, wait, normed, source, query, probs, out):
    hidden = x[...].astype(F32)
    normed[...] = (hidden * row_scale(hidden) * gain).astype(BF16)
    source = normed if source is None else source
    for part in range(x.shape[-1] // HEAD_DIM):
        cols = head(part)
        wait(part)
        queries = (dot(normed[...], weight[:, cols]) * QUERY_SCALE).astype(BF16)
        if query is not None:
            query[:, cols] = queries
        raised = jnp.exp(dot_nt(queries, source[:, cols]))
        shares = raised / jnp.sum(raised, axis=-1, keepdims=True)
        if probs is not None:
            probs[part] = shares
        if out is not None:
            mixture = dot(shares.astype(BF16), source[:, cols])
            out[:, cols] = (x[:, cols].astype(F32) + mixture).astype(BF16)


def attend_backward(source, query, probs, upstream, grad_query, grad_source, add):
    for part in range(source.shape[-1] // HEAD_DIM):
        cols = head(part)
        shares = probs[part]
        up = upstream[:, cols]
        grad_probs = dot_nt(up, source[:, cols])
        values = dot_tn(shares.astype(BF16), up)
        scores = (shares * (grad_probs - jnp.sum(grad_probs * shares, axis=-1, keepdims=True))).astype(BF16)
        grad_query[:, cols] = (dot(scores, source[:, cols]) * QUERY_SCALE).astype(BF16)
        total = dot_tn(scores, query[:, cols]) + values
        grad_source[:, cols] = grad_source[:, cols] + total if add else total


def input_backward(x, gain, weight, wait, grad_query, grad_source, upstream, scaled, out):
    width = x.shape[-1]
    hidden = x[...].astype(F32)
    scales = row_scale(hidden)
    total = jnp.zeros((x.shape[0], 1), F32)
    for part in range(width // HEAD_DIM):
        cols = head(part)
        wait(part)
        grad = gain[:, cols] * dot_nt(grad_query[...], weight[cols, :])
        if grad_source is not None:
            grad = grad + gain[:, cols] * grad_source[:, cols]
        scaled[:, cols] = grad
        total = total + jnp.sum(grad * x[:, cols].astype(F32), axis=-1, keepdims=True)
    factor = scales * scales * scales * (total / width)
    out[...] = (upstream[...].astype(F32) + scales * scaled[...] - hidden * factor).astype(BF16)


def gain_row(x, grad_source):
    hidden = x[...].astype(F32)
    return jnp.sum(grad_source[...] * hidden * row_scale(hidden), axis=0, keepdims=True)


def first_kernel(x_any, weight_any, gain, out, x, weight, normed, weight_sems, sem):
    for part in range(weight_any.shape[0] // HEAD_DIM):
        weight_copy(weight_any, weight, weight_sems, 0, part, False).start()
    rows = pltpu.make_async_copy(x_any, x, sem)
    rows.start()
    rows.wait()
    wait = waiter(weight_any, weight, weight_sems, 0, False)
    count, length, width = x.shape
    for sequence in range(count):
        hidden = x[sequence].astype(F32)
        normed[sequence * length : (sequence + 1) * length] = (hidden * row_scale(hidden) * gain[...]).astype(BF16)
    for part in range(width // HEAD_DIM):
        cols = head(part)
        wait(part)
        queries = (dot(normed[...], weight[0, :, cols]) * QUERY_SCALE).astype(BF16)
        for sequence in range(count):
            rows = slice(sequence * length, (sequence + 1) * length)
            source = normed[rows, cols]
            raised = jnp.exp(dot_nt(queries[rows], source))
            shares = raised / jnp.sum(raised, axis=-1, keepdims=True)
            mixture = dot(shares.astype(BF16), source)
            out[sequence, :, cols] = (x[sequence, :, cols].astype(F32) + mixture).astype(BF16)


def first_call(x, weight, gain):
    count, length, width = x.shape
    return pl.pallas_call(
        first_kernel,
        name="enc_first",
        out_shape=jax.ShapeDtypeStruct(x.shape, BF16),
        in_specs=[ANY, ANY, VMEM],
        out_specs=VMEM,
        scratch_shapes=[
            pltpu.VMEM(x.shape, BF16),
            pltpu.VMEM((1, width, width), BF16),
            pltpu.VMEM((count * length, width), BF16),
            pltpu.SemaphoreType.DMA((1, width // HEAD_DIM)),
            pltpu.SemaphoreType.DMA,
        ],
        compiler_params=PARAMS,
    )(x, weight, gain)


def enc_forward_kernel(
    flags, x_any, recv_any, own, other, gains, mem_gain, mem, *rest
):
    outs, (weight, weight_sems, sem, out_sems, *held) = rest[:9], rest[9:]
    x0, x1, x2, n0, n1, q0, q1, p0, p1 = held
    core, upper = flags[0], flags[1]
    start_weights(core, own, other, weight, weight_sems, (0, 1), False)

    @pl.when(upper == 0)
    def _():
        pltpu.make_async_copy(x_any.at[core], x0, sem).start()

    @pl.when(upper == 1)
    def _():
        pltpu.make_async_copy(recv_any, x0, sem).start()

    pltpu.make_async_copy(recv_any, x0, sem).wait()

    def flush(*places):
        for place in places:
            pltpu.make_async_copy(held[place], outs[place], out_sems.at[place]).start()

    sub_forward(x0, gains[0:1], weight.at[0], waiter(own, weight, weight_sems, 0, False), n0, None, q0, p0, x1)
    flush(0, 1, 3, 5, 7)
    sub_forward(x1, gains[1:2], weight.at[1], waiter(own, weight, weight_sems, 1, False), n1, None, q1, p1, x2)
    flush(2, 4, 6, 8)
    hidden = x2[...].astype(F32)
    mem[...] = (hidden * row_scale(hidden) * mem_gain[...]).astype(BF16)
    for place in range(9):
        pltpu.make_async_copy(held[place], outs[place], out_sems.at[place]).wait()


def enc_forward_call(flags, x, received, own, other, gains, mem_gain):
    length, width = received.shape
    heads = width // HEAD_DIM
    kinds = [((length, width), BF16)] * 7 + [((heads, length, length), F32)] * 2
    results = pl.pallas_call(
        enc_forward_kernel,
        name="enc_forward",
        out_shape=[jax.ShapeDtypeStruct((length, width), BF16)] + [jax.ShapeDtypeStruct(*kind) for kind in kinds],
        in_specs=[SMEM, ANY, ANY, ANY, ANY, VMEM, VMEM],
        out_specs=[VMEM] + [ANY] * 9,
        scratch_shapes=[
            pltpu.VMEM((2, width, width), BF16),
            pltpu.SemaphoreType.DMA((2, heads)),
            pltpu.SemaphoreType.DMA,
            pltpu.SemaphoreType.DMA((9,)),
        ]
        + [pltpu.VMEM(*kind) for kind in kinds],
        compiler_params=PARAMS,
    )(flags, x, received, own, other, gains, mem_gain)
    return results[0], results[1:]


def dec_forward_kernel(flags, x_any, memory, own, other, gains, y1, y2, n0, n1, q0, q1, p0, p1, weight, weight_sems, sem, y0):
    core = flags[0]
    start_weights(core, own, other, weight, weight_sems, (0, 1), False)
    rows = pltpu.make_async_copy(x_any.at[core], y0, sem)
    rows.start()
    rows.wait()
    sub_forward(y0, gains[0:1], weight.at[0], waiter(own, weight, weight_sems, 0, False), n0, memory, q0, p0, y1)
    sub_forward(y1, gains[1:2], weight.at[1], waiter(own, weight, weight_sems, 1, False), n1, memory, q1, p1, y2)


def dec_forward_call(flags, x, memory, own, other, gains):
    length, width = x.shape[1:]
    heads = width // HEAD_DIM
    row = jax.ShapeDtypeStruct((length, width), BF16)
    share = jax.ShapeDtypeStruct((heads, length, memory.shape[0]), F32)
    return pl.pallas_call(
        dec_forward_kernel,
        name="dec_forward",
        out_shape=[row] * 6 + [share] * 2,
        in_specs=[SMEM, ANY, VMEM, ANY, ANY, VMEM],
        out_specs=[VMEM] * 8,
        scratch_shapes=[
            pltpu.VMEM((2, width, width), BF16),
            pltpu.SemaphoreType.DMA((2, heads)),
            pltpu.SemaphoreType.DMA,
            pltpu.VMEM((length, width), BF16),
        ],
        compiler_params=PARAMS,
    )(flags, x, memory, own, other, gains)


def dec_turn_kernel(
    flags, y2, memory, upstream, own, other, gains, out, grad_source, dq0, dq1, n0, n1, weight, weight_sems, y3, u3, q0, q1, p0, p1, scaled
):
    start_weights(flags[0], own, other, weight, weight_sems, (0, 1), False)
    no_wait = lambda part: None
    sub_forward(y2, gains[0:1], weight.at[0], waiter(own, weight, weight_sems, 0, False), n0, memory, q0, p0, y3)
    sub_forward(y3, gains[1:2], weight.at[1], waiter(own, weight, weight_sems, 1, False), n1, memory, q1, p1, None)
    attend_backward(memory, q1, p1, upstream, dq1, grad_source, False)
    input_backward(y3, gains[1:2], weight.at[1], no_wait, dq1, None, upstream, scaled, u3)
    attend_backward(memory, q0, p0, u3, dq0, grad_source, True)
    input_backward(y2, gains[0:1], weight.at[0], no_wait, dq0, None, u3, scaled, out)


def dec_turn_call(flags, y2, memory, upstream, own, other, gains):
    length, width = y2.shape
    heads = width // HEAD_DIM
    row = jax.ShapeDtypeStruct((length, width), BF16)
    return pl.pallas_call(
        dec_turn_kernel,
        name="dec_turn",
        out_shape=[row, jax.ShapeDtypeStruct(memory.shape, F32)] + [row] * 4,
        in_specs=[SMEM, VMEM, VMEM, VMEM, ANY, ANY, VMEM],
        out_specs=[VMEM] * 6,
        scratch_shapes=[
            pltpu.VMEM((2, width, width), BF16),
            pltpu.SemaphoreType.DMA((2, heads)),
            pltpu.VMEM((length, width), BF16),
            pltpu.VMEM((length, width), BF16),
            pltpu.VMEM((length, width), BF16),
            pltpu.VMEM((length, width), BF16),
            pltpu.VMEM((heads, length, memory.shape[0]), F32),
            pltpu.VMEM((heads, length, memory.shape[0]), F32),
            pltpu.VMEM((length, width), F32),
        ],
        compiler_params=PARAMS,
    )(flags, y2, memory, upstream, own, other, gains)


def dec_backward_kernel(
    flags, upstream, memory, y1, q0, q1, p0, p1, own, other, gains, dq0, dq1, source_low, weight, weight_sems, u1, grad_source, scaled
):
    start_weights(flags[0], own, other, weight, weight_sems, (1,), True)
    attend_backward(memory, q1, p1, upstream, dq1, grad_source, False)
    input_backward(y1, gains[1:2], weight.at[1], waiter(own, weight, weight_sems, 1, True), dq1, None, upstream, scaled, u1)
    attend_backward(memory, q0, p0, u1, dq0, grad_source, True)
    source_low[...] = grad_source[...].astype(BF16)


def dec_backward_call(flags, upstream, memory, y1, q0, q1, p0, p1, own, other, gains):
    length, width = upstream.shape
    heads = width // HEAD_DIM
    row = jax.ShapeDtypeStruct((length, width), BF16)
    return pl.pallas_call(
        dec_backward_kernel,
        name="dec_backward",
        out_shape=[row, row, jax.ShapeDtypeStruct(memory.shape, BF16)],
        in_specs=[SMEM] + [VMEM] * 7 + [ANY, ANY, VMEM],
        out_specs=[VMEM] * 3,
        scratch_shapes=[
            pltpu.VMEM((2, width, width), BF16),
            pltpu.SemaphoreType.DMA((2, heads)),
            pltpu.VMEM((length, width), BF16),
            pltpu.VMEM(memory.shape, F32),
            pltpu.VMEM((length, width), F32),
        ],
        compiler_params=PARAMS,
    )(flags, upstream, memory, y1, q0, q1, p0, p1, own, other, gains)


def put_payload(payload, grad_query, x, grad_source):
    length, width = grad_query.shape
    payload[0:length] = grad_query[...]
    place = lax.broadcasted_iota(jnp.int32, (EXTRA_ROWS, width), 0)
    payload[length:] = jnp.where(place == 0, gain_row(x, grad_source), 0.0).astype(BF16)


def enc_backward_kernel(first, flags, *refs):
    if first:
        source_mine, source_recv, mem_gain = refs[:3]
        refs = refs[3:]
    else:
        upstream, done0, done1 = refs[:3]
        refs = refs[3:]
    own, other, gains = refs[:3]
    saved_any = refs[3:12]
    if first:
        out, pay0, pay1 = refs[12:15]
    else:
        pay_own, pay_other = refs[12:14]
        pay0, pay1 = refs[14:16]
    rest = refs[15:] if first else refs[16:]
    weight, weight_sems, in_sems, sems, u2, u1, grad_query, grad_source, scaled = rest[:9]
    held = rest[9:]
    x0, x1, x2, n0, n1, q0, q1, p0, p1 = held
    core, upper = flags[0], flags[1]
    needed = (2, 4, 6, 8, 1, 3, 5, 7, 0) if first else (4, 6, 8, 1, 3, 5, 7, 0)
    for place in needed:
        pltpu.make_async_copy(saved_any[place], held[place], in_sems.at[place]).start()
    start_weights(core, own, other, weight, weight_sems, (1, 0) if first else (1,), True)

    def ready(*places):
        for place in places:
            pltpu.make_async_copy(saved_any[place], held[place], in_sems.at[place]).wait()

    def body():
        if first:
            ready(2)
            hidden = x2[...].astype(F32)
            scales = row_scale(hidden)
            grad = mem_gain[...] * (source_mine[...] + source_recv[...].astype(F32))
            mean = jnp.mean(grad * hidden, axis=-1, keepdims=True)
            u2[...] = (scales * grad - hidden * (scales * scales * scales * mean)).astype(BF16)
            up = u2
        else:
            up = upstream
        ready(4, 6, 8)
        attend_backward(n1, q1, p1, up, grad_query, grad_source, False)
        ready(1)
        put_payload(pay1, grad_query, x1, grad_source)
        input_backward(
            x1, gains[1:2], weight.at[1], waiter(own, weight, weight_sems, 1, True), grad_query, grad_source, up, scaled, u1
        )
        ready(3, 5, 7)
        attend_backward(n0, q0, p0, u1, grad_query, grad_source, False)
        ready(0)
        put_payload(pay0, grad_query, x0, grad_source)
        if first:
            input_backward(
                x0, gains[0:1], weight.at[0], waiter(own, weight, weight_sems, 0, True), grad_query, grad_source, u1, scaled, out
            )

    body()
    if not first:
        for mine in (0, 1):
            for role in (0, 1):

                @pl.when(jnp.logical_and(core == mine, upper == role))
                def _():
                    low, high = (done0, done1) if role else (pay0, pay1)
                    pltpu.make_async_copy(high if mine else low, pay_own, sems.at[0]).start()
                    pltpu.make_async_copy(low if mine else high, pay_other, sems.at[1]).start()

        pltpu.make_async_copy(pay0, pay_own, sems.at[0]).wait()
        pltpu.make_async_copy(pay0, pay_other, sems.at[1]).wait()


def enc_backward_call(first, flags, leading, own, other, gains, saved):
    length, width = saved[0].shape
    heads = width // HEAD_DIM
    row = jax.ShapeDtypeStruct((length, width), BF16)
    payload = jax.ShapeDtypeStruct((length + EXTRA_ROWS, width), BF16)
    kinds = [(value.shape, value.dtype) for value in saved]
    payloads = [] if first else [pltpu.VMEM(payload.shape, BF16)] * 2
    return pl.pallas_call(
        functools.partial(enc_backward_kernel, first),
        name="enc_backward_first" if first else "enc_backward_last",
        out_shape=[row, payload, payload] if first else [payload, payload],
        in_specs=[SMEM] + ([VMEM] * 3 if first else [VMEM, ANY, ANY]) + [ANY, ANY, VMEM] + [ANY] * 9,
        out_specs=[VMEM] * 3 if first else [ANY] * 2,
        scratch_shapes=payloads
        + [
            pltpu.VMEM((2, width, width), BF16),
            pltpu.SemaphoreType.DMA((2, heads)),
            pltpu.SemaphoreType.DMA((9,)),
            pltpu.SemaphoreType.DMA((2,)),
            pltpu.VMEM((length, width), BF16),
            pltpu.VMEM((length, width), BF16),
            pltpu.VMEM((length, width), BF16),
            pltpu.VMEM((length, width), F32),
            pltpu.VMEM((length, width), F32),
        ]
        + [pltpu.VMEM(*kind) for kind in kinds],
        compiler_params=PARAMS,
    )(flags, *leading, own, other, gains, *saved)


def product_kernel(with_gain, length, place, slices, *refs):
    pieces, outs, (held, sems) = refs[:8], refs[8:12], refs[12:]
    width = pieces[0].shape[1]
    for index in range(8):
        pltpu.make_async_copy(pieces[index], held.at[index], sems.at[index]).start()
    for index in range(8):
        pltpu.make_async_copy(pieces[index], held.at[index], sems.at[index]).wait()
    block = slices.shape[0] // 4
    if with_gain:
        extra = jnp.zeros((EXTRA_ROWS, width), F32)
        for index in range(8):
            extra = extra + held[index, length:].astype(F32)
        extra = jnp.sum(extra, axis=0, keepdims=True)
        lanes = lax.broadcasted_iota(jnp.int32, (block, width), 1)
        row = lax.broadcasted_iota(jnp.int32, (block, 1), 0)
    for index in range(4):
        rows = slice(index * block, (index + 1) * block)
        total = jnp.zeros((block, width), F32)
        right = held[:, 0:length].reshape(8 * length, width)
        total = dot(slices[rows], right)
        outs[index][:, 0:width] = total.astype(BF16)
        if with_gain:
            half = block // 2
            feature = place[index * 2] + row
            feature = jnp.where(row < half, feature, place[index * 2 + 1] + row - half)
            column = jnp.sum(jnp.where(lanes == feature, extra, 0.0), axis=-1, keepdims=True)
            outs[index][:, width:] = jnp.broadcast_to(column, (block, GAIN_LANES)).astype(BF16)


def product_call(with_gain, place, slices, pieces):
    length = slices.shape[1] // 8
    rows, width = pieces[0].shape
    wide = width + GAIN_LANES if with_gain else width
    return pl.pallas_call(
        functools.partial(product_kernel, with_gain, length),
        name="product_enc" if with_gain else "product_dec",
        out_shape=[jax.ShapeDtypeStruct((slices.shape[0] // 4, wide), BF16)] * 4,
        in_specs=[SMEM, VMEM] + [ANY] * 8,
        out_specs=[VMEM] * 4,
        scratch_shapes=[pltpu.VMEM((8, rows, width), BF16), pltpu.SemaphoreType.DMA((8,))],
        compiler_params=PARAMS,
    )(place, slices, *pieces)


def device(pipe, high, deep, across):
    return pipe * 32 + (high % 2) * 16 + (deep % 4) * 4 + across % 4


def all_places():
    return [(pipe, high, deep, across) for pipe in range(4) for high in range(2) for deep in range(4) for across in range(4)]


def moved(place, along_x, step, flip):
    pipe, high, deep, across = place
    pipe = pipe ^ 1 if flip else pipe
    return device(pipe, high, deep, across + step) if along_x else device(pipe, high, deep + step, across)


def gather_perm(step, flip):
    return [(device(*place), moved(place, (place[0] + flip) % 2 == 0, step, flip)) for place in all_places()]


def reduce_perm(step):
    return [(device(*place), moved(place, place[0] % 2 == 1, step, 0)) for place in all_places()]


HALF_PERM = [(device(*place), device(place[0], place[1] + 1, place[2], place[3])) for place in all_places()]
SWAP_PERM = [(device(*place), device(place[0] ^ 1, *place[1:])) for place in all_places()]
UP_PERM = [
    (device(pipe, high, deep, across), device(pipe + 2, high + pipe, deep, across))
    for pipe, high, deep, across in all_places()
    if pipe < 2
]
DOWN_PERM = [(target, source) for source, target in UP_PERM]
FIRST_PERM = [(device(*place), device(place[0] + 1, *place[1:])) for place in all_places() if place[0] % 2 == 0]
OUT_PERMS = [
    [(device(1, high, deep, across), device(2 + core, high + core, deep, across)) for _, high, deep, across in all_places()[:32]]
    for core in range(2)
]


def send(value, perm):
    return lax.ppermute(value, ("pipe", "dp"), perm)


def gather(mine, other):
    return (
        [mine(0)]
        + [send(mine(step), gather_perm(step, 0)) for step in (1, 2, 3)]
        + [send(other(step), gather_perm(step, 1)) for step in (0, 1, 2, 3)]
    )


def per_device(enc_in, dec_in, out_grad, enc_weight, dec_weight, enc_gain, dec_gain, mem_gain):
    pipe = lax.axis_index("pipe")
    spot = lax.axis_index("dp")
    core, upper = pipe % 2, pipe // 2
    high, deep, across = spot // 16, (spot // 4) % 4, spot % 4
    even = core == 0
    near, far = jnp.where(even, across, deep), jnp.where(even, deep, across)
    flags = jnp.stack([core, upper]).astype(jnp.int32)
    width = enc_weight.shape[1]
    mem_gain = mem_gain[None]

    enc_own, dec_own = enc_weight[0], dec_weight[0]
    gains = jnp.concatenate([enc_gain, dec_gain], axis=0)
    gains_other = send(gains, SWAP_PERM)
    pair = jnp.where(even, jnp.stack([gains, gains_other]), jnp.stack([gains_other, gains]))
    enc_gains, dec_gains = pair[:, 0], pair[:, 1]
    enc_other = send(enc_own, SWAP_PERM)
    dec_other = send(dec_own, SWAP_PERM)
    upstream = send(jnp.where(even, out_grad[0], out_grad[1]), UP_PERM)

    x1 = send(first_call(enc_in, enc_own, enc_gain), FIRST_PERM)
    x2 = first_call(x1, enc_own, enc_gain)
    received = jnp.where(even, send(x2[0], OUT_PERMS[0]), send(x2[1], OUT_PERMS[1]))
    memory_own, saved = enc_forward_call(flags, enc_in, received, enc_own, enc_other, enc_gains, mem_gain)
    memory = jnp.where(upper == 1, memory_own, send(memory_own, DOWN_PERM))

    y1, y2, n0, n1, q0, q1, p0, p1 = dec_forward_call(flags, dec_in, memory, dec_own, dec_other, dec_gains)
    u2, source_mine, dq0, dq1, m0, m1 = dec_turn_call(
        flags, send(y2, UP_PERM), memory, upstream, dec_own, dec_other, dec_gains
    )
    e0, e1, source_low = dec_backward_call(
        flags, send(u2, DOWN_PERM), memory, y1, q0, q1, p0, p1, dec_own, dec_other, dec_gains
    )

    u_low, pay0, pay1 = enc_backward_call(
        True, flags, (source_mine, send(source_low, UP_PERM), mem_gain), enc_own, enc_other, enc_gains, saved
    )
    pay_own, pay_other = enc_backward_call(
        False, flags, (send(u_low, DOWN_PERM), pay0, pay1), enc_own, enc_other, enc_gains, saved
    )

    def slices_for(lower, upper_part):
        length = lower.shape[0]
        low = lower.T.reshape(2, 4, 4, width // 32, length).transpose(2, 0, 1, 3, 4).reshape(4, width // 4, length)
        top = upper_part.T.reshape(2, 4, 4, width // 32, length).transpose(1, 0, 2, 3, 4).reshape(4, width // 4, length)
        mine, other = jnp.where(even, low, top), jnp.where(even, top, low)
        parts = gather(
            lambda step: lax.dynamic_index_in_dim(mine, (near + step) % 4, 0, keepdims=False),
            lambda step: lax.dynamic_index_in_dim(other, (far + step) % 4, 0, keepdims=False),
        )
        whole = jnp.concatenate(parts, axis=1).reshape(2, 4, width // 32, 8 * length)
        order = (far + jnp.arange(4)) % 4
        halves = (high + jnp.arange(2)) % 2
        whole = whole[halves][:, order].transpose(1, 0, 2, 3)
        return whole.reshape(width // 4, 8 * length)

    def place_of(step, half):
        group, third = jnp.where(even, (far + step) % 4, near), jnp.where(even, near, (far + step) % 4)
        return ((high + half) % 2 * 16 + group * 4 + third) * (width // 32)

    place = jnp.stack([place_of(step, half) for step in range(4) for half in range(2)]).astype(jnp.int32)

    def reduced(blocks):
        half = width // 32
        total = blocks[0].astype(F32)
        for step in (1, 2, 3):
            total = total + send(blocks[step], reduce_perm(step)).astype(F32)
        return total[:half] + send(total[half:].astype(BF16), HALF_PERM).astype(F32)

    def finish(rows, weight, gain):
        start = spot * (width // 32)
        weight_rows = lax.dynamic_slice_in_dim(weight, start, width // 32, 0).astype(F32)
        gain_rows = lax.dynamic_slice_in_dim(gain, start, width // 32, 0)
        return jnp.sum(weight_rows * rows, axis=-1) / gain_rows

    dec_slices = slices_for(jnp.where(upper == 1, m0, n0), jnp.where(upper == 1, m1, n1))
    grad0, grad1 = jnp.where(upper == 1, dq0, e0), jnp.where(upper == 1, dq1, e1)
    grad_own, grad_other = jnp.where(even, grad0, grad1), jnp.where(even, grad1, grad0)
    dec_blocks = product_call(False, place, dec_slices, gather(lambda step: grad_own, lambda step: grad_other))
    dec_rows = reduced(dec_blocks)

    enc_slices = slices_for(saved[3], saved[4])
    enc_blocks = product_call(True, place, enc_slices, gather(lambda step: pay_own, lambda step: pay_other))
    enc_rows = reduced(enc_blocks)
    enc_rows, enc_column = enc_rows[:, :width], enc_rows[:, width]

    return (
        enc_rows[None],
        dec_rows[None],
        (finish(enc_rows, enc_own, enc_gain[0]) + enc_column)[None],
        finish(dec_rows, dec_own, dec_gain[0])[None],
    )


def solution(mesh):
    placed = (
        P("dp", None, None),
        P("dp", None, None),
        P("dp", None, None),
        P("pipe", None, None),
        P("pipe", None, None),
        P("pipe", None),
        P("pipe", None),
        P(),
    )
    return jax.shard_map(
        per_device,
        mesh=mesh,
        in_specs=placed,
        out_specs=(P("pipe", "dp", None), P("pipe", "dp", None), P("pipe", "dp"), P("pipe", "dp")),
        check_vma=False,
    )
```

```python
import functools

import jax
import jax.numpy as jnp
from jax import lax
from jax.experimental import pallas as pl
from jax.experimental.pallas import tpu as pltpu
from jax.sharding import PartitionSpec as P

HEAD_DIM = 256
EPSILON = 1e-06
QUERY_SCALE = 0.0625
EXTRA_ROWS = 16
GAIN_LANES = 128

BF16 = jnp.bfloat16
F32 = jnp.float32
ANY = pl.BlockSpec(memory_space=pl.ANY)
SMEM = pl.BlockSpec(memory_space=pltpu.SMEM)
VMEM = pl.BlockSpec(memory_space=pltpu.VMEM)
PARAMS = pltpu.CompilerParams(vmem_limit_bytes=24 * 2**20)


def dot(left, right):
    return jnp.dot(left, right, preferred_element_type=F32)


def dot_nt(left, right):
    return lax.dot_general(left, right, (((1,), (1,)), ((), ())), preferred_element_type=F32)


def dot_tn(left, right):
    return lax.dot_general(left, right, (((0,), (0,)), ((), ())), preferred_element_type=F32)


def row_scale(values):
    return lax.rsqrt(jnp.mean(values * values, axis=-1, keepdims=True) + EPSILON)


def head(index):
    return slice(index * HEAD_DIM, (index + 1) * HEAD_DIM)


def normal(x, gain):
    hidden = x[...].astype(F32)
    return (hidden * row_scale(hidden) * gain).astype(BF16)


def attend_forward(x, query, source, out):
    heads = [head(part) for part in range(x.shape[-1] // HEAD_DIM)]
    raised = [jnp.exp(dot_nt(query[:, cols], source[:, cols])) for cols in heads]
    low = [(value / jnp.sum(value, axis=-1, keepdims=True)).astype(BF16) for value in raised]
    for cols, shares in zip(heads, low):
        out[:, cols] = (x[:, cols].astype(F32) + dot(shares, source[:, cols])).astype(BF16)


def queries_of(normed, weight, query):
    query[...] = (dot(normed[...], weight[...]) * QUERY_SCALE).astype(BF16)


def attend_backward(source, query, upstream, grad_query, grad_source, add):
    heads = [head(part) for part in range(source.shape[-1] // HEAD_DIM)]
    length = query.shape[0]
    if length % 128 == 0:
        sides = [jnp.concatenate([query[:, cols], upstream[:, cols]], axis=0) for cols in heads]
        both = [dot_nt(source[:, cols], side) for cols, side in zip(heads, sides)]
        raised = [jnp.exp(value[:, :length]) for value in both]
        grads = [value[:, length:] for value in both]
    else:
        raised = [jnp.exp(dot_nt(source[:, cols], query[:, cols])) for cols in heads]
        grads = [dot_nt(source[:, cols], upstream[:, cols]) for cols in heads]
    probs = [value / jnp.sum(value, axis=0, keepdims=True) for value in raised]
    scores = [
        (share * (grad - jnp.sum(grad * share, axis=0, keepdims=True))).astype(BF16) for share, grad in zip(probs, grads)
    ]
    for part, cols in enumerate(heads):
        low = probs[part].astype(BF16)
        grad_query[:, cols] = (dot_tn(scores[part], source[:, cols]) * QUERY_SCALE).astype(BF16)
        if length % 128 == 0:
            total = dot(jnp.concatenate([scores[part], low], axis=1), sides[part])
        else:
            total = dot(scores[part], query[:, cols]) + dot(low, upstream[:, cols])
        grad_source[:, cols] = grad_source[:, cols] + total if add else total


def input_backward(x, gain, weight, grad_query, grad_source, upstream, scaled, out):
    width = x.shape[-1]
    hidden = x[...].astype(F32)
    scales = row_scale(hidden)
    total = jnp.zeros((x.shape[0], 1), F32)
    for part in range(width // HEAD_DIM):
        cols = head(part)
        grad = gain[:, cols] * dot_nt(grad_query[...], weight[cols, :])
        if grad_source is not None:
            grad = grad + gain[:, cols] * grad_source[:, cols]
        scaled[:, cols] = grad
        total = total + jnp.sum(grad * x[:, cols].astype(F32), axis=-1, keepdims=True)
    factor = scales * scales * scales * (total / width)
    out[...] = (upstream[...].astype(F32) + scales * scaled[...] - hidden * factor).astype(BF16)


def gain_row(x, grad_source):
    hidden = x[...].astype(F32)
    return jnp.sum(grad_source[...] * hidden * row_scale(hidden), axis=0, keepdims=True)


def by_core(core, low, high, own, other):
    for mine in (0, 1):

        @pl.when(core == mine)
        def _():
            own[...] = high[...] if mine else low[...]
            other[...] = low[...] if mine else high[...]


def load_kernel(own, other, pair, sems):
    copies = [pltpu.make_async_copy(part, pair.at[slot], sems.at[slot]) for slot, part in enumerate((own, other))]
    for copy in copies:
        copy.start()
    for copy in copies:
        copy.wait()


def load_call(own, other):
    pair = pl.pallas_call(
        load_kernel,
        name="load_weights",
        out_shape=pltpu.VMEM((2,) + own.shape, BF16),
        in_specs=[ANY, ANY],
        out_specs=VMEM,
        scratch_shapes=[pltpu.SemaphoreType.DMA((2,))],
        compiler_params=PARAMS,
    )(own, other)
    return pltpu.with_memory_space_constraint(pair, pltpu.VMEM)


def first_kernel(turn, flags, x, weight_any, gain, out, weight, normed, query, sems):
    @pl.when(jnp.logical_and(flags[0] == turn, flags[1] == 0))
    def _():
        count, length, width = x.shape
        parts = range(width // HEAD_DIM)
        copies = [
            pltpu.make_async_copy(weight_any.at[:, head(part)], weight.at[:, head(part)], sems.at[part]) for part in parts
        ]
        for copy in copies:
            copy.start()
        for sequence in range(count):
            normed[sequence * length : (sequence + 1) * length] = normal(x.at[sequence], gain[...])
        for part in parts:
            copies[part].wait()
            query[:, head(part)] = (dot(normed[...], weight[:, head(part)]) * QUERY_SCALE).astype(BF16)
        for sequence in range(count):
            rows = pl.ds(sequence * length, length)
            attend_forward(x.at[sequence], query.at[rows], normed.at[rows], out.at[sequence])


def first_call(turn, flags, x, weight, gain):
    count, length, width = x.shape
    return pl.pallas_call(
        functools.partial(first_kernel, turn),
        name="enc_first_lower" if turn == 0 else "enc_first_upper",
        out_shape=jax.ShapeDtypeStruct(x.shape, BF16),
        in_specs=[SMEM, VMEM, ANY, VMEM],
        out_specs=VMEM,
        scratch_shapes=[
            pltpu.VMEM((width, width), BF16),
            pltpu.VMEM((count * length, width), BF16),
            pltpu.VMEM((count * length, width), BF16),
            pltpu.SemaphoreType.DMA((width // HEAD_DIM,)),
        ],
        compiler_params=PARAMS,
    )(flags, x, weight, gain)


def enc_forward_kernel(
    flags, x_any, recv0, recv1, pair, gains, mem_gain, mem, x0, x1, x2, n0, n1, q0, q1, n_own, n_other, sem
):
    core, upper = flags[0], flags[1]

    @pl.when(upper == 0)
    def _():
        pltpu.make_async_copy(x_any.at[core], x0, sem).start()

    for mine, received in enumerate((recv0, recv1)):

        @pl.when(jnp.logical_and(upper == 1, core == mine))
        def _():
            pltpu.make_async_copy(received, x0, sem).start()

    pltpu.make_async_copy(recv0, x0, sem).wait()
    n0[...] = normal(x0, gains[0:1])
    queries_of(n0, pair.at[core], q0)
    attend_forward(x0, q0, n0, x1)
    n1[...] = normal(x1, gains[1:2])
    queries_of(n1, pair.at[1 - core], q1)
    attend_forward(x1, q1, n1, x2)
    mem[...] = normal(x2, mem_gain[...])
    by_core(core, n0, n1, n_own, n_other)


def enc_forward_call(flags, x, recv0, recv1, pair, gains, mem_gain):
    row = jax.ShapeDtypeStruct(recv0.shape, BF16)
    return pl.pallas_call(
        enc_forward_kernel,
        name="enc_forward",
        out_shape=[row] * 10,
        in_specs=[SMEM, ANY, ANY, ANY, VMEM, VMEM, VMEM],
        out_specs=[VMEM] * 10,
        scratch_shapes=[pltpu.SemaphoreType.DMA],
        compiler_params=PARAMS,
    )(flags, x, recv0, recv1, pair, gains, mem_gain)


def dec_forward_kernel(flags, x_any, memory, pair, gains, y1, y2, n0, n1, q0, q1, sem, y0):
    core, upper = flags[0], flags[1]

    @pl.when(upper == 0)
    def _():
        rows = pltpu.make_async_copy(x_any.at[core], y0, sem)
        rows.start()
        rows.wait()
        n0[...] = normal(y0, gains[0:1])
        queries_of(n0, pair.at[core], q0)
        attend_forward(y0, q0, memory, y1)
        n1[...] = normal(y1, gains[1:2])
        queries_of(n1, pair.at[1 - core], q1)
        attend_forward(y1, q1, memory, y2)


def dec_forward_call(flags, x, memory, pair, gains):
    row = jax.ShapeDtypeStruct(x.shape[1:], BF16)
    return pl.pallas_call(
        dec_forward_kernel,
        name="dec_forward",
        out_shape=[row] * 6,
        in_specs=[SMEM, ANY, VMEM, VMEM, VMEM],
        out_specs=[VMEM] * 6,
        scratch_shapes=[pltpu.SemaphoreType.DMA, pltpu.VMEM(x.shape[1:], BF16)],
        compiler_params=PARAMS,
    )(flags, x, memory, pair, gains)


def dec_turn_kernel(flags, y2, memory, upstream, pair, gains, out, grad_source, pay0, pay1, n0, n1, y3, u3, q0, q1, dq0, dq1, scaled):
    core, upper = flags[0], flags[1]

    @pl.when(upper == 1)
    def _():
        length = y2.shape[0]
        n0[...] = normal(y2, gains[0:1])
        queries_of(n0, pair.at[core], q0)
        attend_forward(y2, q0, memory, y3)
        n1[...] = normal(y3, gains[1:2])
        queries_of(n1, pair.at[1 - core], q1)
        attend_backward(memory, q1, upstream, dq1, grad_source, False)
        input_backward(y3, gains[1:2], pair.at[1 - core], dq1, None, upstream, scaled, u3)
        attend_backward(memory, q0, u3, dq0, grad_source, True)
        input_backward(y2, gains[0:1], pair.at[core], dq0, None, u3, scaled, out)
        for payload, normed, grad in ((pay0, n0, dq0), (pay1, n1, dq1)):
            payload[0:length] = normed[...]
            payload[length:] = grad[...]


def dec_turn_call(flags, y2, memory, upstream, pair, gains):
    length, width = y2.shape
    row = jax.ShapeDtypeStruct((length, width), BF16)
    payload = jax.ShapeDtypeStruct((2 * length, width), BF16)
    held = pltpu.VMEM((length, width), BF16)
    return pl.pallas_call(
        dec_turn_kernel,
        name="dec_turn",
        out_shape=[row, jax.ShapeDtypeStruct(memory.shape, F32), payload, payload],
        in_specs=[SMEM] + [VMEM] * 5,
        out_specs=[VMEM] * 4,
        scratch_shapes=[held] * 8 + [pltpu.VMEM((length, width), F32)],
        compiler_params=PARAMS,
    )(flags, y2, memory, upstream, pair, gains)


def dec_backward_kernel(
    flags, upstream, memory, y1, n0, n1, q0, q1, pair, gains, done0, done1, source_low, own, other, u1, dq0, dq1, grad_source, scaled, pay0, pay1
):
    core, upper = flags[0], flags[1]

    @pl.when(upper == 0)
    def _():
        length = y1.shape[0]
        attend_backward(memory, q1, upstream, dq1, grad_source, False)
        input_backward(y1, gains[1:2], pair.at[1 - core], dq1, None, upstream, scaled, u1)
        attend_backward(memory, q0, u1, dq0, grad_source, True)
        source_low[...] = grad_source[...].astype(BF16)
        for payload, normed, grad in ((pay0, n0, dq0), (pay1, n1, dq1)):
            payload[0:length] = normed[...]
            payload[length:] = grad[...]
        by_core(core, pay0, pay1, own, other)

    @pl.when(upper == 1)
    def _():
        by_core(core, done0, done1, own, other)


def dec_backward_call(flags, upstream, memory, y1, n0, n1, q0, q1, pair, gains, done0, done1):
    length, width = upstream.shape
    payload = jax.ShapeDtypeStruct((2 * length, width), BF16)
    held = pltpu.VMEM((length, width), BF16)
    return pl.pallas_call(
        dec_backward_kernel,
        name="dec_backward",
        out_shape=[jax.ShapeDtypeStruct(memory.shape, BF16), payload, payload],
        in_specs=[SMEM] + [VMEM] * 11,
        out_specs=[VMEM] * 3,
        scratch_shapes=[held] * 3
        + [pltpu.VMEM(memory.shape, F32), pltpu.VMEM((length, width), F32)]
        + [pltpu.VMEM(payload.shape, BF16)] * 2,
        compiler_params=PARAMS,
    )(flags, upstream, memory, y1, n0, n1, q0, q1, pair, gains, done0, done1)


def put_payload(payload, grad_query, x, grad_source):
    length, width = grad_query.shape
    payload[0:length] = grad_query[...]
    place = lax.broadcasted_iota(jnp.int32, (EXTRA_ROWS, width), 0)
    payload[length:] = jnp.where(place == 0, gain_row(x, grad_source), 0.0).astype(BF16)


def enc_backward_first_kernel(
    flags, source_mine, source_recv, mem_gain, pair, gains, x0, x1, x2, n0, n1, q0, q1, out, pay0, pay1, u2, u1, grad_query, grad_source, scaled
):
    core, upper = flags[0], flags[1]

    @pl.when(upper == 1)
    def _():
        hidden = x2[...].astype(F32)
        scales = row_scale(hidden)
        grad = mem_gain[...] * (source_mine[...] + source_recv[...].astype(F32))
        mean = jnp.mean(grad * hidden, axis=-1, keepdims=True)
        u2[...] = (scales * grad - hidden * (scales * scales * scales * mean)).astype(BF16)
        attend_backward(n1, q1, u2, grad_query, grad_source, False)
        put_payload(pay1, grad_query, x1, grad_source)
        input_backward(x1, gains[1:2], pair.at[1 - core], grad_query, grad_source, u2, scaled, u1)
        attend_backward(n0, q0, u1, grad_query, grad_source, False)
        put_payload(pay0, grad_query, x0, grad_source)
        input_backward(x0, gains[0:1], pair.at[core], grad_query, grad_source, u1, scaled, out)


def enc_backward_first_call(flags, source_mine, source_recv, mem_gain, pair, gains, saved):
    length, width = saved[0].shape
    row = jax.ShapeDtypeStruct((length, width), BF16)
    payload = jax.ShapeDtypeStruct((length + EXTRA_ROWS, width), BF16)
    return pl.pallas_call(
        enc_backward_first_kernel,
        name="enc_backward_first",
        out_shape=[row, payload, payload],
        in_specs=[SMEM] + [VMEM] * 12,
        out_specs=[VMEM] * 3,
        scratch_shapes=[pltpu.VMEM((length, width), BF16)] * 3 + [pltpu.VMEM((length, width), F32)] * 2,
        compiler_params=PARAMS,
    )(flags, source_mine, source_recv, mem_gain, pair, gains, *saved)


def enc_backward_last_kernel(
    flags, upstream, done0, done1, pair, gains, x0, x1, n0, n1, q0, q1, own, other, pay0, pay1, u1, grad_query, grad_source, scaled
):
    core, upper = flags[0], flags[1]

    @pl.when(upper == 0)
    def _():
        attend_backward(n1, q1, upstream, grad_query, grad_source, False)
        put_payload(pay1, grad_query, x1, grad_source)
        input_backward(x1, gains[1:2], pair.at[1 - core], grad_query, grad_source, upstream, scaled, u1)
        attend_backward(n0, q0, u1, grad_query, grad_source, False)
        put_payload(pay0, grad_query, x0, grad_source)
        by_core(core, pay0, pay1, own, other)

    @pl.when(upper == 1)
    def _():
        by_core(core, done0, done1, own, other)


def enc_backward_last_call(flags, upstream, done0, done1, pair, gains, saved):
    x0, x1, _, n0, n1, q0, q1 = saved
    length, width = upstream.shape
    payload = jax.ShapeDtypeStruct((length + EXTRA_ROWS, width), BF16)
    return pl.pallas_call(
        enc_backward_last_kernel,
        name="enc_backward_last",
        out_shape=[payload, payload],
        in_specs=[SMEM] + [VMEM] * 11,
        out_specs=[VMEM] * 2,
        scratch_shapes=[pltpu.VMEM(payload.shape, BF16)] * 2
        + [pltpu.VMEM((length, width), BF16)] * 2
        + [pltpu.VMEM((length, width), F32)] * 2,
        compiler_params=PARAMS,
    )(flags, upstream, done0, done1, pair, gains, x0, x1, n0, n1, q0, q1)


def features(place, index, block):
    row = lax.broadcasted_iota(jnp.int32, (block, 1), 0)
    half = block // 2
    return jnp.where(row < half, place[index * 2] + row, place[index * 2 + 1] + row - half)


def chosen(place, index, block, normed):
    lanes = lax.broadcasted_iota(jnp.int32, (block, normed.shape[-1]), 1)
    ones = jnp.where(lanes == features(place, index, block), 1.0, 0.0).astype(BF16)
    return dot_nt(ones, normed).astype(BF16)


def choose_kernel(place, *refs):
    pieces, out, (held,) = refs[:8], refs[8], refs[9:]
    length, width = pieces[0].shape
    block = out.shape[0] // 4
    for index in range(8):
        held[index * length : (index + 1) * length] = pieces[index][...]
    for index in range(4):
        out[index * block : (index + 1) * block] = chosen(place, index, block, held[...])


def choose_call(place, pieces):
    length, width = pieces[0].shape
    return pl.pallas_call(
        choose_kernel,
        name="choose_enc",
        out_shape=jax.ShapeDtypeStruct((width // 4, 8 * length), BF16),
        in_specs=[SMEM] + [VMEM] * 8,
        out_specs=VMEM,
        scratch_shapes=[pltpu.VMEM((8 * length, width), BF16)],
        compiler_params=PARAMS,
    )(place, *pieces)


def dec_product_kernel(place, *refs):
    pieces, outs, (normed, grads) = refs[:8], refs[8:12], refs[12:]
    length = pieces[0].shape[0] // 2
    for index in range(8):
        normed[index * length : (index + 1) * length] = pieces[index][0:length]
        grads[index * length : (index + 1) * length] = pieces[index][length:]
    block = outs[0].shape[0]
    for index in range(4):
        outs[index][...] = dot(chosen(place, index, block, normed[...]), grads[...]).astype(BF16)


def dec_product_call(place, pieces):
    rows, width = pieces[0].shape
    return pl.pallas_call(
        dec_product_kernel,
        name="product_dec",
        out_shape=[jax.ShapeDtypeStruct((width // 16, width), BF16)] * 4,
        in_specs=[SMEM] + [VMEM] * 8,
        out_specs=[VMEM] * 4,
        scratch_shapes=[pltpu.VMEM((4 * rows, width), BF16)] * 2,
        compiler_params=PARAMS,
    )(place, *pieces)


def enc_product_kernel(place, slices, *refs):
    pieces, outs, (held,) = refs[:8], refs[8:12], refs[12:]
    length, width = slices.shape[1] // 8, pieces[0].shape[1]
    block = slices.shape[0] // 4
    extra = jnp.zeros((EXTRA_ROWS, width), F32)
    for index in range(8):
        held[index * length : (index + 1) * length] = pieces[index][0:length]
        extra = extra + pieces[index][length:].astype(F32)
    extra = jnp.sum(extra, axis=0, keepdims=True)
    for index in range(4):
        outs[index][:, 0:width] = dot(slices[index * block : (index + 1) * block], held[...]).astype(BF16)
        lanes = lax.broadcasted_iota(jnp.int32, (block, width), 1)
        column = jnp.sum(jnp.where(lanes == features(place, index, block), extra, 0.0), axis=-1, keepdims=True)
        outs[index][:, width:] = jnp.broadcast_to(column, (block, GAIN_LANES)).astype(BF16)


def enc_product_call(place, slices, pieces):
    width = pieces[0].shape[1]
    return pl.pallas_call(
        enc_product_kernel,
        name="product_enc",
        out_shape=[jax.ShapeDtypeStruct((slices.shape[0] // 4, width + GAIN_LANES), BF16)] * 4,
        in_specs=[SMEM] + [VMEM] * 9,
        out_specs=[VMEM] * 4,
        scratch_shapes=[pltpu.VMEM((slices.shape[1], width), BF16)],
        compiler_params=PARAMS,
    )(place, slices, *pieces)


def device(pipe, high, deep, across):
    return pipe * 32 + (high % 2) * 16 + (deep % 4) * 4 + across % 4


def all_places():
    return [(pipe, high, deep, across) for pipe in range(4) for high in range(2) for deep in range(4) for across in range(4)]


def moved(place, along_x, step, flip):
    pipe, high, deep, across = place
    pipe = pipe ^ 1 if flip else pipe
    return device(pipe, high, deep, across + step) if along_x else device(pipe, high, deep + step, across)


def gather_perm(step, flip):
    return [(device(*place), moved(place, (place[0] + flip) % 2 == 0, step, flip)) for place in all_places()]


def reduce_perm(step):
    return [(device(*place), moved(place, place[0] % 2 == 1, step, 0)) for place in all_places()]


HALF_PERM = [(device(*place), device(place[0], place[1] + 1, place[2], place[3])) for place in all_places()]
SWAP_PERM = [(device(*place), device(place[0] ^ 1, *place[1:])) for place in all_places()]
UP_PERM = [
    (device(pipe, high, deep, across), device(pipe + 2, high + pipe, deep, across))
    for pipe, high, deep, across in all_places()
    if pipe < 2
]
DOWN_PERM = [(target, source) for source, target in UP_PERM]
FIRST_PERM = [(device(*place), device(place[0] + 1, *place[1:])) for place in all_places() if place[0] % 2 == 0]
OUT_PERMS = [
    [(device(1, high, deep, across), device(2 + core, high + core, deep, across)) for _, high, deep, across in all_places()[:32]]
    for core in range(2)
]


def send(value, perm):
    return lax.ppermute(value, ("pipe", "dp"), perm)


def gather(mine, other):
    return (
        [mine]
        + [send(mine, gather_perm(step, 0)) for step in (1, 2, 3)]
        + [send(other, gather_perm(step, 1)) for step in (0, 1, 2, 3)]
    )


def after(value, *earlier):
    return lax.optimization_barrier((value, earlier))[0]


def per_device(enc_in, dec_in, out_grad, enc_weight, dec_weight, enc_gain, dec_gain, mem_gain):
    pipe = lax.axis_index("pipe")
    spot = lax.axis_index("dp")
    core, upper = pipe % 2, pipe // 2
    high, deep, across = spot // 16, (spot // 4) % 4, spot % 4
    even = core == 0
    near, far = jnp.where(even, across, deep), jnp.where(even, deep, across)
    flags = jnp.stack([core, upper]).astype(jnp.int32)
    width = enc_weight.shape[1]
    mem_gain = mem_gain[None]

    def place_of(step, half):
        group, third = jnp.where(even, (far + step) % 4, near), jnp.where(even, near, (far + step) % 4)
        return ((high + half) % 2 * 16 + group * 4 + third) * (width // 32)

    place = jnp.stack([place_of(step, half) for step in range(4) for half in range(2)]).astype(jnp.int32)

    enc_own, dec_own = enc_weight[0], dec_weight[0]
    gains = jnp.concatenate([enc_gain, dec_gain], axis=0)
    gains_other = send(gains, SWAP_PERM)
    pair = jnp.where(even, jnp.stack([gains, gains_other]), jnp.stack([gains_other, gains]))
    enc_gains, dec_gains = pair[:, 0], pair[:, 1]
    upstream = send(jnp.where(even, out_grad[0], out_grad[1]), UP_PERM)

    x1 = send(first_call(0, flags, enc_in, enc_own, enc_gain), FIRST_PERM)
    enc_other = send(after(enc_own, x1), SWAP_PERM)
    x2 = first_call(1, flags, x1, enc_own, enc_gain)
    received = [send(x2[sequence], OUT_PERMS[sequence]) for sequence in range(2)]
    enc_pair = load_call(enc_own, enc_other)
    dec_other = send(after(dec_own, enc_other), SWAP_PERM)
    memory, *saved, n_own, n_other = enc_forward_call(flags, enc_in, *received, enc_pair, enc_gains, mem_gain)
    memory_recv = send(memory, DOWN_PERM)
    normed_pieces = gather(n_own, n_other)
    dec_pair = load_call(dec_own, dec_other)
    memory = jnp.where(upper == 1, memory, memory_recv)

    y1, y2, n0, n1, q0, q1 = dec_forward_call(flags, dec_in, memory, dec_pair, dec_gains)
    u2, source_mine, done0, done1 = dec_turn_call(flags, send(y2, UP_PERM), memory, upstream, dec_pair, dec_gains)
    slices = choose_call(place, normed_pieces)
    source_low, dec_own_pay, dec_other_pay = dec_backward_call(
        flags, after(send(u2, DOWN_PERM), slices), memory, y1, n0, n1, q0, q1, dec_pair, dec_gains, done0, done1
    )
    source_recv = send(source_low, UP_PERM)
    dec_pieces = gather(dec_own_pay, dec_other_pay)

    u_low, done0, done1 = enc_backward_first_call(flags, source_mine, source_recv, mem_gain, enc_pair, enc_gains, saved)
    dec_blocks = dec_product_call(place, dec_pieces)
    own_pay, other_pay = enc_backward_last_call(
        flags, after(send(u_low, DOWN_PERM), *dec_blocks), done0, done1, enc_pair, enc_gains, saved
    )

    def reduced(blocks):
        half = width // 32
        total = blocks[0].astype(F32)
        for step in (1, 2, 3):
            total = total + send(blocks[step], reduce_perm(step)).astype(F32)
        return total[:half] + send(total[half:].astype(BF16), HALF_PERM).astype(F32)

    def finish(rows, weight, gain):
        start = spot * (width // 32)
        weight_rows = lax.dynamic_slice_in_dim(weight, start, width // 32, 0).astype(F32)
        gain_rows = lax.dynamic_slice_in_dim(gain, start, width // 32, 0)
        return jnp.sum(weight_rows * rows, axis=-1) / gain_rows

    dec_rows = reduced(dec_blocks)
    enc_rows = reduced(enc_product_call(place, slices, gather(own_pay, other_pay)))
    enc_rows, enc_column = enc_rows[:, :width], enc_rows[:, width]

    return (
        enc_rows[None],
        dec_rows[None],
        (finish(enc_rows, enc_own, enc_gain[0]) + enc_column)[None],
        finish(dec_rows, dec_own, dec_gain[0])[None],
    )


def solution(mesh):
    placed = (
        P("dp", None, None),
        P("dp", None, None),
        P("dp", None, None),
        P("pipe", None, None),
        P("pipe", None, None),
        P("pipe", None),
        P("pipe", None),
        P(),
    )
    return jax.shard_map(
        per_device,
        mesh=mesh,
        in_specs=placed,
        out_specs=(P("pipe", "dp", None), P("pipe", "dp", None), P("pipe", "dp"), P("pipe", "dp")),
        check_vma=False,
    )
```

```python
import functools

import jax
import jax.numpy as jnp
from jax import lax
from jax.experimental import pallas as pl
from jax.experimental.pallas import tpu as pltpu
from jax.sharding import PartitionSpec as P

HEAD_DIM = 256
EPSILON = 1e-06
QUERY_SCALE = 0.0625
EXTRA_ROWS = 16
GAIN_LANES = 128

BF16 = jnp.bfloat16
F32 = jnp.float32
ANY = pl.BlockSpec(memory_space=pl.ANY)
SMEM = pl.BlockSpec(memory_space=pltpu.SMEM)
VMEM = pl.BlockSpec(memory_space=pltpu.VMEM)
HBM = pl.BlockSpec(memory_space=pltpu.HBM)
WIDE_PARAMS = pltpu.CompilerParams(vmem_limit_bytes=20 * 2**20)
PARAMS = pltpu.CompilerParams(vmem_limit_bytes=12 * 2**20)


def dot(left, right):
    return jnp.dot(left, right, preferred_element_type=F32)


def dot_nt(left, right):
    return lax.dot_general(left, right, (((1,), (1,)), ((), ())), preferred_element_type=F32)


def dot_tn(left, right):
    return lax.dot_general(left, right, (((0,), (0,)), ((), ())), preferred_element_type=F32)


def row_scale(values):
    return lax.rsqrt(jnp.mean(values * values, axis=-1, keepdims=True) + EPSILON)


def head(index):
    return slice(index * HEAD_DIM, (index + 1) * HEAD_DIM)


def normal(x, gain):
    hidden = x[...].astype(F32)
    return (hidden * row_scale(hidden) * gain).astype(BF16)


def attend_forward(x, query, source, out):
    heads = [head(part) for part in range(x.shape[-1] // HEAD_DIM)]
    raised = [jnp.exp(dot_nt(query[:, cols], source[:, cols])) for cols in heads]
    low = [(value / jnp.sum(value, axis=-1, keepdims=True)).astype(BF16) for value in raised]
    for cols, shares in zip(heads, low):
        out[:, cols] = (x[:, cols].astype(F32) + dot(shares, source[:, cols])).astype(BF16)


def queries_of(weight, normed, query):
    query[...] = (dot(normed[...], weight[...]) * QUERY_SCALE).astype(BF16)


def attend_backward(source, query, upstream, grad_query, grad_source, add):
    heads = [head(part) for part in range(source.shape[-1] // HEAD_DIM)]
    length = query.shape[0]
    if length % 128 == 0:
        sides = [jnp.concatenate([query[:, cols], upstream[:, cols]], axis=0) for cols in heads]
        both = [dot_nt(source[:, cols], side) for cols, side in zip(heads, sides)]
        raised = [jnp.exp(value[:, :length]) for value in both]
        grads = [value[:, length:] for value in both]
    else:
        raised = [jnp.exp(dot_nt(source[:, cols], query[:, cols])) for cols in heads]
        grads = [dot_nt(source[:, cols], upstream[:, cols]) for cols in heads]
    probs = [value / jnp.sum(value, axis=0, keepdims=True) for value in raised]
    scores = [
        (share * (grad - jnp.sum(grad * share, axis=0, keepdims=True))).astype(BF16) for share, grad in zip(probs, grads)
    ]
    for part, cols in enumerate(heads):
        low = probs[part].astype(BF16)
        grad_query[:, cols] = (dot_tn(scores[part], source[:, cols]) * QUERY_SCALE).astype(BF16)
        if length % 128 == 0:
            total = dot(jnp.concatenate([scores[part], low], axis=1), sides[part])
        else:
            total = dot(scores[part], query[:, cols]) + dot(low, upstream[:, cols])
        grad_source[:, cols] = grad_source[:, cols] + total if add else total


def input_backward(weight, x, gain, grad_query, grad_source, upstream, scaled, out):
    length, width = x.shape

    for part in range(width // HEAD_DIM):
        cols = head(part)
        if length % 128 == 0:
            scaled[:, cols] = dot_nt(weight[cols, :], grad_query[...]).T
        else:
            scaled[:, cols] = dot_nt(grad_query[...], weight[cols, :])
    hidden = x[...].astype(F32)
    scales = row_scale(hidden)
    grad = scaled[...] if grad_source is None else scaled[...] + grad_source[...]
    grad = gain * grad
    mean = jnp.mean(grad * hidden, axis=-1, keepdims=True)
    factor = scales * scales * scales * mean
    out[...] = (upstream[...].astype(F32) + scales * grad - hidden * factor).astype(BF16)


def gain_row(x, grad_source):
    hidden = x[...].astype(F32)
    return jnp.sum(grad_source[...] * hidden * row_scale(hidden), axis=0, keepdims=True)


def by_core(core, low, high, own, other):
    for mine in (0, 1):

        @pl.when(core == mine)
        def _():
            own[...] = high[...] if mine else low[...]
            other[...] = low[...] if mine else high[...]


def load_kernel(own, other, pair, sems):
    copies = [pltpu.make_async_copy(part, pair.at[slot], sems.at[slot]) for slot, part in enumerate((own, other))]
    for copy in copies:
        copy.start()
    for copy in copies:
        copy.wait()


def load_call(own, other):
    return pl.pallas_call(
        load_kernel,
        name="load_weights",
        out_shape=pltpu.VMEM((2,) + own.shape, BF16),
        in_specs=[HBM, ANY],
        out_specs=VMEM,
        scratch_shapes=[pltpu.SemaphoreType.DMA((2,))],
        compiler_params=PARAMS,
    )(own, other)


def pinned(value):
    return pltpu.with_memory_space_constraint(value, pltpu.VMEM)


def first_kernel(turn, flags, x, weight_any, gain, out, weight, normed, query, sems):
    @pl.when(jnp.logical_and(flags[0] == turn, flags[1] == 0))
    def _():
        count, length, width = x.shape
        parts = range(width // HEAD_DIM)
        copies = [
            pltpu.make_async_copy(weight_any.at[:, head(part)], weight.at[:, head(part)], sems.at[part]) for part in parts
        ]
        for copy in copies:
            copy.start()
        for sequence in range(count):
            normed[sequence * length : (sequence + 1) * length] = normal(x.at[sequence], gain[...])
        for part in parts:
            copies[part].wait()
            query[:, head(part)] = (dot(normed[...], weight[:, head(part)]) * QUERY_SCALE).astype(BF16)
        for sequence in range(count):
            rows = pl.ds(sequence * length, length)
            attend_forward(x.at[sequence], query.at[rows], normed.at[rows], out.at[sequence])


def first_call(turn, flags, x, weight, gain):
    count, length, width = x.shape
    return pl.pallas_call(
        functools.partial(first_kernel, turn),
        name="enc_first_lower" if turn == 0 else "enc_first_upper",
        out_shape=jax.ShapeDtypeStruct(x.shape, BF16),
        in_specs=[SMEM, VMEM, HBM, VMEM],
        out_specs=VMEM,
        scratch_shapes=[
            pltpu.VMEM((width, width), BF16),
            pltpu.VMEM((count * length, width), BF16),
            pltpu.VMEM((count * length, width), BF16),
            pltpu.SemaphoreType.DMA((width // HEAD_DIM,)),
        ],
        compiler_params=WIDE_PARAMS,
    )(flags, x, weight, gain)


def enc_forward_kernel(
    flags, x_any, recv0, recv1, pair, gains, mem_gain, mem, x0, x1, x2, n0, n1, q0, q1, n_own, n_other, sem
):
    core, upper = flags[0], flags[1]

    @pl.when(upper == 0)
    def _():
        pltpu.make_async_copy(x_any.at[core], x0, sem).start()

    for mine, received in enumerate((recv0, recv1)):

        @pl.when(jnp.logical_and(upper == 1, core == mine))
        def _():
            pltpu.make_async_copy(received, x0, sem).start()

    pltpu.make_async_copy(recv0, x0, sem).wait()
    n0[...] = normal(x0, gains[0:1])
    queries_of(pair.at[core], n0, q0)
    attend_forward(x0, q0, n0, x1)
    n1[...] = normal(x1, gains[1:2])
    queries_of(pair.at[1 - core], n1, q1)
    attend_forward(x1, q1, n1, x2)
    mem[...] = normal(x2, mem_gain[...])
    by_core(core, n0, n1, n_own, n_other)


def enc_forward_call(flags, x, recv0, recv1, pair, gains, mem_gain):
    row = jax.ShapeDtypeStruct(recv0.shape, BF16)
    return pl.pallas_call(
        enc_forward_kernel,
        name="enc_forward",
        out_shape=[row] * 10,
        in_specs=[SMEM, ANY, ANY, ANY] + [VMEM] * 3,
        out_specs=[VMEM] * 10,
        scratch_shapes=[pltpu.SemaphoreType.DMA],
        compiler_params=PARAMS,
    )(flags, x, recv0, recv1, pinned(pair), gains, mem_gain)


def dec_query_kernel(flags, x_any, pair, gains, n0, q0, sem, y0):
    core, upper = flags[0], flags[1]

    @pl.when(upper == 0)
    def _():
        rows = pltpu.make_async_copy(x_any.at[core], y0, sem)
        rows.start()
        rows.wait()
        n0[...] = normal(y0, gains[0:1])
        queries_of(pair.at[core], n0, q0)


def dec_query_call(flags, x, pair, gains):
    row = jax.ShapeDtypeStruct(x.shape[1:], BF16)
    return pl.pallas_call(
        dec_query_kernel,
        name="dec_query",
        out_shape=[row] * 2,
        in_specs=[SMEM, ANY, VMEM, VMEM],
        out_specs=[VMEM] * 2,
        scratch_shapes=[pltpu.SemaphoreType.DMA, pltpu.VMEM(x.shape[1:], BF16)],
        compiler_params=PARAMS,
    )(flags, x, pinned(pair), gains)


def dec_forward_kernel(flags, x_any, memory, q0, pair, gains, y1, y2, n1, q1, sem, y0):
    core, upper = flags[0], flags[1]

    @pl.when(upper == 0)
    def _():
        rows = pltpu.make_async_copy(x_any.at[core], y0, sem)
        rows.start()
        rows.wait()
        attend_forward(y0, q0, memory, y1)
        n1[...] = normal(y1, gains[1:2])
        queries_of(pair.at[1 - core], n1, q1)
        attend_forward(y1, q1, memory, y2)


def dec_forward_call(flags, x, memory, q0, pair, gains):
    row = jax.ShapeDtypeStruct(x.shape[1:], BF16)
    return pl.pallas_call(
        dec_forward_kernel,
        name="dec_forward",
        out_shape=[row] * 4,
        in_specs=[SMEM, ANY] + [VMEM] * 4,
        out_specs=[VMEM] * 4,
        scratch_shapes=[pltpu.SemaphoreType.DMA, pltpu.VMEM(x.shape[1:], BF16)],
        compiler_params=PARAMS,
    )(flags, x, memory, q0, pinned(pair), gains)


def dec_turn_kernel(
    flags, y2, memory, upstream, pair, gains, out, grad_source, pay0, pay1, n0, n1, y3, u3, q0, q1, dq0, dq1, scaled
):
    core, upper = flags[0], flags[1]

    @pl.when(upper == 1)
    def _():
        length = y2.shape[0]
        n0[...] = normal(y2, gains[0:1])
        queries_of(pair.at[core], n0, q0)
        attend_forward(y2, q0, memory, y3)
        n1[...] = normal(y3, gains[1:2])
        queries_of(pair.at[1 - core], n1, q1)
        attend_backward(memory, q1, upstream, dq1, grad_source, False)
        input_backward(pair.at[1 - core], y3, gains[1:2], dq1, None, upstream, scaled, u3)
        attend_backward(memory, q0, u3, dq0, grad_source, True)
        input_backward(pair.at[core], y2, gains[0:1], dq0, None, u3, scaled, out)
        for payload, normed, grad in ((pay0, n0, dq0), (pay1, n1, dq1)):
            payload[0:length] = normed[...]
            payload[length:] = grad[...]


def dec_turn_call(flags, y2, memory, upstream, pair, gains):
    length, width = y2.shape
    row = jax.ShapeDtypeStruct((length, width), BF16)
    payload = jax.ShapeDtypeStruct((2 * length, width), BF16)
    held = pltpu.VMEM((length, width), BF16)
    return pl.pallas_call(
        dec_turn_kernel,
        name="dec_turn",
        out_shape=[row, jax.ShapeDtypeStruct(memory.shape, F32), payload, payload],
        in_specs=[SMEM] + [VMEM] * 5,
        out_specs=[VMEM] * 4,
        scratch_shapes=[held] * 8 + [pltpu.VMEM((length, width), F32)],
        compiler_params=PARAMS,
    )(flags, y2, memory, upstream, pinned(pair), gains)


def dec_backward_kernel(
    flags, upstream, memory, y1, n0, n1, q0, q1, pair, gains, done0, done1, source_low, out_own, out_other, u1, dq0, dq1, grad_source, scaled, pay0, pay1
):
    core, upper = flags[0], flags[1]

    @pl.when(upper == 0)
    def _():
        length = y1.shape[0]
        attend_backward(memory, q1, upstream, dq1, grad_source, False)
        input_backward(pair.at[1 - core], y1, gains[1:2], dq1, None, upstream, scaled, u1)
        attend_backward(memory, q0, u1, dq0, grad_source, True)
        source_low[...] = grad_source[...].astype(BF16)
        for payload, normed, grad in ((pay0, n0, dq0), (pay1, n1, dq1)):
            payload[0:length] = normed[...]
            payload[length:] = grad[...]
        by_core(core, pay0, pay1, out_own, out_other)

    @pl.when(upper == 1)
    def _():
        by_core(core, done0, done1, out_own, out_other)


def dec_backward_call(flags, upstream, memory, y1, n0, n1, q0, q1, pair, gains, done0, done1):
    length, width = upstream.shape
    payload = jax.ShapeDtypeStruct((2 * length, width), BF16)
    held = pltpu.VMEM((length, width), BF16)
    return pl.pallas_call(
        dec_backward_kernel,
        name="dec_backward",
        out_shape=[jax.ShapeDtypeStruct(memory.shape, BF16), payload, payload],
        in_specs=[SMEM] + [VMEM] * 11,
        out_specs=[VMEM] * 3,
        scratch_shapes=[held] * 3
        + [pltpu.VMEM(memory.shape, F32), pltpu.VMEM((length, width), F32)]
        + [pltpu.VMEM(payload.shape, BF16)] * 2,
        compiler_params=PARAMS,
    )(flags, upstream, memory, y1, n0, n1, q0, q1, pinned(pair), gains, done0, done1)


def put_payload(payload, grad_query, x, grad_source):
    length, width = grad_query.shape
    payload[0:length] = grad_query[...]
    place = lax.broadcasted_iota(jnp.int32, (EXTRA_ROWS, width), 0)
    payload[length:] = jnp.where(place == 0, gain_row(x, grad_source), 0.0).astype(BF16)


def enc_backward_first_kernel(
    flags, source_mine, source_recv, mem_gain, pair, gains, x0, x1, x2, n0, n1, q0, q1, out, pay0, pay1, u2, u1, grad_query, grad_source, scaled
):
    core, upper = flags[0], flags[1]

    @pl.when(upper == 1)
    def _():
        hidden = x2[...].astype(F32)
        scales = row_scale(hidden)
        grad = mem_gain[...] * (source_mine[...] + source_recv[...].astype(F32))
        mean = jnp.mean(grad * hidden, axis=-1, keepdims=True)
        u2[...] = (scales * grad - hidden * (scales * scales * scales * mean)).astype(BF16)
        attend_backward(n1, q1, u2, grad_query, grad_source, False)
        put_payload(pay1, grad_query, x1, grad_source)
        input_backward(pair.at[1 - core], x1, gains[1:2], grad_query, grad_source, u2, scaled, u1)
        attend_backward(n0, q0, u1, grad_query, grad_source, False)
        put_payload(pay0, grad_query, x0, grad_source)
        input_backward(pair.at[core], x0, gains[0:1], grad_query, grad_source, u1, scaled, out)


def enc_backward_first_call(flags, source_mine, source_recv, mem_gain, pair, gains, saved):
    length, width = saved[0].shape
    row = jax.ShapeDtypeStruct((length, width), BF16)
    payload = jax.ShapeDtypeStruct((length + EXTRA_ROWS, width), BF16)
    return pl.pallas_call(
        enc_backward_first_kernel,
        name="enc_backward_first",
        out_shape=[row, payload, payload],
        in_specs=[SMEM] + [VMEM] * 12,
        out_specs=[VMEM] * 3,
        scratch_shapes=[pltpu.VMEM((length, width), BF16)] * 3 + [pltpu.VMEM((length, width), F32)] * 2,
        compiler_params=PARAMS,
    )(flags, source_mine, source_recv, mem_gain, pinned(pair), gains, *saved)


def enc_backward_last_kernel(
    flags, upstream, done0, done1, pair, gains, x0, x1, n0, n1, q0, q1, out_own, out_other, pay0, pay1, u1, grad_query, grad_source, scaled
):
    core, upper = flags[0], flags[1]

    @pl.when(upper == 0)
    def _():
        attend_backward(n1, q1, upstream, grad_query, grad_source, False)
        put_payload(pay1, grad_query, x1, grad_source)
        input_backward(pair.at[1 - core], x1, gains[1:2], grad_query, grad_source, upstream, scaled, u1)
        attend_backward(n0, q0, u1, grad_query, grad_source, False)
        put_payload(pay0, grad_query, x0, grad_source)
        by_core(core, pay0, pay1, out_own, out_other)

    @pl.when(upper == 1)
    def _():
        by_core(core, done0, done1, out_own, out_other)


def enc_backward_last_call(flags, upstream, done0, done1, pair, gains, saved):
    x0, x1, _, n0, n1, q0, q1 = saved
    length, width = upstream.shape
    payload = jax.ShapeDtypeStruct((length + EXTRA_ROWS, width), BF16)
    return pl.pallas_call(
        enc_backward_last_kernel,
        name="enc_backward_last",
        out_shape=[payload, payload],
        in_specs=[SMEM] + [VMEM] * 11,
        out_specs=[VMEM] * 2,
        scratch_shapes=[pltpu.VMEM(payload.shape, BF16)] * 2
        + [pltpu.VMEM((length, width), BF16)] * 2
        + [pltpu.VMEM((length, width), F32)] * 2,
        compiler_params=PARAMS,
    )(flags, upstream, done0, done1, pinned(pair), gains, x0, x1, n0, n1, q0, q1)


def features(place, index, block):
    row = lax.broadcasted_iota(jnp.int32, (block, 1), 0)
    half = block // 2
    return jnp.where(row < half, place[index * 2] + row, place[index * 2 + 1] + row - half)


def ones_at(place, index, block, width):
    lanes = lax.broadcasted_iota(jnp.int32, (block, width), 1)
    return jnp.where(lanes == features(place, index, block), 1.0, 0.0).astype(BF16)


def choose_kernel(place, *refs):
    pieces, out, (ones,) = refs[:8], refs[8], refs[9:]
    length, width = pieces[0].shape
    block = out.shape[0] // 4
    for index in range(4):
        ones[index * block : (index + 1) * block] = ones_at(place, index, block, width)
    for index in range(8):
        out[:, index * length : (index + 1) * length] = dot_nt(ones[...], pieces[index][...]).astype(BF16)


def choose_call(place, pieces):
    length, width = pieces[0].shape
    return pl.pallas_call(
        choose_kernel,
        name="choose_enc",
        out_shape=jax.ShapeDtypeStruct((width // 4, 8 * length), BF16),
        in_specs=[SMEM] + [VMEM] * 8,
        out_specs=VMEM,
        scratch_shapes=[pltpu.VMEM((width // 4, width), BF16)],
        compiler_params=PARAMS,
    )(place, *pieces)


def dec_product_kernel(place, *refs):
    pieces, outs, (normed, grads) = refs[:8], refs[8:12], refs[12:]
    length = pieces[0].shape[0] // 2
    for index in range(8):
        normed[index * length : (index + 1) * length] = pieces[index][0:length]
        grads[index * length : (index + 1) * length] = pieces[index][length:]
    block = outs[0].shape[0]
    for index in range(4):
        columns = dot_nt(ones_at(place, index, block, normed.shape[1]), normed[...]).astype(BF16)
        outs[index][...] = dot(columns, grads[...]).astype(BF16)


def dec_product_call(place, pieces):
    rows, width = pieces[0].shape
    return pl.pallas_call(
        dec_product_kernel,
        name="product_dec",
        out_shape=[jax.ShapeDtypeStruct((width // 16, width), BF16)] * 4,
        in_specs=[SMEM] + [VMEM] * 8,
        out_specs=[VMEM] * 4,
        scratch_shapes=[pltpu.VMEM((4 * rows, width), BF16)] * 2,
        compiler_params=PARAMS,
    )(place, *pieces)


def enc_product_kernel(place, slices, *refs):
    pieces, outs, (held,) = refs[:8], refs[8:12], refs[12:]
    length, width = slices.shape[1] // 8, pieces[0].shape[1]
    block = slices.shape[0] // 4
    extra = jnp.zeros((EXTRA_ROWS, width), F32)
    for index in range(8):
        held[index * length : (index + 1) * length] = pieces[index][0:length]
        extra = extra + pieces[index][length:].astype(F32)
    extra = jnp.sum(extra, axis=0, keepdims=True)
    for index in range(4):
        outs[index][:, 0:width] = dot(slices[index * block : (index + 1) * block], held[...]).astype(BF16)
        lanes = lax.broadcasted_iota(jnp.int32, (block, width), 1)
        column = jnp.sum(jnp.where(lanes == features(place, index, block), extra, 0.0), axis=-1, keepdims=True)
        outs[index][:, width:] = jnp.broadcast_to(column, (block, GAIN_LANES)).astype(BF16)


def enc_product_call(place, slices, pieces):
    width = pieces[0].shape[1]
    return pl.pallas_call(
        enc_product_kernel,
        name="product_enc",
        out_shape=[jax.ShapeDtypeStruct((slices.shape[0] // 4, width + GAIN_LANES), BF16)] * 4,
        in_specs=[SMEM] + [VMEM] * 9,
        out_specs=[VMEM] * 4,
        scratch_shapes=[pltpu.VMEM((slices.shape[1], width), BF16)],
        compiler_params=PARAMS,
    )(place, slices, *pieces)


def finish_kernel(spot, low, recv, weight_any, gain, rows, gain_out, weight, sem):
    count, width = weight.shape
    copy = pltpu.make_async_copy(weight_any.at[pl.ds(pl.multiple_of(spot[0] * count, count), count)], weight, sem)
    copy.start()
    total = low[...] + recv[...].astype(F32)
    rows[...] = total[:, :width]
    copy.wait()
    column = jnp.sum(weight[...].astype(F32) * total[:, :width], axis=-1, keepdims=True) / gain[...]
    if low.shape[1] > width:
        column = column + total[:, width : width + 1]
    gain_out[...] = column


def finish_call(spot, low, recv, weight, gain):
    count, width = low.shape[0], weight.shape[1]
    return pl.pallas_call(
        finish_kernel,
        name="finish_enc" if low.shape[1] > width else "finish_dec",
        out_shape=[jax.ShapeDtypeStruct((count, width), F32), jax.ShapeDtypeStruct((count, 1), F32)],
        in_specs=[SMEM, VMEM, VMEM, HBM, VMEM],
        out_specs=[VMEM] * 2,
        scratch_shapes=[pltpu.VMEM((count, width), BF16), pltpu.SemaphoreType.DMA],
        compiler_params=PARAMS,
    )(spot, low, recv, weight, gain)


def device(pipe, high, deep, across):
    return pipe * 32 + (high % 2) * 16 + (deep % 4) * 4 + across % 4


def all_places():
    return [(pipe, high, deep, across) for pipe in range(4) for high in range(2) for deep in range(4) for across in range(4)]


def moved(place, along_x, step, flip):
    pipe, high, deep, across = place
    pipe = pipe ^ 1 if flip else pipe
    return device(pipe, high, deep, across + step) if along_x else device(pipe, high, deep + step, across)


def gather_perm(step, flip):
    return [(device(*place), moved(place, (place[0] + flip) % 2 == 0, step, flip)) for place in all_places()]


def reduce_perm(step):
    return [(device(*place), moved(place, place[0] % 2 == 1, step, 0)) for place in all_places()]


HALF_PERM = [(device(*place), device(place[0], place[1] + 1, place[2], place[3])) for place in all_places()]
SWAP_PERM = [(device(*place), device(place[0] ^ 1, *place[1:])) for place in all_places()]
UP_PERM = [
    (device(pipe, high, deep, across), device(pipe + 2, high + pipe, deep, across))
    for pipe, high, deep, across in all_places()
    if pipe < 2
]
DOWN_PERM = [(target, source) for source, target in UP_PERM]
FIRST_PERM = [(device(*place), device(place[0] + 1, *place[1:])) for place in all_places() if place[0] % 2 == 0]
OUT_PERMS = [
    [(device(1, high, deep, across), device(2 + core, high + core, deep, across)) for _, high, deep, across in all_places()[:32]]
    for core in range(2)
]


def send(value, perm):
    return lax.ppermute(value, ("pipe", "dp"), perm)


def gather(mine, other):
    return (
        [mine]
        + [send(mine, gather_perm(step, 0)) for step in (1, 2, 3)]
        + [send(other, gather_perm(step, 1)) for step in (0, 1, 2, 3)]
    )


def after(value, *earlier):
    return lax.optimization_barrier((value, earlier))[0]


def per_device(enc_in, dec_in, out_grad, enc_weight, dec_weight, enc_gain, dec_gain, mem_gain):
    pipe = lax.axis_index("pipe")
    spot = lax.axis_index("dp")
    core, upper = pipe % 2, pipe // 2
    high, deep, across = spot // 16, (spot // 4) % 4, spot % 4
    even = core == 0
    near, far = jnp.where(even, across, deep), jnp.where(even, deep, across)
    flags = jnp.stack([core, upper]).astype(jnp.int32)
    width = enc_weight.shape[1]
    mem_gain = mem_gain[None]

    def place_of(step, half):
        group, third = jnp.where(even, (far + step) % 4, near), jnp.where(even, near, (far + step) % 4)
        return ((high + half) % 2 * 16 + group * 4 + third) * (width // 32)

    place = jnp.stack([place_of(step, half) for step in range(4) for half in range(2)]).astype(jnp.int32)

    enc_own, dec_own = enc_weight[0], dec_weight[0]
    gains = jnp.concatenate([enc_gain, dec_gain], axis=0)
    gains_other = send(gains, SWAP_PERM)
    pair = jnp.where(even, jnp.stack([gains, gains_other]), jnp.stack([gains_other, gains]))
    enc_gains, dec_gains = pair[:, 0], pair[:, 1]

    x1 = send(first_call(0, flags, enc_in, enc_own, enc_gain), FIRST_PERM)
    enc_other = send(after(enc_own, x1, gains_other), SWAP_PERM)
    x2 = first_call(1, flags, x1, enc_own, enc_gain)
    received = [send(x2[sequence], OUT_PERMS[sequence]) for sequence in range(2)]
    enc_pair = load_call(enc_own, after(enc_other, x2))
    dec_other = send(after(dec_own, enc_other), SWAP_PERM)
    upstream = send(after(jnp.where(even, out_grad[0], out_grad[1]), x2), UP_PERM)
    memory, *saved, n_own, n_other = enc_forward_call(
        flags, enc_in, *received, enc_pair, enc_gains, mem_gain
    )
    memory_recv = send(memory, DOWN_PERM)
    dec_pair = load_call(dec_own, after(dec_other, memory))
    normed_pieces = gather(n_own, n_other)
    n0, q0 = dec_query_call(flags, dec_in, dec_pair, dec_gains)

    y1, y2, n1, q1 = dec_forward_call(flags, dec_in, memory_recv, q0, dec_pair, dec_gains)
    u2, source_mine, done0, done1 = dec_turn_call(
        flags, send(y2, UP_PERM), memory, upstream, dec_pair, dec_gains
    )
    source_low, dec_own_pay, dec_other_pay = dec_backward_call(
        flags, send(u2, DOWN_PERM), memory_recv, y1, n0, n1, q0, q1, dec_pair, dec_gains, done0, done1
    )
    dec_pieces = gather(dec_own_pay, dec_other_pay)
    slices = choose_call(place, after(normed_pieces, source_low))

    u_low, done0, done1 = enc_backward_first_call(
        flags, source_mine, after(send(source_low, UP_PERM), slices), mem_gain, enc_pair, enc_gains, saved
    )
    dec_blocks = dec_product_call(place, after(dec_pieces, u_low))
    own_pay, other_pay = enc_backward_last_call(
        flags, after(send(u_low, DOWN_PERM), *dec_blocks), done0, done1, enc_pair, enc_gains, saved
    )

    start = spot * (width // 32)
    spots = spot.astype(jnp.int32)[None]

    def reduced(blocks):
        total = blocks[0].astype(F32)
        for step in (1, 2, 3):
            total = total + send(blocks[step], reduce_perm(step)).astype(F32)
        return total[: width // 32], total[width // 32 :].astype(BF16)

    def gain_rows(gain):
        return lax.dynamic_slice_in_dim(gain[0], start, width // 32, 0)[:, None]

    dec_low, dec_high = reduced(dec_blocks)
    enc_pieces = after(gather(own_pay, other_pay), dec_low, dec_high)
    enc_low, enc_high = reduced(enc_product_call(place, slices, enc_pieces))
    dec_rows, dec_column = finish_call(spots, dec_low, send(dec_high, HALF_PERM), dec_own, gain_rows(dec_gain))
    enc_rows, enc_column = finish_call(spots, enc_low, send(enc_high, HALF_PERM), enc_own, gain_rows(enc_gain))
    return enc_rows[None], dec_rows[None], enc_column[None, :, 0], dec_column[None, :, 0]


def solution(mesh):
    placed = (
        P("dp", None, None),
        P("dp", None, None),
        P("dp", None, None),
        P("pipe", None, None),
        P("pipe", None, None),
        P("pipe", None),
        P("pipe", None),
        P(),
    )
    return jax.shard_map(
        per_device,
        mesh=mesh,
        in_specs=placed,
        out_specs=(P("pipe", "dp", None), P("pipe", "dp", None), P("pipe", "dp"), P("pipe", "dp")),
        check_vma=False,
    )
```

```python
import functools

import jax
import jax.numpy as jnp
from jax import lax
from jax.experimental import pallas as pl
from jax.experimental.pallas import tpu as pltpu
from jax.sharding import PartitionSpec as P

HEAD_DIM = 256
EPSILON = 1e-06
QUERY_SCALE = 0.0625
EXTRA_ROWS = 16
GAIN_LANES = 128

BF16 = jnp.bfloat16
F32 = jnp.float32
ANY = pl.BlockSpec(memory_space=pl.ANY)
SMEM = pl.BlockSpec(memory_space=pltpu.SMEM)
VMEM = pl.BlockSpec(memory_space=pltpu.VMEM)
HBM = pl.BlockSpec(memory_space=pltpu.HBM)
FIRST_PARAMS = pltpu.CompilerParams(vmem_limit_bytes=48 * 2**20)
WIDE_PARAMS = pltpu.CompilerParams(vmem_limit_bytes=52 * 2**20)
PARAMS = pltpu.CompilerParams(vmem_limit_bytes=12 * 2**20)


def dot(left, right):
    return jnp.dot(left, right, preferred_element_type=F32)


def dot_nt(left, right):
    return lax.dot_general(left, right, (((1,), (1,)), ((), ())), preferred_element_type=F32)


def dot_tn(left, right):
    return lax.dot_general(left, right, (((0,), (0,)), ((), ())), preferred_element_type=F32)


def row_scale(values):
    return lax.rsqrt(jnp.mean(values * values, axis=-1, keepdims=True) + EPSILON)


def head(index):
    return slice(index * HEAD_DIM, (index + 1) * HEAD_DIM)


def normal(x, gain):
    hidden = x[...].astype(F32)
    return (hidden * row_scale(hidden) * gain).astype(BF16)


def attend_forward(x, query, source, out):
    heads = [head(part) for part in range(x.shape[-1] // HEAD_DIM)]
    raised = [jnp.exp(dot_nt(query[:, cols], source[:, cols])) for cols in heads]
    low = [(value / jnp.sum(value, axis=-1, keepdims=True)).astype(BF16) for value in raised]
    for cols, shares in zip(heads, low):
        out[:, cols] = (x[:, cols].astype(F32) + dot(shares, source[:, cols])).astype(BF16)


def with_weight(core, section, own, other, body):
    for mine in (0, 1):

        @pl.when(core == mine)
        def _():
            body(own if mine == section else other)


def queries_of(core, section, own, other, normed, query):
    def body(weight):
        query[...] = (dot(normed[...], weight[...]) * QUERY_SCALE).astype(BF16)

    with_weight(core, section, own, other, body)


def attend_backward(source, query, upstream, grad_query, grad_source, add):
    heads = [head(part) for part in range(source.shape[-1] // HEAD_DIM)]
    length = query.shape[0]
    if length % 128 == 0:
        sides = [jnp.concatenate([query[:, cols], upstream[:, cols]], axis=0) for cols in heads]
        both = [dot_nt(source[:, cols], side) for cols, side in zip(heads, sides)]
        raised = [jnp.exp(value[:, :length]) for value in both]
        grads = [value[:, length:] for value in both]
    else:
        raised = [jnp.exp(dot_nt(source[:, cols], query[:, cols])) for cols in heads]
        grads = [dot_nt(source[:, cols], upstream[:, cols]) for cols in heads]
    probs = [value / jnp.sum(value, axis=0, keepdims=True) for value in raised]
    scores = [
        (share * (grad - jnp.sum(grad * share, axis=0, keepdims=True))).astype(BF16) for share, grad in zip(probs, grads)
    ]
    for part, cols in enumerate(heads):
        low = probs[part].astype(BF16)
        grad_query[:, cols] = (dot_tn(scores[part], source[:, cols]) * QUERY_SCALE).astype(BF16)
        if length % 128 == 0:
            total = dot(jnp.concatenate([scores[part], low], axis=1), sides[part])
        else:
            total = dot(scores[part], query[:, cols]) + dot(low, upstream[:, cols])
        grad_source[:, cols] = grad_source[:, cols] + total if add else total


def grad_normed(weight, grad_query, scaled, wait=None):
    length, width = grad_query.shape
    for part in range(width // HEAD_DIM):
        cols = head(part)
        if wait is not None:
            wait(part)
        if length % 128 == 0:
            scaled[:, cols] = dot_nt(weight[cols, :], grad_query[...]).T
        else:
            scaled[:, cols] = dot_nt(grad_query[...], weight[cols, :])


def input_backward(x, gain, grad_source, upstream, scaled, out):
    hidden = x[...].astype(F32)
    scales = row_scale(hidden)
    grad = scaled[...] if grad_source is None else scaled[...] + grad_source[...]
    grad = gain * grad
    mean = jnp.mean(grad * hidden, axis=-1, keepdims=True)
    factor = scales * scales * scales * mean
    out[...] = (upstream[...].astype(F32) + scales * grad - hidden * factor).astype(BF16)


def dec_input_backward(core, section, own, other, x, gain, grad_query, upstream, scaled, out):
    with_weight(core, section, own, other, lambda weight: grad_normed(weight, grad_query, scaled))
    input_backward(x, gain, None, upstream, scaled, out)


def row_copy(source, buffer, sems, slot, part):
    return pltpu.make_async_copy(source.at[head(part)], buffer.at[slot, head(part)], sems.at[slot, part])


def start_rows(core, own, other, buffer, sems, slots):
    for mine in (0, 1):

        @pl.when(core == mine)
        def _():
            for slot in slots:
                for part in range(own.shape[0] // HEAD_DIM):
                    row_copy(own if slot == mine else other, buffer, sems, slot, part).start()


def gain_row(x, grad_source):
    hidden = x[...].astype(F32)
    return jnp.sum(grad_source[...] * hidden * row_scale(hidden), axis=0, keepdims=True)


def by_core(core, low, high, own, other):
    for mine in (0, 1):

        @pl.when(core == mine)
        def _():
            own[...] = high[...] if mine else low[...]
            other[...] = low[...] if mine else high[...]


def load_kernel(source, gate, out, sem):
    copy = pltpu.make_async_copy(source, out, sem)
    copy.start()
    copy.wait()


def load_call(weight, gate):
    out = pl.pallas_call(
        load_kernel,
        name="load_weight",
        out_shape=pltpu.VMEM(weight.shape, BF16),
        in_specs=[ANY, ANY],
        out_specs=VMEM,
        scratch_shapes=[pltpu.SemaphoreType.DMA],
        compiler_params=PARAMS,
    )(weight, gate)
    return pinned(out)


def pinned(value):
    return pltpu.with_memory_space_constraint(value, pltpu.VMEM)


def gate_call(weight, gate):
    out = pl.pallas_call(
        lambda weight, gate, out: None,
        name="gate",
        out_shape=pltpu.VMEM(weight.shape, BF16),
        in_specs=[VMEM, ANY],
        out_specs=VMEM,
        input_output_aliases={0: 0},
        compiler_params=PARAMS,
    )(weight, gate)
    return pinned(out)


def both_sequences(x, normed, query, out):
    count, length, width = x.shape
    for sequence in range(count):
        rows = pl.ds(sequence * length, length)
        attend_forward(x.at[sequence], query.at[rows], normed.at[rows], out.at[sequence])


def both_normal(x, gain, normed):
    count, length, width = x.shape
    for sequence in range(count):
        normed[sequence * length : (sequence + 1) * length] = normal(x.at[sequence], gain[...])


def first_lower_kernel(flags, x, weight_any, gain, out, weight, normed, query, sems):
    parts = range(x.shape[-1] // HEAD_DIM)
    copies = [
        pltpu.make_async_copy(weight_any.at[:, head(part)], weight.at[:, head(part)], sems.at[part]) for part in parts
    ]
    for copy in copies:
        copy.start()
    active = jnp.logical_and(flags[0] == 0, flags[1] == 0)

    @pl.when(active)
    def _():
        both_normal(x, gain, normed)
        for part in parts:
            copies[part].wait()
            query[:, head(part)] = (dot(normed[...], weight[:, head(part)]) * QUERY_SCALE).astype(BF16)
        both_sequences(x, normed, query, out)

    @pl.when(jnp.logical_not(active))
    def _():
        for copy in copies:
            copy.wait()


def first_upper_kernel(flags, x, weight, gain, out, normed, query):
    @pl.when(jnp.logical_and(flags[0] == 1, flags[1] == 0))
    def _():
        both_normal(x, gain, normed)
        query[...] = (dot(normed[...], weight[...]) * QUERY_SCALE).astype(BF16)
        both_sequences(x, normed, query, out)


def first_lower_call(flags, x, weight, gain):
    count, length, width = x.shape
    out, held = pl.pallas_call(
        first_lower_kernel,
        name="enc_first_lower",
        out_shape=[jax.ShapeDtypeStruct(x.shape, BF16), pltpu.VMEM((width, width), BF16)],
        in_specs=[SMEM, VMEM, ANY, VMEM],
        out_specs=[VMEM] * 2,
        scratch_shapes=[pltpu.VMEM((count * length, width), BF16)] * 2
        + [pltpu.SemaphoreType.DMA((width // HEAD_DIM,))],
        compiler_params=FIRST_PARAMS,
    )(flags, x, weight, gain)
    return out, pinned(held)


def first_upper_call(flags, x, weight, gain):
    count, length, width = x.shape
    return pl.pallas_call(
        first_upper_kernel,
        name="enc_first_upper",
        out_shape=jax.ShapeDtypeStruct(x.shape, BF16),
        in_specs=[SMEM, VMEM, VMEM, VMEM],
        out_specs=VMEM,
        scratch_shapes=[pltpu.VMEM((count * length, width), BF16)] * 2,
        compiler_params=PARAMS,
    )(flags, x, weight, gain)


def enc_forward_kernel(
    flags, x_any, recv0, recv1, own, other, gains, mem_gain, mem, x0, x1, x2, n0, n1, q0, q1, n_own, n_other, sem
):
    core, upper = flags[0], flags[1]

    @pl.when(upper == 0)
    def _():
        pltpu.make_async_copy(x_any.at[core], x0, sem).start()

    for mine, received in enumerate((recv0, recv1)):

        @pl.when(jnp.logical_and(upper == 1, core == mine))
        def _():
            pltpu.make_async_copy(received, x0, sem).start()

    pltpu.make_async_copy(recv0, x0, sem).wait()
    n0[...] = normal(x0, gains[0:1])
    queries_of(core, 0, own, other, n0, q0)
    attend_forward(x0, q0, n0, x1)
    n1[...] = normal(x1, gains[1:2])
    queries_of(core, 1, own, other, n1, q1)
    attend_forward(x1, q1, n1, x2)
    mem[...] = normal(x2, mem_gain[...])
    by_core(core, n0, n1, n_own, n_other)


def enc_forward_call(flags, x, recv0, recv1, own, other, gains, mem_gain):
    row = jax.ShapeDtypeStruct(recv0.shape, BF16)
    return pl.pallas_call(
        enc_forward_kernel,
        name="enc_forward",
        out_shape=[row] * 10,
        in_specs=[SMEM, ANY, ANY, ANY] + [VMEM] * 4,
        out_specs=[VMEM] * 10,
        scratch_shapes=[pltpu.SemaphoreType.DMA],
        compiler_params=PARAMS,
    )(flags, x, recv0, recv1, own, other, gains, mem_gain)


def dec_query_kernel(flags, x_any, own, other, gains, n0, q0, sem, y0):
    core, upper = flags[0], flags[1]

    @pl.when(upper == 0)
    def _():
        rows = pltpu.make_async_copy(x_any.at[core], y0, sem)
        rows.start()
        rows.wait()
        n0[...] = normal(y0, gains[0:1])
        queries_of(core, 0, own, other, n0, q0)


def dec_query_call(flags, x, own, other, gains):
    row = jax.ShapeDtypeStruct(x.shape[1:], BF16)
    return pl.pallas_call(
        dec_query_kernel,
        name="dec_query",
        out_shape=[row] * 2,
        in_specs=[SMEM, ANY, VMEM, VMEM, VMEM],
        out_specs=[VMEM] * 2,
        scratch_shapes=[pltpu.SemaphoreType.DMA, pltpu.VMEM(x.shape[1:], BF16)],
        compiler_params=PARAMS,
    )(flags, x, own, other, gains)


def dec_forward_kernel(flags, x_any, memory, q0, own, other, gains, y1, y2, n1, q1, sem, y0):
    core, upper = flags[0], flags[1]

    @pl.when(upper == 0)
    def _():
        rows = pltpu.make_async_copy(x_any.at[core], y0, sem)
        rows.start()
        rows.wait()
        attend_forward(y0, q0, memory, y1)
        n1[...] = normal(y1, gains[1:2])
        queries_of(core, 1, own, other, n1, q1)
        attend_forward(y1, q1, memory, y2)


def dec_forward_call(flags, x, memory, q0, own, other, gains):
    row = jax.ShapeDtypeStruct(x.shape[1:], BF16)
    return pl.pallas_call(
        dec_forward_kernel,
        name="dec_forward",
        out_shape=[row] * 4,
        in_specs=[SMEM, ANY] + [VMEM] * 5,
        out_specs=[VMEM] * 4,
        scratch_shapes=[pltpu.SemaphoreType.DMA, pltpu.VMEM(x.shape[1:], BF16)],
        compiler_params=PARAMS,
    )(flags, x, memory, q0, own, other, gains)


def dec_turn_kernel(
    flags, y2, memory, upstream, own, other, gains, out, grad_source, pay0, pay1, n0, n1, y3, u3, q0, q1, dq0, dq1, scaled
):
    core, upper = flags[0], flags[1]

    @pl.when(upper == 1)
    def _():
        length = y2.shape[0]
        n0[...] = normal(y2, gains[0:1])
        queries_of(core, 0, own, other, n0, q0)
        attend_forward(y2, q0, memory, y3)
        n1[...] = normal(y3, gains[1:2])
        queries_of(core, 1, own, other, n1, q1)
        attend_backward(memory, q1, upstream, dq1, grad_source, False)
        dec_input_backward(core, 1, own, other, y3, gains[1:2], dq1, upstream, scaled, u3)
        attend_backward(memory, q0, u3, dq0, grad_source, True)
        dec_input_backward(core, 0, own, other, y2, gains[0:1], dq0, u3, scaled, out)
        for payload, normed, grad in ((pay0, n0, dq0), (pay1, n1, dq1)):
            payload[0:length] = normed[...]
            payload[length:] = grad[...]


def dec_turn_call(flags, y2, memory, upstream, own, other, gains):
    length, width = y2.shape
    row = jax.ShapeDtypeStruct((length, width), BF16)
    payload = jax.ShapeDtypeStruct((2 * length, width), BF16)
    held = pltpu.VMEM((length, width), BF16)
    return pl.pallas_call(
        dec_turn_kernel,
        name="dec_turn",
        out_shape=[row, jax.ShapeDtypeStruct(memory.shape, F32), payload, payload],
        in_specs=[SMEM] + [VMEM] * 6,
        out_specs=[VMEM] * 4,
        scratch_shapes=[held] * 8 + [pltpu.VMEM((length, width), F32)],
        compiler_params=PARAMS,
    )(flags, y2, memory, upstream, own, other, gains)


def dec_backward_kernel(
    flags, upstream, memory, y1, n0, n1, q0, q1, own, other, gains, done0, done1, gate, source_low, out_own, out_other, u1, dq0, dq1, grad_source, scaled, pay0, pay1
):
    core, upper = flags[0], flags[1]

    @pl.when(upper == 0)
    def _():
        length = y1.shape[0]
        attend_backward(memory, q1, upstream, dq1, grad_source, False)
        dec_input_backward(core, 1, own, other, y1, gains[1:2], dq1, upstream, scaled, u1)
        attend_backward(memory, q0, u1, dq0, grad_source, True)
        source_low[...] = grad_source[...].astype(BF16)
        for payload, normed, grad in ((pay0, n0, dq0), (pay1, n1, dq1)):
            payload[0:length] = normed[...]
            payload[length:] = grad[...]
        by_core(core, pay0, pay1, out_own, out_other)

    @pl.when(upper == 1)
    def _():
        by_core(core, done0, done1, out_own, out_other)


def dec_backward_call(flags, upstream, memory, y1, n0, n1, q0, q1, own, other, gains, done0, done1, gate):
    length, width = upstream.shape
    payload = jax.ShapeDtypeStruct((2 * length, width), BF16)
    held = pltpu.VMEM((length, width), BF16)
    return pl.pallas_call(
        dec_backward_kernel,
        name="dec_backward",
        out_shape=[jax.ShapeDtypeStruct(memory.shape, BF16), payload, payload],
        in_specs=[SMEM] + [VMEM] * 12 + [ANY],
        out_specs=[VMEM] * 3,
        scratch_shapes=[held] * 3
        + [pltpu.VMEM(memory.shape, F32), pltpu.VMEM((length, width), F32)]
        + [pltpu.VMEM(payload.shape, BF16)] * 2,
        compiler_params=PARAMS,
    )(flags, upstream, memory, y1, n0, n1, q0, q1, own, other, gains, done0, done1, gate)


def put_payload(payload, grad_query, x, grad_source):
    length, width = grad_query.shape
    payload[0:length] = grad_query[...]
    place = lax.broadcasted_iota(jnp.int32, (EXTRA_ROWS, width), 0)
    payload[length:] = jnp.where(place == 0, gain_row(x, grad_source), 0.0).astype(BF16)


def enc_backward_first_kernel(
    flags, source_mine, source_recv, mem_gain, own, other, gains, x0, x1, x2, n0, n1, q0, q1, out, pay0, pay1, weight, weight_sems, u2, u1, grad_query, grad_source, scaled
):
    core, upper = flags[0], flags[1]

    @pl.when(upper == 1)
    def _():
        start_rows(core, own, other, weight, weight_sems, (1, 0))
        hidden = x2[...].astype(F32)
        scales = row_scale(hidden)
        grad = mem_gain[...] * (source_mine[...] + source_recv[...].astype(F32))
        mean = jnp.mean(grad * hidden, axis=-1, keepdims=True)
        u2[...] = (scales * grad - hidden * (scales * scales * scales * mean)).astype(BF16)
        attend_backward(n1, q1, u2, grad_query, grad_source, False)
        put_payload(pay1, grad_query, x1, grad_source)
        wait = lambda part: row_copy(own, weight, weight_sems, 1, part).wait()
        grad_normed(weight.at[1], grad_query, scaled, wait)
        input_backward(x1, gains[1:2], grad_source, u2, scaled, u1)
        attend_backward(n0, q0, u1, grad_query, grad_source, False)
        put_payload(pay0, grad_query, x0, grad_source)
        wait = lambda part: row_copy(own, weight, weight_sems, 0, part).wait()
        grad_normed(weight.at[0], grad_query, scaled, wait)
        input_backward(x0, gains[0:1], grad_source, u1, scaled, out)


def enc_backward_first_call(flags, source_mine, source_recv, mem_gain, own, other, gains, saved):
    length, width = saved[0].shape
    row = jax.ShapeDtypeStruct((length, width), BF16)
    payload = jax.ShapeDtypeStruct((length + EXTRA_ROWS, width), BF16)
    return pl.pallas_call(
        enc_backward_first_kernel,
        name="enc_backward_first",
        out_shape=[row, payload, payload],
        in_specs=[SMEM] + [VMEM] * 3 + [ANY] * 2 + [VMEM] * 8,
        out_specs=[VMEM] * 3,
        scratch_shapes=[pltpu.VMEM((2, width, width), BF16), pltpu.SemaphoreType.DMA((2, width // HEAD_DIM))]
        + [pltpu.VMEM((length, width), BF16)] * 3
        + [pltpu.VMEM((length, width), F32)] * 2,
        compiler_params=WIDE_PARAMS,
    )(flags, source_mine, source_recv, mem_gain, own, other, gains, *saved)


def enc_backward_last_kernel(
    flags, upstream, done0, done1, own, other, gains, x0, x1, n0, n1, q0, q1, gate, out_own, out_other, weight, weight_sems, pay0, pay1, u1, grad_query, grad_source, scaled
):
    core, upper = flags[0], flags[1]

    @pl.when(upper == 0)
    def _():
        start_rows(core, own, other, weight, weight_sems, (1,))
        attend_backward(n1, q1, upstream, grad_query, grad_source, False)
        put_payload(pay1, grad_query, x1, grad_source)
        wait = lambda part: row_copy(own, weight, weight_sems, 1, part).wait()
        grad_normed(weight.at[1], grad_query, scaled, wait)
        input_backward(x1, gains[1:2], grad_source, upstream, scaled, u1)
        attend_backward(n0, q0, u1, grad_query, grad_source, False)
        put_payload(pay0, grad_query, x0, grad_source)
        by_core(core, pay0, pay1, out_own, out_other)

    @pl.when(upper == 1)
    def _():
        by_core(core, done0, done1, out_own, out_other)


def enc_backward_last_call(flags, upstream, done0, done1, own, other, gains, saved, gate):
    x0, x1, _, n0, n1, q0, q1 = saved
    length, width = upstream.shape
    payload = jax.ShapeDtypeStruct((length + EXTRA_ROWS, width), BF16)
    return pl.pallas_call(
        enc_backward_last_kernel,
        name="enc_backward_last",
        out_shape=[payload, payload],
        in_specs=[SMEM] + [VMEM] * 3 + [ANY] * 2 + [VMEM] * 7 + [ANY],
        out_specs=[VMEM] * 2,
        scratch_shapes=[pltpu.VMEM((2, width, width), BF16), pltpu.SemaphoreType.DMA((2, width // HEAD_DIM))]
        + [pltpu.VMEM(payload.shape, BF16)] * 2
        + [pltpu.VMEM((length, width), BF16)] * 2
        + [pltpu.VMEM((length, width), F32)] * 2,
        compiler_params=WIDE_PARAMS,
    )(flags, upstream, done0, done1, own, other, gains, x0, x1, n0, n1, q0, q1, gate)


def features(place, index, block):
    row = lax.broadcasted_iota(jnp.int32, (block, 1), 0)
    half = block // 2
    return jnp.where(row < half, place[index * 2] + row, place[index * 2 + 1] + row - half)


def ones_at(place, index, block, width):
    lanes = lax.broadcasted_iota(jnp.int32, (block, width), 1)
    return jnp.where(lanes == features(place, index, block), 1.0, 0.0).astype(BF16)


def choose_kernel(place, *refs):
    pieces, out, (ones,) = refs[:4], refs[5], refs[6:]
    rows, width = pieces[0].shape
    block = out.shape[0] // 4
    for index in range(4):
        ones[index * block : (index + 1) * block] = ones_at(place, index, block, width)
    for index in range(4):
        out[:, index * rows : (index + 1) * rows] = dot_nt(ones[...], pieces[index][...]).astype(BF16)


def choose_call(place, pieces, gate):
    rows, width = pieces[0].shape
    return pl.pallas_call(
        choose_kernel,
        name="choose_enc",
        out_shape=jax.ShapeDtypeStruct((width // 4, 4 * rows), BF16),
        in_specs=[SMEM] + [VMEM] * 4 + [ANY],
        out_specs=VMEM,
        scratch_shapes=[pltpu.VMEM((width // 4, width), BF16)],
        compiler_params=PARAMS,
    )(place, *pieces, gate)


def dec_product_kernel(place, *refs):
    pieces, outs, (normed, grads) = refs[:4], refs[4:8], refs[8:]
    length = pieces[0].shape[0] // 4
    for index in range(8):
        start = index % 2 * 2 * length
        normed[index * length : (index + 1) * length] = pieces[index // 2][start : start + length]
        grads[index * length : (index + 1) * length] = pieces[index // 2][start + length : start + 2 * length]
    block = outs[0].shape[0]
    for index in range(4):
        columns = dot_nt(ones_at(place, index, block, normed.shape[1]), normed[...]).astype(BF16)
        outs[index][...] = dot(columns, grads[...]).astype(BF16)


def dec_product_call(place, pieces):
    rows, width = pieces[0].shape
    return pl.pallas_call(
        dec_product_kernel,
        name="product_dec",
        out_shape=[jax.ShapeDtypeStruct((width // 16, width), BF16)] * 4,
        in_specs=[SMEM] + [VMEM] * 4,
        out_specs=[VMEM] * 4,
        scratch_shapes=[pltpu.VMEM((2 * rows, width), BF16)] * 2,
        compiler_params=PARAMS,
    )(place, *pieces)


def enc_product_kernel(place, slices, *refs):
    pieces, outs, (held,) = refs[:4], refs[4:8], refs[8:]
    length, width = slices.shape[1] // 8, pieces[0].shape[1]
    block = slices.shape[0] // 4
    extra = jnp.zeros((EXTRA_ROWS, width), F32)
    for index in range(8):
        start = index % 2 * (length + EXTRA_ROWS)
        held[index * length : (index + 1) * length] = pieces[index // 2][start : start + length]
        extra = extra + pieces[index // 2][start + length : start + length + EXTRA_ROWS].astype(F32)
    extra = jnp.sum(extra, axis=0, keepdims=True)
    for index in range(4):
        outs[index][:, 0:width] = dot(slices[index * block : (index + 1) * block], held[...]).astype(BF16)
        lanes = lax.broadcasted_iota(jnp.int32, (block, width), 1)
        column = jnp.sum(jnp.where(lanes == features(place, index, block), extra, 0.0), axis=-1, keepdims=True)
        outs[index][:, width:] = jnp.broadcast_to(column, (block, GAIN_LANES)).astype(BF16)


def enc_product_call(place, slices, pieces):
    width = pieces[0].shape[1]
    return pl.pallas_call(
        enc_product_kernel,
        name="product_enc",
        out_shape=[jax.ShapeDtypeStruct((slices.shape[0] // 4, width + GAIN_LANES), BF16)] * 4,
        in_specs=[SMEM] + [VMEM] * 5,
        out_specs=[VMEM] * 4,
        scratch_shapes=[pltpu.VMEM((slices.shape[1], width), BF16)],
        compiler_params=PARAMS,
    )(place, slices, *pieces)


def finish_kernel(spot, low, recv, weight_any, gain, rows, gain_out, weight, sem):
    count, width = weight.shape
    copy = pltpu.make_async_copy(weight_any.at[pl.ds(pl.multiple_of(spot[0] * count, count), count)], weight, sem)
    copy.start()
    total = low[...] + recv[...].astype(F32)
    rows[...] = total[:, :width]
    copy.wait()
    column = jnp.sum(weight[...].astype(F32) * total[:, :width], axis=-1, keepdims=True) / gain[...]
    if low.shape[1] > width:
        column = column + total[:, width : width + 1]
    gain_out[...] = column


def finish_call(spot, low, recv, weight, gain):
    count, width = low.shape[0], weight.shape[1]
    return pl.pallas_call(
        finish_kernel,
        name="finish_enc" if low.shape[1] > width else "finish_dec",
        out_shape=[jax.ShapeDtypeStruct((count, width), F32), jax.ShapeDtypeStruct((count, 1), F32)],
        in_specs=[SMEM, VMEM, VMEM, HBM, VMEM],
        out_specs=[VMEM] * 2,
        scratch_shapes=[pltpu.VMEM((count, width), BF16), pltpu.SemaphoreType.DMA],
        compiler_params=PARAMS,
    )(spot, low, recv, weight, gain)


def device(pipe, high, deep, across):
    return pipe * 32 + (high % 2) * 16 + (deep % 4) * 4 + across % 4


def all_places():
    return [(pipe, high, deep, across) for pipe in range(4) for high in range(2) for deep in range(4) for across in range(4)]


def moved(place, along_x, step):
    pipe, high, deep, across = place
    return device(pipe, high, deep, across + step) if along_x else device(pipe, high, deep + step, across)


def gather_perm(step):
    return [(device(*place), moved(place, place[0] % 2 == 0, step)) for place in all_places()]


def reduce_perm(step):
    return [(device(*place), moved(place, place[0] % 2 == 1, step)) for place in all_places()]


HALF_PERM = [(device(*place), device(place[0], place[1] + 1, place[2], place[3])) for place in all_places()]
SWAP_PERM = [(device(*place), device(place[0] ^ 1, *place[1:])) for place in all_places()]
UP_PERM = [
    (device(pipe, high, deep, across), device(pipe + 2, high + pipe, deep, across))
    for pipe, high, deep, across in all_places()
    if pipe < 2
]
DOWN_PERM = [(target, source) for source, target in UP_PERM]
FIRST_PERM = [(device(*place), device(place[0] + 1, *place[1:])) for place in all_places() if place[0] % 2 == 0]
OUT_PERMS = [
    [(device(1, high, deep, across), device(2 + core, high + core, deep, across)) for _, high, deep, across in all_places()[:32]]
    for core in range(2)
]


def send(value, perm):
    return lax.ppermute(value, ("pipe", "dp"), perm)


def gather(mine, other):
    whole = jnp.concatenate([mine, send(other, SWAP_PERM)], axis=0)
    return [whole] + [send(whole, gather_perm(step)) for step in (1, 2, 3)]


def per_device(enc_in, dec_in, out_grad, enc_weight, dec_weight, enc_gain, dec_gain, mem_gain):
    pipe = lax.axis_index("pipe")
    spot = lax.axis_index("dp")
    core, upper = pipe % 2, pipe // 2
    high, deep, across = spot // 16, (spot // 4) % 4, spot % 4
    even = core == 0
    near, far = jnp.where(even, across, deep), jnp.where(even, deep, across)
    flags = jnp.stack([core, upper]).astype(jnp.int32)
    width = enc_weight.shape[1]
    mem_gain = mem_gain[None]

    def place_of(step, half):
        group, third = jnp.where(even, (far + step) % 4, near), jnp.where(even, near, (far + step) % 4)
        return ((high + half) % 2 * 16 + group * 4 + third) * (width // 32)

    place = jnp.stack([place_of(step, half) for step in range(4) for half in range(2)]).astype(jnp.int32)

    enc_own, dec_own = enc_weight[0], dec_weight[0]
    gains = jnp.concatenate([enc_gain, dec_gain], axis=0)
    gains_other = send(gains, SWAP_PERM)
    pair = jnp.where(even, jnp.stack([gains, gains_other]), jnp.stack([gains_other, gains]))
    enc_gains, dec_gains = pair[:, 0], pair[:, 1]

    x1, held = first_lower_call(flags, enc_in, enc_own, enc_gain)
    x1 = send(x1, FIRST_PERM)
    held = gate_call(held, x1)
    enc_other = send(held, SWAP_PERM)
    x2 = first_upper_call(flags, x1, held, enc_gain)
    received = [send(x2[sequence], OUT_PERMS[sequence]) for sequence in range(2)]
    held_other = load_call(enc_other, x2)
    dec_held = load_call(dec_own, held_other)
    dec_other = send(dec_held, SWAP_PERM)
    memory, *saved, n_own, n_other = enc_forward_call(flags, enc_in, *received, held, held_other, enc_gains, mem_gain)
    memory_recv = send(memory, DOWN_PERM)
    normed_pieces = gather(n_own, n_other)
    upstream = send(jnp.where(even, out_grad[0], out_grad[1]), UP_PERM)
    dec_weights = (dec_held, load_call(dec_other, memory))
    n0, q0 = dec_query_call(flags, dec_in, *dec_weights, dec_gains)

    y1, y2, n1, q1 = dec_forward_call(flags, dec_in, memory_recv, q0, *dec_weights, dec_gains)
    u2, source_mine, done0, done1 = dec_turn_call(
        flags, send(y2, UP_PERM), memory, upstream, *dec_weights, dec_gains
    )
    slices = choose_call(place, normed_pieces, source_mine)
    source_low, dec_own_pay, dec_other_pay = dec_backward_call(
        flags, send(u2, DOWN_PERM), memory_recv, y1, n0, n1, q0, q1, *dec_weights, dec_gains, done0, done1, slices
    )
    dec_pieces = gather(dec_own_pay, dec_other_pay)

    u_low, done0, done1 = enc_backward_first_call(
        flags, source_mine, send(source_low, UP_PERM), mem_gain, enc_own, enc_other, enc_gains, saved
    )
    dec_blocks = dec_product_call(place, dec_pieces)
    own_pay, other_pay = enc_backward_last_call(
        flags, send(u_low, DOWN_PERM), done0, done1, enc_own, enc_other, enc_gains, saved, dec_blocks[0]
    )

    start = spot * (width // 32)
    spots = spot.astype(jnp.int32)[None]

    def reduced(blocks):
        total = blocks[0].astype(F32)
        for step in (1, 2, 3):
            total = total + send(blocks[step], reduce_perm(step)).astype(F32)
        return total[: width // 32], total[width // 32 :].astype(BF16)

    def gain_rows(gain):
        return lax.dynamic_slice_in_dim(gain[0], start, width // 32, 0)[:, None]

    dec_low, dec_high = reduced(dec_blocks)
    enc_low, enc_high = reduced(enc_product_call(place, slices, gather(own_pay, other_pay)))
    dec_rows, dec_column = finish_call(spots, dec_low, send(dec_high, HALF_PERM), dec_own, gain_rows(dec_gain))
    enc_rows, enc_column = finish_call(spots, enc_low, send(enc_high, HALF_PERM), enc_own, gain_rows(enc_gain))
    return enc_rows[None], dec_rows[None], enc_column[None, :, 0], dec_column[None, :, 0]


def solution(mesh):
    placed = (
        P("dp", None, None),
        P("dp", None, None),
        P("dp", None, None),
        P("pipe", None, None),
        P("pipe", None, None),
        P("pipe", None),
        P("pipe", None),
        P(),
    )
    return jax.shard_map(
        per_device,
        mesh=mesh,
        in_specs=placed,
        out_specs=(P("pipe", "dp", None), P("pipe", "dp", None), P("pipe", "dp"), P("pipe", "dp")),
        check_vma=False,
    )
```

```python
import functools

import jax
import jax.numpy as jnp
from jax import lax
from jax.experimental import pallas as pl
from jax.experimental.pallas import tpu as pltpu
from jax.sharding import PartitionSpec as P

HEAD_DIM = 256
EPSILON = 1e-06
QUERY_SCALE = 0.0625
EXTRA_ROWS = 16
GAIN_LANES = 128

BF16 = jnp.bfloat16
F32 = jnp.float32
def takes(microseconds):
    return pl.CostEstimate(flops=int(microseconds * 10**9), bytes_accessed=0, transcendentals=0)


ANY = pl.BlockSpec(memory_space=pl.ANY)
SMEM = pl.BlockSpec(memory_space=pltpu.SMEM)
VMEM = pl.BlockSpec(memory_space=pltpu.VMEM)
HBM = pl.BlockSpec(memory_space=pltpu.HBM)
PARAMS = pltpu.CompilerParams(vmem_limit_bytes=18 * 2**20)


def dot(left, right):
    return jnp.dot(left, right, preferred_element_type=F32)


def dot_nt(left, right):
    return lax.dot_general(left, right, (((1,), (1,)), ((), ())), preferred_element_type=F32)


def dot_tn(left, right):
    return lax.dot_general(left, right, (((0,), (0,)), ((), ())), preferred_element_type=F32)


def row_scale(values):
    return lax.rsqrt(jnp.mean(values * values, axis=-1, keepdims=True) + EPSILON)


def head(index):
    return slice(index * HEAD_DIM, (index + 1) * HEAD_DIM)


def normal(x, gain):
    hidden = x[...].astype(F32)
    return (hidden * row_scale(hidden) * gain).astype(BF16)


def attend_forward(x, query, source, out):
    heads = [head(part) for part in range(x.shape[-1] // HEAD_DIM)]
    raised = [jnp.exp(dot_nt(query[:, cols], source[:, cols])) for cols in heads]
    low = [(value / jnp.sum(value, axis=-1, keepdims=True)).astype(BF16) for value in raised]
    for cols, shares in zip(heads, low):
        out[:, cols] = (x[:, cols].astype(F32) + dot(shares, source[:, cols])).astype(BF16)


def queries_of(weight, normed, query):
    query[...] = (dot(normed[...], weight[...]) * QUERY_SCALE).astype(BF16)


def attend_backward(source, query, upstream, grad_query, grad_source, add):
    heads = [head(part) for part in range(source.shape[-1] // HEAD_DIM)]
    length = query.shape[0]
    if length % 128 == 0:
        sides = [jnp.concatenate([query[:, cols], upstream[:, cols]], axis=0) for cols in heads]
        both = [dot_nt(source[:, cols], side) for cols, side in zip(heads, sides)]
        raised = [jnp.exp(value[:, :length]) for value in both]
        grads = [value[:, length:] for value in both]
    else:
        raised = [jnp.exp(dot_nt(source[:, cols], query[:, cols])) for cols in heads]
        grads = [dot_nt(source[:, cols], upstream[:, cols]) for cols in heads]
    probs = [value / jnp.sum(value, axis=0, keepdims=True) for value in raised]
    scores = [
        (share * (grad - jnp.sum(grad * share, axis=0, keepdims=True))).astype(BF16) for share, grad in zip(probs, grads)
    ]
    for part, cols in enumerate(heads):
        low = probs[part].astype(BF16)
        grad_query[:, cols] = (dot_tn(scores[part], source[:, cols]) * QUERY_SCALE).astype(BF16)
        if length % 128 == 0:
            total = dot(jnp.concatenate([scores[part], low], axis=1), sides[part])
        else:
            total = dot(scores[part], query[:, cols]) + dot(low, upstream[:, cols])
        grad_source[:, cols] = grad_source[:, cols] + total if add else total


def grad_normed(weight, grad_query, scaled, wait=None):
    length, width = grad_query.shape
    for part in range(width // HEAD_DIM):
        cols = head(part)
        if wait is not None:
            wait(part)
        if length % 128 == 0:
            scaled[:, cols] = dot_nt(weight[cols, :], grad_query[...]).T
        else:
            scaled[:, cols] = dot_nt(grad_query[...], weight[cols, :])


def input_backward(x, gain, grad_source, upstream, scaled, out):
    hidden = x[...].astype(F32)
    scales = row_scale(hidden)
    grad = scaled[...] if grad_source is None else scaled[...] + grad_source[...]
    grad = gain * grad
    mean = jnp.mean(grad * hidden, axis=-1, keepdims=True)
    factor = scales * scales * scales * mean
    out[...] = (upstream[...].astype(F32) + scales * grad - hidden * factor).astype(BF16)


def dec_input_backward(weight, x, gain, grad_query, upstream, scaled, out):
    grad_normed(weight, grad_query, scaled)
    input_backward(x, gain, None, upstream, scaled, out)


def row_copy(source, buffer, sems, part):
    return pltpu.make_async_copy(source.at[head(part)], buffer.at[head(part)], sems.at[part])


def start_rows(core, section, own, other, buffer, sems):
    for mine in (0, 1):

        @pl.when(core == mine)
        def _():
            for part in range(own.shape[0] // HEAD_DIM):
                row_copy(own if section == mine else other, buffer, sems, part).start()


def gain_row(x, grad_source):
    hidden = x[...].astype(F32)
    return jnp.sum(grad_source[...] * hidden * row_scale(hidden), axis=0, keepdims=True)


def by_core(core, low, high, own, other):
    for mine in (0, 1):

        @pl.when(core == mine)
        def _():
            own[...] = high[...] if mine else low[...]
            other[...] = low[...] if mine else high[...]


def load_kernel(own, other, gate, pair, sems):
    copies = [pltpu.make_async_copy(part, pair.at[slot], sems.at[slot]) for slot, part in enumerate((own, other))]
    for copy in copies:
        copy.start()
    for copy in copies:
        copy.wait()


def load_call(own, other, gate):
    pair = pl.pallas_call(
        load_kernel,
        name="load_weights",
        cost_estimate=takes(4),
        out_shape=pltpu.VMEM((2,) + own.shape, BF16),
        in_specs=[ANY] * 3,
        out_specs=VMEM,
        scratch_shapes=[pltpu.SemaphoreType.DMA((2,))],
        compiler_params=PARAMS,
    )(own, other, gate)
    return pinned(pair)


def pinned(value):
    return pltpu.with_memory_space_constraint(value, pltpu.VMEM)


def gate_call(weight, *gates):
    out = pl.pallas_call(
        lambda *refs: None,
        name="gate",
        cost_estimate=takes(0),
        out_shape=jax.ShapeDtypeStruct(weight.shape, BF16),
        in_specs=[ANY] * (1 + len(gates)),
        out_specs=ANY,
        input_output_aliases={0: 0},
        compiler_params=PARAMS,
    )(weight, *gates)
    return out


def both_sequences(x, normed, query, out):
    count, length, width = x.shape
    for sequence in range(count):
        rows = pl.ds(sequence * length, length)
        attend_forward(x.at[sequence], query.at[rows], normed.at[rows], out.at[sequence])


def both_normal(x, gain, normed):
    count, length, width = x.shape
    for sequence in range(count):
        normed[sequence * length : (sequence + 1) * length] = normal(x.at[sequence], gain[...])


def first_lower_kernel(flags, x, weight_any, gain, out, weight, normed, query, sems):
    parts = range(x.shape[-1] // HEAD_DIM)
    copies = [
        pltpu.make_async_copy(weight_any.at[:, head(part)], weight.at[:, head(part)], sems.at[part]) for part in parts
    ]
    for copy in copies:
        copy.start()
    active = jnp.logical_and(flags[0] == 0, flags[1] == 0)

    @pl.when(active)
    def _():
        both_normal(x, gain, normed)
        for part in parts:
            copies[part].wait()
            query[:, head(part)] = (dot(normed[...], weight[:, head(part)]) * QUERY_SCALE).astype(BF16)
        both_sequences(x, normed, query, out)

    @pl.when(jnp.logical_not(active))
    def _():
        for copy in copies:
            copy.wait()


def first_upper_kernel(flags, x, weight, gain, later, out, held, normed, query, sem):
    copy = pltpu.make_async_copy(later, held, sem)
    copy.start()

    @pl.when(jnp.logical_and(flags[0] == 1, flags[1] == 0))
    def _():
        both_normal(x, gain, normed)
        query[...] = (dot(normed[...], weight[...]) * QUERY_SCALE).astype(BF16)
        both_sequences(x, normed, query, out)

    copy.wait()


def first_lower_call(flags, x, weight, gain):
    count, length, width = x.shape
    out, held = pl.pallas_call(
        first_lower_kernel,
        name="enc_first_lower",
        cost_estimate=takes(6),
        out_shape=[jax.ShapeDtypeStruct(x.shape, BF16), pltpu.VMEM((width, width), BF16)],
        in_specs=[SMEM, VMEM, ANY, VMEM],
        out_specs=[VMEM] * 2,
        scratch_shapes=[pltpu.VMEM((count * length, width), BF16)] * 2
        + [pltpu.SemaphoreType.DMA((width // HEAD_DIM,))],
        compiler_params=PARAMS,
    )(flags, x, weight, gain)
    return out, pinned(held)


def first_upper_call(flags, x, weight, gain, later):
    count, length, width = x.shape
    return pl.pallas_call(
        first_upper_kernel,
        name="enc_first_upper",
        cost_estimate=takes(4),
        out_shape=[jax.ShapeDtypeStruct(x.shape, BF16), jax.ShapeDtypeStruct(later.shape, BF16)],
        in_specs=[SMEM, VMEM, VMEM, VMEM, ANY],
        out_specs=[VMEM, ANY],
        scratch_shapes=[pltpu.VMEM((count * length, width), BF16)] * 2 + [pltpu.SemaphoreType.DMA],
        compiler_params=PARAMS,
    )(flags, x, weight, gain, later)


def enc_forward_kernel(
    flags, x_any, recv0, recv1, pair, gains, mem_gain, mem, n_own, n_other, saved, sem
):
    core, upper = flags[0], flags[1]
    x0, x1, x2, n0, n1, q0, q1 = [saved.at[place] for place in range(7)]

    @pl.when(upper == 0)
    def _():
        pltpu.make_async_copy(x_any.at[core], x0, sem).start()

    for mine, received in enumerate((recv0, recv1)):

        @pl.when(jnp.logical_and(upper == 1, core == mine))
        def _():
            pltpu.make_async_copy(received, x0, sem).start()

    pltpu.make_async_copy(recv0, x0, sem).wait()
    n0[...] = normal(x0, gains[0:1])
    queries_of(pair.at[core], n0, q0)
    attend_forward(x0, q0, n0, x1)
    n1[...] = normal(x1, gains[1:2])
    queries_of(pair.at[1 - core], n1, q1)
    attend_forward(x1, q1, n1, x2)
    mem[...] = normal(x2, mem_gain[...])
    by_core(core, n0, n1, n_own, n_other)


def enc_forward_call(flags, x, recv0, recv1, pair, gains, mem_gain):
    row = jax.ShapeDtypeStruct(recv0.shape, BF16)
    return pl.pallas_call(
        enc_forward_kernel,
        name="enc_forward",
        cost_estimate=takes(5.3),
        out_shape=[row] * 3 + [jax.ShapeDtypeStruct((7,) + recv0.shape, BF16)],
        in_specs=[SMEM, ANY, ANY, ANY] + [VMEM] * 3,
        out_specs=[VMEM] * 4,
        scratch_shapes=[pltpu.SemaphoreType.DMA],
        compiler_params=PARAMS,
    )(flags, x, recv0, recv1, pair, gains, mem_gain)


def dec_query_kernel(flags, x_any, pair, gains, ahead, sem, y0):
    core, upper = flags[0], flags[1]
    n0, q0 = ahead.at[0], ahead.at[1]

    @pl.when(upper == 0)
    def _():
        rows = pltpu.make_async_copy(x_any.at[core], y0, sem)
        rows.start()
        rows.wait()
        n0[...] = normal(y0, gains[0:1])
        queries_of(pair.at[core], n0, q0)


def dec_query_call(flags, x, pair, gains):
    return pl.pallas_call(
        dec_query_kernel,
        name="dec_query",
        cost_estimate=takes(2.4),
        out_shape=jax.ShapeDtypeStruct((2,) + x.shape[1:], BF16),
        in_specs=[SMEM, ANY, VMEM, VMEM],
        out_specs=VMEM,
        scratch_shapes=[pltpu.SemaphoreType.DMA, pltpu.VMEM(x.shape[1:], BF16)],
        compiler_params=PARAMS,
    )(flags, x, pair, gains)


def dec_forward_kernel(flags, x_any, memory, ahead, pair, gains, y2, saved, sem, y0):
    core, upper = flags[0], flags[1]
    q0 = ahead.at[1]
    y1, n1, q1 = [saved.at[place] for place in range(3)]

    @pl.when(upper == 0)
    def _():
        rows = pltpu.make_async_copy(x_any.at[core], y0, sem)
        rows.start()
        rows.wait()
        attend_forward(y0, q0, memory, y1)
        n1[...] = normal(y1, gains[1:2])
        queries_of(pair.at[1 - core], n1, q1)
        attend_forward(y1, q1, memory, y2)


def dec_forward_call(flags, x, memory, ahead, pair, gains):
    row = jax.ShapeDtypeStruct(x.shape[1:], BF16)
    return pl.pallas_call(
        dec_forward_kernel,
        name="dec_forward",
        cost_estimate=takes(3.3),
        out_shape=[row, jax.ShapeDtypeStruct((3,) + x.shape[1:], BF16)],
        in_specs=[SMEM, ANY] + [VMEM] * 4,
        out_specs=[VMEM] * 2,
        scratch_shapes=[pltpu.SemaphoreType.DMA, pltpu.VMEM(x.shape[1:], BF16)],
        compiler_params=PARAMS,
    )(flags, x, memory, ahead, pair, gains)


def dec_turn_kernel(
    flags, y2, memory, upstream, pair, gains, out, grad_source, pays, n0, n1, y3, u3, q0, q1, dq0, dq1, scaled
):
    core, upper = flags[0], flags[1]

    @pl.when(upper == 1)
    def _():
        length = y2.shape[0]
        n0[...] = normal(y2, gains[0:1])
        queries_of(pair.at[core], n0, q0)
        attend_forward(y2, q0, memory, y3)
        n1[...] = normal(y3, gains[1:2])
        queries_of(pair.at[1 - core], n1, q1)
        attend_backward(memory, q1, upstream, dq1, grad_source, False)
        dec_input_backward(pair.at[1 - core], y3, gains[1:2], dq1, upstream, scaled, u3)
        attend_backward(memory, q0, u3, dq0, grad_source, True)
        dec_input_backward(pair.at[core], y2, gains[0:1], dq0, u3, scaled, out)
        for payload, normed, grad in ((pays.at[0], n0, dq0), (pays.at[1], n1, dq1)):
            payload[0:length] = normed[...]
            payload[length:] = grad[...]


def dec_turn_call(flags, y2, memory, upstream, pair, gains):
    length, width = y2.shape
    row = jax.ShapeDtypeStruct((length, width), BF16)
    payload = jax.ShapeDtypeStruct((2, 2 * length, width), BF16)
    held = pltpu.VMEM((length, width), BF16)
    return pl.pallas_call(
        dec_turn_kernel,
        name="dec_turn",
        cost_estimate=takes(11),
        out_shape=[row, jax.ShapeDtypeStruct(memory.shape, F32), payload],
        in_specs=[SMEM] + [VMEM] * 5,
        out_specs=[VMEM] * 3,
        scratch_shapes=[held] * 8 + [pltpu.VMEM((length, width), F32)],
        compiler_params=PARAMS,
    )(flags, y2, memory, upstream, pair, gains)


def dec_backward_kernel(
    flags, upstream, memory, ahead, saved, pair, gains, done, gate, source_low, out_own, out_other, u1, dq0, dq1, grad_source, scaled, pay0, pay1
):
    core, upper = flags[0], flags[1]
    n0, q0 = ahead.at[0], ahead.at[1]
    y1, n1, q1 = [saved.at[place] for place in range(3)]

    @pl.when(upper == 0)
    def _():
        length = y1.shape[0]
        attend_backward(memory, q1, upstream, dq1, grad_source, False)
        dec_input_backward(pair.at[1 - core], y1, gains[1:2], dq1, upstream, scaled, u1)
        attend_backward(memory, q0, u1, dq0, grad_source, True)
        source_low[...] = grad_source[...].astype(BF16)
        for payload, normed, grad in ((pay0, n0, dq0), (pay1, n1, dq1)):
            payload[0:length] = normed[...]
            payload[length:] = grad[...]
        by_core(core, pay0, pay1, out_own, out_other)

    @pl.when(upper == 1)
    def _():
        by_core(core, done.at[0], done.at[1], out_own, out_other)


def dec_backward_call(flags, upstream, memory, ahead, saved, pair, gains, done, gate):
    length, width = upstream.shape
    payload = jax.ShapeDtypeStruct((2 * length, width), BF16)
    held = pltpu.VMEM((length, width), BF16)
    return pl.pallas_call(
        dec_backward_kernel,
        name="dec_backward",
        cost_estimate=takes(5.5),
        out_shape=[jax.ShapeDtypeStruct(memory.shape, BF16), payload, payload],
        in_specs=[SMEM] + [VMEM] * 7 + [ANY],
        out_specs=[VMEM] * 3,
        scratch_shapes=[held] * 3
        + [pltpu.VMEM(memory.shape, F32), pltpu.VMEM((length, width), F32)]
        + [pltpu.VMEM(payload.shape, BF16)] * 2,
        compiler_params=PARAMS,
    )(flags, upstream, memory, ahead, saved, pair, gains, done, gate)


def put_payload(payload, grad_query, x, grad_source):
    length, width = grad_query.shape
    payload[0:length] = grad_query[...]
    place = lax.broadcasted_iota(jnp.int32, (EXTRA_ROWS, width), 0)
    payload[length:] = jnp.where(place == 0, gain_row(x, grad_source), 0.0).astype(BF16)


def enc_backward_first_kernel(
    flags, source_mine, source_recv, mem_gain, own, other, gains, saved, out, pay0, pay1, weight, weight_sems, u2, u1, grad_query, grad_source, scaled
):
    x0, x1, x2, n0, n1, q0, q1 = [saved.at[place] for place in range(7)]
    core, upper = flags[0], flags[1]

    @pl.when(upper == 1)
    def _():
        start_rows(core, 1, own, other, weight, weight_sems)
        wait = lambda part: row_copy(own, weight, weight_sems, part).wait()
        hidden = x2[...].astype(F32)
        scales = row_scale(hidden)
        grad = mem_gain[...] * (source_mine[...] + source_recv[...].astype(F32))
        mean = jnp.mean(grad * hidden, axis=-1, keepdims=True)
        u2[...] = (scales * grad - hidden * (scales * scales * scales * mean)).astype(BF16)
        attend_backward(n1, q1, u2, grad_query, grad_source, False)
        put_payload(pay1, grad_query, x1, grad_source)
        grad_normed(weight, grad_query, scaled, wait)
        start_rows(core, 0, own, other, weight, weight_sems)
        input_backward(x1, gains[1:2], grad_source, u2, scaled, u1)
        attend_backward(n0, q0, u1, grad_query, grad_source, False)
        put_payload(pay0, grad_query, x0, grad_source)
        grad_normed(weight, grad_query, scaled, wait)
        input_backward(x0, gains[0:1], grad_source, u1, scaled, out)


def enc_backward_first_call(flags, source_mine, source_recv, mem_gain, own, other, gains, saved):
    length, width = saved.shape[1:]
    row = jax.ShapeDtypeStruct((length, width), BF16)
    payload = jax.ShapeDtypeStruct((length + EXTRA_ROWS, width), BF16)
    return pl.pallas_call(
        enc_backward_first_kernel,
        name="enc_backward_first",
        cost_estimate=takes(10),
        out_shape=[row, payload, payload],
        in_specs=[SMEM] + [VMEM] * 3 + [ANY] * 2 + [VMEM] * 2,
        out_specs=[VMEM] * 3,
        scratch_shapes=[pltpu.VMEM((width, width), BF16), pltpu.SemaphoreType.DMA((width // HEAD_DIM,))]
        + [pltpu.VMEM((length, width), BF16)] * 3
        + [pltpu.VMEM((length, width), F32)] * 2,
        compiler_params=PARAMS,
    )(flags, source_mine, source_recv, mem_gain, own, other, gains, saved)


def enc_backward_last_kernel(
    flags, upstream, done0, done1, own, other, gains, saved, gate, out_own, out_other, weight, weight_sems, pay0, pay1, u1, grad_query, grad_source, scaled
):
    x0, x1, _, n0, n1, q0, q1 = [saved.at[place] for place in range(7)]
    core, upper = flags[0], flags[1]

    @pl.when(upper == 0)
    def _():
        start_rows(core, 1, own, other, weight, weight_sems)
        wait = lambda part: row_copy(own, weight, weight_sems, part).wait()
        attend_backward(n1, q1, upstream, grad_query, grad_source, False)
        put_payload(pay1, grad_query, x1, grad_source)
        grad_normed(weight, grad_query, scaled, wait)
        input_backward(x1, gains[1:2], grad_source, upstream, scaled, u1)
        attend_backward(n0, q0, u1, grad_query, grad_source, False)
        put_payload(pay0, grad_query, x0, grad_source)
        by_core(core, pay0, pay1, out_own, out_other)

    @pl.when(upper == 1)
    def _():
        by_core(core, done0, done1, out_own, out_other)


def enc_backward_last_call(flags, upstream, done0, done1, own, other, gains, saved, gate):
    length, width = upstream.shape
    payload = jax.ShapeDtypeStruct((length + EXTRA_ROWS, width), BF16)
    return pl.pallas_call(
        enc_backward_last_kernel,
        name="enc_backward_last",
        cost_estimate=takes(7),
        out_shape=[payload, payload],
        in_specs=[SMEM] + [VMEM] * 3 + [ANY] * 2 + [VMEM] * 2 + [ANY],
        out_specs=[VMEM] * 2,
        scratch_shapes=[pltpu.VMEM((width, width), BF16), pltpu.SemaphoreType.DMA((width // HEAD_DIM,))]
        + [pltpu.VMEM(payload.shape, BF16)] * 2
        + [pltpu.VMEM((length, width), BF16)] * 2
        + [pltpu.VMEM((length, width), F32)] * 2,
        compiler_params=PARAMS,
    )(flags, upstream, done0, done1, own, other, gains, saved, gate)


def features(place, index, block):
    row = lax.broadcasted_iota(jnp.int32, (block, 1), 0)
    half = block // 2
    return jnp.where(row < half, place[index * 2] + row, place[index * 2 + 1] + row - half)


def ones_at(place, index, block, width):
    lanes = lax.broadcasted_iota(jnp.int32, (block, width), 1)
    return jnp.where(lanes == features(place, index, block), 1.0, 0.0).astype(BF16)


def choose_kernel(place, *refs):
    pieces, out, (ones,) = refs[:4], refs[5], refs[6:]
    rows, width = pieces[0].shape
    block = out.shape[0] // 4
    for index in range(4):
        ones[index * block : (index + 1) * block] = ones_at(place, index, block, width)
    for index in range(4):
        out[:, index * rows : (index + 1) * rows] = dot_nt(ones[...], pieces[index][...]).astype(BF16)


def choose_call(place, pieces, gate):
    rows, width = pieces[0].shape
    return pl.pallas_call(
        choose_kernel,
        name="choose_enc",
        cost_estimate=takes(4.3),
        out_shape=jax.ShapeDtypeStruct((width // 4, 4 * rows), BF16),
        in_specs=[SMEM] + [VMEM] * 4 + [ANY],
        out_specs=VMEM,
        scratch_shapes=[pltpu.VMEM((width // 4, width), BF16)],
        compiler_params=PARAMS,
    )(place, *pieces, gate)


def dec_product_kernel(place, *refs):
    pieces, outs, (normed, grads) = refs[:4], refs[4:6], refs[6:]
    length = pieces[0].shape[0] // 4
    for index in range(8):
        start = index % 2 * 2 * length
        normed[index * length : (index + 1) * length] = pieces[index // 2][start : start + length]
        grads[index * length : (index + 1) * length] = pieces[index // 2][start + length : start + 2 * length]
    half = outs[0].shape[0] // 4
    for index in range(4):
        columns = dot_nt(ones_at(place, index, 2 * half, normed.shape[1]), normed[...]).astype(BF16)
        product = dot(columns, grads[...]).astype(BF16)
        for side in range(2):
            outs[side][index * half : (index + 1) * half] = product[side * half : (side + 1) * half]


def dec_product_call(place, pieces):
    rows, width = pieces[0].shape
    return pl.pallas_call(
        dec_product_kernel,
        name="product_dec",
        cost_estimate=takes(4.4),
        out_shape=[jax.ShapeDtypeStruct((width // 8, width), BF16)] * 2,
        in_specs=[SMEM] + [VMEM] * 4,
        out_specs=[VMEM] * 2,
        scratch_shapes=[pltpu.VMEM((2 * rows, width), BF16)] * 2,
        compiler_params=PARAMS,
    )(place, *pieces)


def enc_product_kernel(place, slices, *refs):
    pieces, outs, (held,) = refs[:4], refs[4:8], refs[8:]
    length, width = slices.shape[1] // 8, pieces[0].shape[1]
    block = slices.shape[0] // 4
    extra = jnp.zeros((EXTRA_ROWS, width), F32)
    for index in range(8):
        start = index % 2 * (length + EXTRA_ROWS)
        held[index * length : (index + 1) * length] = pieces[index // 2][start : start + length]
        extra = extra + pieces[index // 2][start + length : start + length + EXTRA_ROWS].astype(F32)
    extra = jnp.sum(extra, axis=0, keepdims=True)
    for index in range(4):
        outs[index][:, 0:width] = dot(slices[index * block : (index + 1) * block], held[...]).astype(BF16)
        lanes = lax.broadcasted_iota(jnp.int32, (block, width), 1)
        column = jnp.sum(jnp.where(lanes == features(place, index, block), extra, 0.0), axis=-1, keepdims=True)
        outs[index][:, width:] = jnp.broadcast_to(column, (block, GAIN_LANES)).astype(BF16)


def enc_product_call(place, slices, pieces):
    width = pieces[0].shape[1]
    return pl.pallas_call(
        enc_product_kernel,
        name="product_enc",
        cost_estimate=takes(3.5),
        out_shape=[jax.ShapeDtypeStruct((slices.shape[0] // 4, width + GAIN_LANES), BF16)] * 4,
        in_specs=[SMEM] + [VMEM] * 5,
        out_specs=[VMEM] * 4,
        scratch_shapes=[pltpu.VMEM((slices.shape[1], width), BF16)],
        compiler_params=PARAMS,
    )(place, slices, *pieces)


def finish_kernel(low, recv, weight, gain, rows, gain_out):
    width = weight.shape[1]
    total = low[...].astype(F32)
    for part in recv:
        total = total + part[...].astype(F32)
    rows[...] = total[:, :width]
    column = jnp.sum(weight[...].astype(F32) * total[:, :width], axis=-1, keepdims=True) / gain[...]
    if low.shape[1] > width:
        column = column + total[:, width : width + 1]
    gain_out[...] = column


def finish_call(low, recv, weight, gain):
    count, width = weight.shape

    def kernel(low, *refs):
        finish_kernel(low, refs[: len(recv)], *refs[len(recv) :])

    return pl.pallas_call(
        kernel,
        name="finish_enc" if low.shape[1] > width else "finish_dec",
        out_shape=[jax.ShapeDtypeStruct((count, width), F32), jax.ShapeDtypeStruct((count, 1), F32)],
        in_specs=[VMEM] * (3 + len(recv)),
        out_specs=[VMEM] * 2,
        compiler_params=PARAMS,
    )(low, *recv, weight, gain)


def device(pipe, high, deep, across):
    return pipe * 32 + (high % 2) * 16 + (deep % 4) * 4 + across % 4


def all_places():
    return [(pipe, high, deep, across) for pipe in range(4) for high in range(2) for deep in range(4) for across in range(4)]


def moved(place, along_x, step):
    pipe, high, deep, across = place
    return device(pipe, high, deep, across + step) if along_x else device(pipe, high, deep + step, across)


def gather_perm(step):
    return [(device(*place), moved(place, place[0] % 2 == 0, step)) for place in all_places()]


def reduce_perm(step):
    return [(device(*place), moved(place, place[0] % 2 == 1, step)) for place in all_places()]


HALF_PERM = [(device(*place), device(place[0], place[1] + 1, place[2], place[3])) for place in all_places()]
SWAP_PERM = [(device(*place), device(place[0] ^ 1, *place[1:])) for place in all_places()]
UP_PERM = [
    (device(pipe, high, deep, across), device(pipe + 2, high + pipe, deep, across))
    for pipe, high, deep, across in all_places()
    if pipe < 2
]
DOWN_PERM = [(target, source) for source, target in UP_PERM]
FIRST_PERM = [(device(*place), device(place[0] + 1, *place[1:])) for place in all_places() if place[0] % 2 == 0]
OUT_PERMS = [
    [(device(1, high, deep, across), device(2 + core, high + core, deep, across)) for _, high, deep, across in all_places()[:32]]
    for core in range(2)
]


def send(value, perm):
    return lax.ppermute(value, ("pipe", "dp"), perm)


def gather(mine, other):
    whole = jnp.concatenate([mine, send(other, SWAP_PERM)], axis=0)
    return [whole] + [send(whole, gather_perm(step)) for step in (1, 2, 3)]


def per_device(enc_in, dec_in, out_grad, enc_weight, dec_weight, enc_gain, dec_gain, mem_gain):
    pipe = lax.axis_index("pipe")
    spot = lax.axis_index("dp")
    core, upper = pipe % 2, pipe // 2
    high, deep, across = spot // 16, (spot // 4) % 4, spot % 4
    even = core == 0
    near, far = jnp.where(even, across, deep), jnp.where(even, deep, across)
    flags = jnp.stack([core, upper]).astype(jnp.int32)
    width = enc_weight.shape[1]
    mem_gain = mem_gain[None]

    def place_of(step, half):
        group, third = jnp.where(even, (far + step) % 4, near), jnp.where(even, near, (far + step) % 4)
        return ((high + half) % 2 * 16 + group * 4 + third) * (width // 32)

    place = jnp.stack([place_of(step, half) for step in range(4) for half in range(2)]).astype(jnp.int32)

    enc_own, dec_own = enc_weight[0], dec_weight[0]
    gains = jnp.concatenate([enc_gain, dec_gain], axis=0)
    gains_other = send(gains, SWAP_PERM)
    pair = jnp.where(even, jnp.stack([gains, gains_other]), jnp.stack([gains_other, gains]))
    enc_gains, dec_gains = pair[:, 0], pair[:, 1]

    x1, held = first_lower_call(flags, enc_in, enc_own, enc_gain)
    x1 = send(x1, FIRST_PERM)
    held = gate_call(held, x1, gains_other)
    enc_other = send(held, SWAP_PERM)
    x2, dec_held = first_upper_call(flags, x1, held, enc_gain, dec_own)
    received = [send(x2[sequence], OUT_PERMS[sequence]) for sequence in range(2)]
    enc_pair = load_call(held, enc_other, x2)
    memory, n_own, n_other, saved = enc_forward_call(flags, enc_in, *received, enc_pair, enc_gains, mem_gain)
    memory_recv = send(memory, DOWN_PERM)
    normed_pieces = gather(n_own, n_other)
    upstream = send(jnp.where(even, out_grad[0], out_grad[1]), UP_PERM)
    dec_other = send(dec_held, SWAP_PERM)
    dec_pair = load_call(dec_own, dec_other, memory)
    ahead = dec_query_call(flags, dec_in, dec_pair, dec_gains)

    y2, dec_saved = dec_forward_call(flags, dec_in, memory_recv, ahead, dec_pair, dec_gains)
    dec_pair = load_call(dec_own, dec_other, dec_saved)
    u2, source_mine, dec_done = dec_turn_call(flags, send(y2, UP_PERM), memory, upstream, dec_pair, dec_gains)
    dec_pair = load_call(dec_own, dec_other, dec_done)
    slices = choose_call(place, normed_pieces, source_mine)
    source_low, dec_own_pay, dec_other_pay = dec_backward_call(
        flags, send(u2, DOWN_PERM), memory_recv, ahead, dec_saved, dec_pair, dec_gains, dec_done, slices
    )
    dec_pieces = gather(dec_own_pay, dec_other_pay)

    u_low, done0, done1 = enc_backward_first_call(
        flags, source_mine, send(source_low, UP_PERM), mem_gain, enc_own, enc_other, enc_gains, saved
    )
    dec_blocks = dec_product_call(place, dec_pieces)
    own_pay, other_pay = enc_backward_last_call(
        flags, send(u_low, DOWN_PERM), done0, done1, enc_own, enc_other, enc_gains, saved, dec_blocks[0]
    )

    count = width // 32

    def rows_of(weight, gain):
        start = spot * count
        return (
            lax.dynamic_slice_in_dim(weight, start, count, 0),
            lax.dynamic_slice_in_dim(gain[0], start, count, 0)[:, None],
        )

    dec_sum = (dec_blocks[0].astype(F32) + send(dec_blocks[1], HALF_PERM).astype(F32)).astype(BF16)
    dec_parts = [dec_sum[step * count : (step + 1) * count] for step in range(4)]
    dec_recv = [send(dec_parts[step], reduce_perm(step)) for step in (1, 2, 3)]

    enc_blocks = enc_product_call(place, slices, gather(own_pay, other_pay))
    enc_sum = enc_blocks[0].astype(F32)
    for step in (1, 2, 3):
        enc_sum = enc_sum + send(enc_blocks[step], reduce_perm(step)).astype(F32)
    enc_recv = send(enc_sum[count:].astype(BF16), HALF_PERM)

    dec_rows, dec_column = finish_call(dec_parts[0], dec_recv, *rows_of(dec_own, dec_gain))
    enc_rows, enc_column = finish_call(enc_sum[:count], [enc_recv], *rows_of(enc_own, enc_gain))
    return enc_rows[None], dec_rows[None], enc_column[None, :, 0], dec_column[None, :, 0]


def solution(mesh):
    placed = (
        P("dp", None, None),
        P("dp", None, None),
        P("dp", None, None),
        P("pipe", None, None),
        P("pipe", None, None),
        P("pipe", None),
        P("pipe", None),
        P(),
    )
    return jax.shard_map(
        per_device,
        mesh=mesh,
        in_specs=placed,
        out_specs=(P("pipe", "dp", None), P("pipe", "dp", None), P("pipe", "dp"), P("pipe", "dp")),
        check_vma=False,
    )
```

```python
import functools

import jax
import jax.numpy as jnp
from jax import lax
from jax.experimental import pallas as pl
from jax.experimental.pallas import tpu as pltpu
from jax.sharding import PartitionSpec as P

HEAD_DIM = 256
EPSILON = 1e-06
QUERY_SCALE = 0.0625
EXTRA_ROWS = 16
GAIN_LANES = 128

BF16 = jnp.bfloat16
F32 = jnp.float32
def takes(microseconds):
    return pl.CostEstimate(flops=int(microseconds * 10**9), bytes_accessed=0, transcendentals=0)


ANY = pl.BlockSpec(memory_space=pl.ANY)
SMEM = pl.BlockSpec(memory_space=pltpu.SMEM)
VMEM = pl.BlockSpec(memory_space=pltpu.VMEM)
HBM = pl.BlockSpec(memory_space=pltpu.HBM)
PARAMS = pltpu.CompilerParams(vmem_limit_bytes=14 * 2**20)


def dot(left, right):
    return jnp.dot(left, right, preferred_element_type=F32)


def dot_nt(left, right):
    return lax.dot_general(left, right, (((1,), (1,)), ((), ())), preferred_element_type=F32)


def dot_tn(left, right):
    return lax.dot_general(left, right, (((0,), (0,)), ((), ())), preferred_element_type=F32)


def row_scale(values):
    return lax.rsqrt(jnp.mean(values * values, axis=-1, keepdims=True) + EPSILON)


def head(index):
    return slice(index * HEAD_DIM, (index + 1) * HEAD_DIM)


def normal(x, gain):
    hidden = x[...].astype(F32)
    return (hidden * row_scale(hidden) * gain).astype(BF16)


def attend_forward(x, query, source, out):
    heads = [head(part) for part in range(x.shape[-1] // HEAD_DIM)]
    raised = [jnp.exp(dot_nt(query[:, cols], source[:, cols])) for cols in heads]
    low = [(value / jnp.sum(value, axis=-1, keepdims=True)).astype(BF16) for value in raised]
    for cols, shares in zip(heads, low):
        out[:, cols] = (x[:, cols].astype(F32) + dot(shares, source[:, cols])).astype(BF16)


def queries_of(weight, normed, query):
    query[...] = (dot(normed[...], weight[...]) * QUERY_SCALE).astype(BF16)


def attend_backward(source, query, upstream, grad_query, grad_source, add):
    heads = [head(part) for part in range(source.shape[-1] // HEAD_DIM)]
    length = query.shape[0]
    if length % 128 == 0:
        sides = [jnp.concatenate([query[:, cols], upstream[:, cols]], axis=0) for cols in heads]
        both = [dot_nt(source[:, cols], side) for cols, side in zip(heads, sides)]
        raised = [jnp.exp(value[:, :length]) for value in both]
        grads = [value[:, length:] for value in both]
    else:
        raised = [jnp.exp(dot_nt(source[:, cols], query[:, cols])) for cols in heads]
        grads = [dot_nt(source[:, cols], upstream[:, cols]) for cols in heads]
    probs = [value / jnp.sum(value, axis=0, keepdims=True) for value in raised]
    scores = [
        (share * (grad - jnp.sum(grad * share, axis=0, keepdims=True))).astype(BF16) for share, grad in zip(probs, grads)
    ]
    for part, cols in enumerate(heads):
        low = probs[part].astype(BF16)
        grad_query[:, cols] = (dot_tn(scores[part], source[:, cols]) * QUERY_SCALE).astype(BF16)
        if length % 128 == 0:
            total = dot(jnp.concatenate([scores[part], low], axis=1), sides[part])
        else:
            total = dot(scores[part], query[:, cols]) + dot(low, upstream[:, cols])
        grad_source[:, cols] = grad_source[:, cols] + total if add else total


def grad_normed(weight, grad_query, scaled):
    length, width = grad_query.shape
    for part in range(width // HEAD_DIM):
        cols = head(part)
        if length % 128 == 0:
            scaled[:, cols] = dot_nt(weight[cols, :], grad_query[...]).T
        else:
            scaled[:, cols] = dot_nt(grad_query[...], weight[cols, :])


def input_backward(x, gain, grad_source, upstream, scaled, out):
    hidden = x[...].astype(F32)
    scales = row_scale(hidden)
    grad = scaled[...] if grad_source is None else scaled[...] + grad_source[...]
    grad = gain * grad
    mean = jnp.mean(grad * hidden, axis=-1, keepdims=True)
    factor = scales * scales * scales * mean
    out[...] = (upstream[...].astype(F32) + scales * grad - hidden * factor).astype(BF16)


def dec_input_backward(weight, x, gain, grad_query, upstream, scaled, out):
    grad_normed(weight, grad_query, scaled)
    input_backward(x, gain, None, upstream, scaled, out)


def gain_row(x, grad_source):
    hidden = x[...].astype(F32)
    return jnp.sum(grad_source[...] * hidden * row_scale(hidden), axis=0, keepdims=True)


def by_core(core, low, high, own, other):
    for mine in (0, 1):

        @pl.when(core == mine)
        def _():
            own[...] = high[...] if mine else low[...]
            other[...] = low[...] if mine else high[...]


def load_kernel(own, other, gate, pair, sems):
    copies = [pltpu.make_async_copy(part, pair.at[slot], sems.at[slot]) for slot, part in enumerate((own, other))]
    for copy in copies:
        copy.start()
    for copy in copies:
        copy.wait()


def load_call(own, other, gate):
    pair = pl.pallas_call(
        load_kernel,
        name="load_weights",
        cost_estimate=takes(4),
        out_shape=pltpu.VMEM((2,) + own.shape, BF16),
        in_specs=[ANY] * 3,
        out_specs=VMEM,
        scratch_shapes=[pltpu.SemaphoreType.DMA((2,))],
        compiler_params=PARAMS,
    )(streamed(own), streamed(other), gate)
    return pinned(pair)


def streamed(value):
    return pltpu.with_memory_space_constraint(value, pltpu.HBM)


def pinned(value):
    return pltpu.with_memory_space_constraint(value, pltpu.VMEM)


def both_sequences(x, normed, query, out):
    count, length, width = x.shape
    for sequence in range(count):
        rows = pl.ds(sequence * length, length)
        attend_forward(x.at[sequence], query.at[rows], normed.at[rows], out.at[sequence])


def both_normal(x, gain, normed):
    count, length, width = x.shape
    for sequence in range(count):
        normed[sequence * length : (sequence + 1) * length] = normal(x.at[sequence], gain[...])


def first_lower_kernel(flags, x_any, weight_any, gain, out, weight, x, normed, query, x_sem, sems):
    parts = range(x.shape[-1] // HEAD_DIM)
    rows = pltpu.make_async_copy(x_any, x, x_sem)
    rows.start()
    copies = [
        pltpu.make_async_copy(weight_any.at[:, head(part)], weight.at[:, head(part)], sems.at[part]) for part in parts
    ]
    for copy in copies:
        copy.start()
    rows.wait()
    active = jnp.logical_and(flags[0] == 0, flags[1] == 0)

    @pl.when(active)
    def _():
        both_normal(x, gain, normed)
        middle = len(parts) // 2
        for half in (parts[:middle], parts[middle:]):
            for part in half:
                copies[part].wait()
            for part in half:
                query[:, head(part)] = (dot(normed[...], weight[:, head(part)]) * QUERY_SCALE).astype(BF16)
        both_sequences(x, normed, query, out)

    @pl.when(jnp.logical_not(active))
    def _():
        for copy in copies:
            copy.wait()


def first_lower_call(flags, x, weight, gain):
    count, length, width = x.shape
    out, held = pl.pallas_call(
        first_lower_kernel,
        name="enc_first_lower",
        cost_estimate=takes(6),
        out_shape=[jax.ShapeDtypeStruct(x.shape, BF16), pltpu.VMEM((width, width), BF16)],
        in_specs=[SMEM, ANY, ANY, VMEM],
        out_specs=[VMEM] * 2,
        scratch_shapes=[pltpu.VMEM(x.shape, BF16)]
        + [pltpu.VMEM((count * length, width), BF16)] * 2
        + [pltpu.SemaphoreType.DMA, pltpu.SemaphoreType.DMA((width // HEAD_DIM,))],
        compiler_params=PARAMS,
    )(flags, streamed(x), streamed(weight), gain)
    return out, pinned(held)


def first_upper_kernel(flags, x, weight, gain, gate, out, normed, query):
    @pl.when(jnp.logical_and(flags[0] == 1, flags[1] == 0))
    def _():
        both_normal(x, gain, normed)
        query[...] = (dot(normed[...], weight[...]) * QUERY_SCALE).astype(BF16)
        both_sequences(x, normed, query, out)


def first_upper_call(flags, x, weight, gain, gate):
    count, length, width = x.shape
    return pl.pallas_call(
        first_upper_kernel,
        name="enc_first_upper",
        cost_estimate=takes(4),
        out_shape=jax.ShapeDtypeStruct(x.shape, BF16),
        in_specs=[SMEM, VMEM, VMEM, VMEM, ANY],
        out_specs=VMEM,
        scratch_shapes=[pltpu.VMEM((count * length, width), BF16)] * 2,
        compiler_params=PARAMS,
    )(flags, x, weight, gain, gate)


def enc_forward_kernel(
    flags, x_any, recv0, recv1, pair, gains, mem_gain, mem, n_own, n_other, saved, sem
):
    core, upper = flags[0], flags[1]
    x0, x1, x2, n0, n1, q0, q1 = [saved.at[place] for place in range(7)]

    @pl.when(upper == 0)
    def _():
        pltpu.make_async_copy(x_any.at[core], x0, sem).start()

    for mine, received in enumerate((recv0, recv1)):

        @pl.when(jnp.logical_and(upper == 1, core == mine))
        def _():
            pltpu.make_async_copy(received, x0, sem).start()

    pltpu.make_async_copy(recv0, x0, sem).wait()
    n0[...] = normal(x0, gains[0:1])
    queries_of(pair.at[core], n0, q0)
    attend_forward(x0, q0, n0, x1)
    n1[...] = normal(x1, gains[1:2])
    queries_of(pair.at[1 - core], n1, q1)
    attend_forward(x1, q1, n1, x2)
    mem[...] = normal(x2, mem_gain[...])
    by_core(core, n0, n1, n_own, n_other)


def enc_forward_call(flags, x, recv0, recv1, pair, gains, mem_gain):
    row = jax.ShapeDtypeStruct(recv0.shape, BF16)
    return pl.pallas_call(
        enc_forward_kernel,
        name="enc_forward",
        cost_estimate=takes(5.3),
        out_shape=[row] * 3 + [jax.ShapeDtypeStruct((7,) + recv0.shape, BF16)],
        in_specs=[SMEM, ANY, ANY, ANY] + [VMEM] * 3,
        out_specs=[VMEM] * 4,
        scratch_shapes=[pltpu.SemaphoreType.DMA],
        compiler_params=PARAMS,
    )(flags, streamed(x), recv0, recv1, pair, gains, mem_gain)


def dec_query_kernel(flags, x_any, pair, gains, ahead, sem, y0):
    core, upper = flags[0], flags[1]
    n0, q0 = ahead.at[0], ahead.at[1]

    @pl.when(upper == 0)
    def _():
        rows = pltpu.make_async_copy(x_any.at[core], y0, sem)
        rows.start()
        rows.wait()
        n0[...] = normal(y0, gains[0:1])
        queries_of(pair.at[core], n0, q0)


def dec_query_call(flags, x, pair, gains):
    return pl.pallas_call(
        dec_query_kernel,
        name="dec_query",
        cost_estimate=takes(2.4),
        out_shape=jax.ShapeDtypeStruct((2,) + x.shape[1:], BF16),
        in_specs=[SMEM, ANY, VMEM, VMEM],
        out_specs=VMEM,
        scratch_shapes=[pltpu.SemaphoreType.DMA, pltpu.VMEM(x.shape[1:], BF16)],
        compiler_params=PARAMS,
    )(flags, x, pair, gains)


def dec_forward_kernel(flags, x_any, memory, ahead, pair, gains, y2, saved, sem, y0):
    core, upper = flags[0], flags[1]
    q0 = ahead.at[1]
    y1, n1, q1 = [saved.at[place] for place in range(3)]

    @pl.when(upper == 0)
    def _():
        rows = pltpu.make_async_copy(x_any.at[core], y0, sem)
        rows.start()
        rows.wait()
        attend_forward(y0, q0, memory, y1)
        n1[...] = normal(y1, gains[1:2])
        queries_of(pair.at[1 - core], n1, q1)
        attend_forward(y1, q1, memory, y2)


def dec_forward_call(flags, x, memory, ahead, pair, gains):
    row = jax.ShapeDtypeStruct(x.shape[1:], BF16)
    return pl.pallas_call(
        dec_forward_kernel,
        name="dec_forward",
        cost_estimate=takes(3.3),
        out_shape=[row, jax.ShapeDtypeStruct((3,) + x.shape[1:], BF16)],
        in_specs=[SMEM, ANY] + [VMEM] * 4,
        out_specs=[VMEM] * 2,
        scratch_shapes=[pltpu.SemaphoreType.DMA, pltpu.VMEM(x.shape[1:], BF16)],
        compiler_params=PARAMS,
    )(flags, x, memory, ahead, pair, gains)


def dec_turn_kernel(
    flags, y2, memory, upstream, pair, gains, out, grad_source, pays, n0, n1, y3, u3, q0, q1, dq0, dq1, scaled
):
    core, upper = flags[0], flags[1]

    @pl.when(upper == 1)
    def _():
        length = y2.shape[0]
        n0[...] = normal(y2, gains[0:1])
        queries_of(pair.at[core], n0, q0)
        attend_forward(y2, q0, memory, y3)
        n1[...] = normal(y3, gains[1:2])
        queries_of(pair.at[1 - core], n1, q1)
        attend_backward(memory, q1, upstream, dq1, grad_source, False)
        dec_input_backward(pair.at[1 - core], y3, gains[1:2], dq1, upstream, scaled, u3)
        attend_backward(memory, q0, u3, dq0, grad_source, True)
        dec_input_backward(pair.at[core], y2, gains[0:1], dq0, u3, scaled, out)
        for payload, normed, grad in ((pays.at[0], n0, dq0), (pays.at[1], n1, dq1)):
            payload[0:length] = normed[...]
            payload[length:] = grad[...]


def dec_turn_call(flags, y2, memory, upstream, pair, gains):
    length, width = y2.shape
    row = jax.ShapeDtypeStruct((length, width), BF16)
    payload = jax.ShapeDtypeStruct((2, 2 * length, width), BF16)
    held = pltpu.VMEM((length, width), BF16)
    return pl.pallas_call(
        dec_turn_kernel,
        name="dec_turn",
        cost_estimate=takes(11),
        out_shape=[row, jax.ShapeDtypeStruct(memory.shape, F32), payload],
        in_specs=[SMEM] + [VMEM] * 5,
        out_specs=[VMEM] * 3,
        scratch_shapes=[held] * 8 + [pltpu.VMEM((length, width), F32)],
        compiler_params=PARAMS,
    )(flags, y2, memory, upstream, pair, gains)


def dec_backward_kernel(
    flags, upstream, memory, ahead, saved, pair, gains, done, source_low, out_own, out_other, u1, dq0, dq1, grad_source, scaled, pay0, pay1
):
    core, upper = flags[0], flags[1]
    n0, q0 = ahead.at[0], ahead.at[1]
    y1, n1, q1 = [saved.at[place] for place in range(3)]

    @pl.when(upper == 0)
    def _():
        length = y1.shape[0]
        attend_backward(memory, q1, upstream, dq1, grad_source, False)
        dec_input_backward(pair.at[1 - core], y1, gains[1:2], dq1, upstream, scaled, u1)
        attend_backward(memory, q0, u1, dq0, grad_source, True)
        source_low[...] = grad_source[...].astype(BF16)
        for payload, normed, grad in ((pay0, n0, dq0), (pay1, n1, dq1)):
            payload[0:length] = normed[...]
            payload[length:] = grad[...]
        by_core(core, pay0, pay1, out_own, out_other)

    @pl.when(upper == 1)
    def _():
        by_core(core, done.at[0], done.at[1], out_own, out_other)


def dec_backward_call(flags, upstream, memory, ahead, saved, pair, gains, done):
    length, width = upstream.shape
    payload = jax.ShapeDtypeStruct((2 * length, width), BF16)
    held = pltpu.VMEM((length, width), BF16)
    return pl.pallas_call(
        dec_backward_kernel,
        name="dec_backward",
        cost_estimate=takes(5.5),
        out_shape=[jax.ShapeDtypeStruct(memory.shape, BF16), payload, payload],
        in_specs=[SMEM] + [VMEM] * 7,
        out_specs=[VMEM] * 3,
        scratch_shapes=[held] * 3
        + [pltpu.VMEM(memory.shape, F32), pltpu.VMEM((length, width), F32)]
        + [pltpu.VMEM(payload.shape, BF16)] * 2,
        compiler_params=PARAMS,
    )(flags, upstream, memory, ahead, saved, pair, gains, done)


def put_payload(core, payload, grad_query, x, grad_source):
    length, width = grad_query.shape
    payload[0:length] = grad_query[...]
    place = lax.broadcasted_iota(jnp.int32, (EXTRA_ROWS, width), 0)
    payload[length:] = jnp.where(place == core, gain_row(x, grad_source), 0.0).astype(BF16)


def enc_backward_first_kernel(
    flags, source_mine, source_recv, mem_gain, pair, gains, saved, out, pay0, pay1, u2, u1, grad_query, grad_source, scaled
):
    x0, x1, x2, n0, n1, q0, q1 = [saved.at[place] for place in range(7)]
    core, upper = flags[0], flags[1]

    @pl.when(upper == 1)
    def _():
        hidden = x2[...].astype(F32)
        scales = row_scale(hidden)
        grad = mem_gain[...] * (source_mine[...] + source_recv[...].astype(F32))
        mean = jnp.mean(grad * hidden, axis=-1, keepdims=True)
        u2[...] = (scales * grad - hidden * (scales * scales * scales * mean)).astype(BF16)
        attend_backward(n1, q1, u2, grad_query, grad_source, False)
        put_payload(core, pay1, grad_query, x1, grad_source)
        grad_normed(pair.at[1 - core], grad_query, scaled)
        input_backward(x1, gains[1:2], grad_source, u2, scaled, u1)
        attend_backward(n0, q0, u1, grad_query, grad_source, False)
        put_payload(core, pay0, grad_query, x0, grad_source)
        grad_normed(pair.at[core], grad_query, scaled)
        input_backward(x0, gains[0:1], grad_source, u1, scaled, out)


def enc_backward_first_call(flags, source_mine, source_recv, mem_gain, pair, gains, saved):
    length, width = saved.shape[1:]
    row = jax.ShapeDtypeStruct((length, width), BF16)
    payload = jax.ShapeDtypeStruct((length + EXTRA_ROWS, width), BF16)
    return pl.pallas_call(
        enc_backward_first_kernel,
        name="enc_backward_first",
        cost_estimate=takes(10),
        out_shape=[row, payload, payload],
        in_specs=[SMEM] + [VMEM] * 3 + [VMEM] * 3,
        out_specs=[VMEM] * 3,
        scratch_shapes=[pltpu.VMEM((length, width), BF16)] * 3
        + [pltpu.VMEM((length, width), F32)] * 2,
        compiler_params=PARAMS,
    )(flags, source_mine, source_recv, mem_gain, pair, gains, saved)


def enc_backward_last_kernel(
    flags, upstream, done0, done1, pair, gains, saved, gate, later_gate, out_own, out_other, pay0, pay1, u1, grad_query, grad_source, scaled
):
    x0, x1, _, n0, n1, q0, q1 = [saved.at[place] for place in range(7)]
    core, upper = flags[0], flags[1]

    @pl.when(upper == 0)
    def _():
        attend_backward(n1, q1, upstream, grad_query, grad_source, False)
        put_payload(core, pay1, grad_query, x1, grad_source)
        grad_normed(pair.at[1 - core], grad_query, scaled)
        input_backward(x1, gains[1:2], grad_source, upstream, scaled, u1)
        attend_backward(n0, q0, u1, grad_query, grad_source, False)
        put_payload(core, pay0, grad_query, x0, grad_source)
        by_core(core, pay0, pay1, out_own, out_other)

    @pl.when(upper == 1)
    def _():
        by_core(core, done0, done1, out_own, out_other)


def enc_backward_last_call(flags, upstream, done0, done1, pair, gains, saved, *gates):
    length, width = upstream.shape
    payload = jax.ShapeDtypeStruct((length + EXTRA_ROWS, width), BF16)
    return pl.pallas_call(
        enc_backward_last_kernel,
        name="enc_backward_last",
        cost_estimate=takes(7),
        out_shape=[payload, payload],
        in_specs=[SMEM] + [VMEM] * 3 + [VMEM] * 3 + [ANY] * 2,
        out_specs=[VMEM] * 2,
        scratch_shapes=[pltpu.VMEM(payload.shape, BF16)] * 2
        + [pltpu.VMEM((length, width), BF16)] * 2
        + [pltpu.VMEM((length, width), F32)] * 2,
        compiler_params=PARAMS,
    )(flags, upstream, done0, done1, pair, gains, saved, *gates)


def features(place, index, block):
    row = lax.broadcasted_iota(jnp.int32, (block, 1), 0)
    half = block // 2
    return jnp.where(row < half, place[index * 2] + row, place[index * 2 + 1] + row - half)


def ones_at(place, index, block, width):
    lanes = lax.broadcasted_iota(jnp.int32, (block, width), 1)
    return jnp.where(lanes == features(place, index, block), 1.0, 0.0).astype(BF16)


def choose_kernel(place, *refs):
    pieces, out, (ones,) = refs[:4], refs[5], refs[6:]
    rows, width = pieces[0].shape
    block = out.shape[0] // 4
    for index in range(4):
        ones[index * block : (index + 1) * block] = ones_at(place, index, block, width)
    for index in range(4):
        out[:, index * rows : (index + 1) * rows] = dot_nt(ones[...], pieces[index][...]).astype(BF16)


def choose_call(place, pieces, gate):
    rows, width = pieces[0].shape
    return pl.pallas_call(
        choose_kernel,
        name="choose_enc",
        cost_estimate=takes(4.3),
        out_shape=jax.ShapeDtypeStruct((width // 4, 4 * rows), BF16),
        in_specs=[SMEM] + [VMEM] * 4 + [ANY],
        out_specs=VMEM,
        scratch_shapes=[pltpu.VMEM((width // 4, width), BF16)],
        compiler_params=PARAMS,
    )(place, *pieces, gate)


def dec_product_kernel(place, *refs):
    pieces, outs, (normed, grads) = refs[:4], refs[4:6], refs[6:]
    length = pieces[0].shape[0] // 4
    for index in range(8):
        start = index % 2 * 2 * length
        normed[index * length : (index + 1) * length] = pieces[index // 2][start : start + length]
        grads[index * length : (index + 1) * length] = pieces[index // 2][start + length : start + 2 * length]
    half = outs[0].shape[0] // 4
    for index in range(4):
        columns = dot_nt(ones_at(place, index, 2 * half, normed.shape[1]), normed[...]).astype(BF16)
        product = dot(columns, grads[...]).astype(BF16)
        for side in range(2):
            outs[side][index * half : (index + 1) * half] = product[side * half : (side + 1) * half]


def dec_product_call(place, pieces):
    rows, width = pieces[0].shape
    return pl.pallas_call(
        dec_product_kernel,
        name="product_dec",
        cost_estimate=takes(4.4),
        out_shape=[jax.ShapeDtypeStruct((width // 8, width), BF16)] * 2,
        in_specs=[SMEM] + [VMEM] * 4,
        out_specs=[VMEM] * 2,
        scratch_shapes=[pltpu.VMEM((2 * rows, width), BF16)] * 2,
        compiler_params=PARAMS,
    )(place, *pieces)


def enc_product_kernel(place, slices, *refs):
    pieces, outs, (held,) = refs[:4], refs[4:8], refs[8:]
    length, width = slices.shape[1] // 8, pieces[0].shape[1]
    block = slices.shape[0] // 4
    extra = jnp.zeros((EXTRA_ROWS, width), F32)
    for index in range(4):
        held[2 * index * length : 2 * (index + 1) * length] = pieces[index][0 : 2 * length]
        extra = extra + pieces[index][2 * length :].astype(F32)
    extra = jnp.sum(extra, axis=0, keepdims=True)
    for index in range(4):
        outs[index][:, 0:width] = dot(slices[index * block : (index + 1) * block], held[...]).astype(BF16)
        lanes = lax.broadcasted_iota(jnp.int32, (block, width), 1)
        column = jnp.sum(jnp.where(lanes == features(place, index, block), extra, 0.0), axis=-1, keepdims=True)
        outs[index][:, width:] = jnp.broadcast_to(column, (block, GAIN_LANES)).astype(BF16)


def enc_product_call(place, slices, pieces):
    width = pieces[0].shape[1]
    return pl.pallas_call(
        enc_product_kernel,
        name="product_enc",
        cost_estimate=takes(3.5),
        out_shape=[jax.ShapeDtypeStruct((slices.shape[0] // 4, width + GAIN_LANES), BF16)] * 4,
        in_specs=[SMEM] + [VMEM] * 5,
        out_specs=[VMEM] * 4,
        scratch_shapes=[pltpu.VMEM((slices.shape[1], width), BF16)],
        compiler_params=PARAMS,
    )(place, slices, *pieces)


def finish_kernel(low, recv, weight, gain, rows, gain_out):
    width = weight.shape[1]
    total = low[...].astype(F32)
    for part in recv:
        total = total + part[...].astype(F32)
    rows[...] = total[:, :width]
    column = jnp.sum(weight[...].astype(F32) * total[:, :width], axis=-1, keepdims=True) / gain[...]
    if low.shape[1] > width:
        column = column + total[:, width : width + 1]
    gain_out[...] = column


def finish_call(low, recv, weight, gain):
    count, width = weight.shape

    def kernel(low, *refs):
        finish_kernel(low, refs[: len(recv)], *refs[len(recv) :])

    return pl.pallas_call(
        kernel,
        name="finish_enc" if low.shape[1] > width else "finish_dec",
        out_shape=[jax.ShapeDtypeStruct((count, width), F32), jax.ShapeDtypeStruct((count, 1), F32)],
        in_specs=[VMEM] * (3 + len(recv)),
        out_specs=[VMEM] * 2,
        compiler_params=PARAMS,
    )(low, *recv, weight, gain)


def device(pipe, high, deep, across):
    return pipe * 32 + (high % 2) * 16 + (deep % 4) * 4 + across % 4


def all_places():
    return [(pipe, high, deep, across) for pipe in range(4) for high in range(2) for deep in range(4) for across in range(4)]


def moved(place, along_x, step):
    pipe, high, deep, across = place
    return device(pipe, high, deep, across + step) if along_x else device(pipe, high, deep + step, across)


def gather_perm(step):
    return [(device(*place), moved(place, place[0] % 2 == 0, step)) for place in all_places()]


def reduce_perm(step):
    return [(device(*place), moved(place, place[0] % 2 == 1, step)) for place in all_places()]


HALF_PERM = [(device(*place), device(place[0], place[1] + 1, place[2], place[3])) for place in all_places()]
SWAP_PERM = [(device(*place), device(place[0] ^ 1, *place[1:])) for place in all_places()]
UP_PERM = [
    (device(pipe, high, deep, across), device(pipe + 2, high + pipe, deep, across))
    for pipe, high, deep, across in all_places()
    if pipe < 2
]
DOWN_PERM = [(target, source) for source, target in UP_PERM]
FIRST_PERM = [(device(*place), device(place[0] + 1, *place[1:])) for place in all_places() if place[0] % 2 == 0]
OUT_PERMS = [
    [(device(1, high, deep, across), device(2 + core, high + core, deep, across)) for _, high, deep, across in all_places()[:32]]
    for core in range(2)
]


def send(value, perm):
    return lax.ppermute(value, ("pipe", "dp"), perm)


def gather(mine, other, extra=0):
    other = send(other, SWAP_PERM)
    if extra:
        rows = mine.shape[0] - extra
        whole = jnp.concatenate([mine[:rows], other[:rows], mine[rows:] + other[rows:]], axis=0)
    else:
        whole = jnp.concatenate([mine, other], axis=0)
    return [whole] + [send(whole, gather_perm(step)) for step in (1, 2, 3)]


def per_device(enc_in, dec_in, out_grad, enc_weight, dec_weight, enc_gain, dec_gain, mem_gain):
    pipe = lax.axis_index("pipe")
    spot = lax.axis_index("dp")
    core, upper = pipe % 2, pipe // 2
    high, deep, across = spot // 16, (spot // 4) % 4, spot % 4
    even = core == 0
    near, far = jnp.where(even, across, deep), jnp.where(even, deep, across)
    flags = jnp.stack([core, upper]).astype(jnp.int32)
    width = enc_weight.shape[1]
    mem_gain = mem_gain[None]

    def place_of(step, half):
        group, third = jnp.where(even, (far + step) % 4, near), jnp.where(even, near, (far + step) % 4)
        return ((high + half) % 2 * 16 + group * 4 + third) * (width // 32)

    place = jnp.stack([place_of(step, half) for step in range(4) for half in range(2)]).astype(jnp.int32)

    enc_own, dec_own = enc_weight[0], dec_weight[0]
    gains = jnp.concatenate([enc_gain, dec_gain], axis=0)
    gains_other = send(gains, SWAP_PERM)
    pair = jnp.where(even, jnp.stack([gains, gains_other]), jnp.stack([gains_other, gains]))
    enc_gains, dec_gains = pair[:, 0], pair[:, 1]

    enc_other = send(enc_own, SWAP_PERM)
    x1, held = first_lower_call(flags, enc_in, enc_own, enc_gain)
    x1 = send(x1, FIRST_PERM)
    x2 = first_upper_call(flags, x1, held, enc_gain, gains_other)
    received = [send(x2[sequence], OUT_PERMS[sequence]) for sequence in range(2)]
    enc_pair = load_call(enc_own, enc_other, x2)
    memory, n_own, n_other, saved = enc_forward_call(flags, enc_in, *received, enc_pair, enc_gains, mem_gain)
    memory_recv = send(memory, DOWN_PERM)
    normed_pieces = gather(n_own, n_other)
    upstream = send(jnp.where(even, out_grad[0], out_grad[1]), UP_PERM)
    dec_other = send(dec_own, SWAP_PERM)
    dec_pair = load_call(dec_own, dec_other, memory)
    ahead = dec_query_call(flags, dec_in, dec_pair, dec_gains)

    y2, dec_saved = dec_forward_call(flags, dec_in, memory_recv, ahead, dec_pair, dec_gains)
    dec_pair = load_call(dec_own, dec_other, dec_saved)
    u2, source_mine, dec_done = dec_turn_call(flags, send(y2, UP_PERM), memory, upstream, dec_pair, dec_gains)
    dec_pair = load_call(dec_own, dec_other, dec_done)
    source_low, dec_own_pay, dec_other_pay = dec_backward_call(
        flags, send(u2, DOWN_PERM), memory_recv, ahead, dec_saved, dec_pair, dec_gains, dec_done
    )
    dec_pieces = gather(dec_own_pay, dec_other_pay)
    enc_pair = load_call(enc_own, enc_other, source_low)

    u_low, done0, done1 = enc_backward_first_call(
        flags, source_mine, send(source_low, UP_PERM), mem_gain, enc_pair, enc_gains, saved
    )
    dec_blocks = dec_product_call(place, dec_pieces)
    slices = choose_call(place, normed_pieces, u_low)
    own_pay, other_pay = enc_backward_last_call(
        flags, send(u_low, DOWN_PERM), done0, done1, enc_pair, enc_gains, saved, dec_blocks[0], slices
    )

    count = width // 32

    def rows_of(weight, gain):
        start = spot * count
        return (
            lax.dynamic_slice_in_dim(weight, start, count, 0),
            lax.dynamic_slice_in_dim(gain[0], start, count, 0)[:, None],
        )

    dec_sum = (dec_blocks[0].astype(F32) + send(dec_blocks[1], HALF_PERM).astype(F32)).astype(BF16)
    dec_parts = [dec_sum[step * count : (step + 1) * count] for step in range(4)]
    dec_recv = [send(dec_parts[step], reduce_perm(step)) for step in (1, 2, 3)]

    enc_blocks = enc_product_call(place, slices, gather(own_pay, other_pay, EXTRA_ROWS))
    enc_sum = enc_blocks[0].astype(F32)
    for step in (1, 2, 3):
        enc_sum = enc_sum + send(enc_blocks[step], reduce_perm(step)).astype(F32)
    enc_recv = send(enc_sum[count:].astype(BF16), HALF_PERM)

    dec_rows, dec_column = finish_call(dec_parts[0], dec_recv, *rows_of(dec_own, dec_gain))
    enc_rows, enc_column = finish_call(enc_sum[:count], [enc_recv], *rows_of(enc_own, enc_gain))
    return enc_rows[None], dec_rows[None], enc_column[None, :, 0], dec_column[None, :, 0]


def solution(mesh):
    placed = (
        P("dp", None, None),
        P("dp", None, None),
        P("dp", None, None),
        P("pipe", None, None),
        P("pipe", None, None),
        P("pipe", None),
        P("pipe", None),
        P(),
    )
    return jax.shard_map(
        per_device,
        mesh=mesh,
        in_specs=placed,
        out_specs=(P("pipe", "dp", None), P("pipe", "dp", None), P("pipe", "dp"), P("pipe", "dp")),
        check_vma=False,
    )
```

```python
import functools

import jax
import jax.numpy as jnp
from jax import lax
from jax.experimental import pallas as pl
from jax.experimental.pallas import tpu as pltpu
from jax.sharding import PartitionSpec as P

HEAD_DIM = 256
EPSILON = 1e-06
QUERY_SCALE = 0.0625
EXTRA_ROWS = 16
GAIN_LANES = 128

BF16 = jnp.bfloat16
F32 = jnp.float32
def takes(microseconds):
    return pl.CostEstimate(flops=int(microseconds * 10**9), bytes_accessed=0, transcendentals=0)


ANY = pl.BlockSpec(memory_space=pl.ANY)
SMEM = pl.BlockSpec(memory_space=pltpu.SMEM)
VMEM = pl.BlockSpec(memory_space=pltpu.VMEM)
HBM = pl.BlockSpec(memory_space=pltpu.HBM)
PARAMS = pltpu.CompilerParams(vmem_limit_bytes=16 * 2**20)


def dot(left, right):
    return jnp.dot(left, right, preferred_element_type=F32)


def dot_nt(left, right):
    return lax.dot_general(left, right, (((1,), (1,)), ((), ())), preferred_element_type=F32)


def dot_tn(left, right):
    return lax.dot_general(left, right, (((0,), (0,)), ((), ())), preferred_element_type=F32)


def row_scale(values):
    return lax.rsqrt(jnp.mean(values * values, axis=-1, keepdims=True) + EPSILON)


def head(index):
    return slice(index * HEAD_DIM, (index + 1) * HEAD_DIM)


def normal(x, gain):
    hidden = x[...].astype(F32)
    return (hidden * row_scale(hidden) * gain).astype(BF16)


def attend_forward(x, query, source, out):
    heads = [head(part) for part in range(x.shape[-1] // HEAD_DIM)]
    raised = [jnp.exp(dot_nt(query[:, cols], source[:, cols])) for cols in heads]
    low = [(value / jnp.sum(value, axis=-1, keepdims=True)).astype(BF16) for value in raised]
    for cols, shares in zip(heads, low):
        out[:, cols] = (x[:, cols].astype(F32) + dot(shares, source[:, cols])).astype(BF16)


def queries_of(weight, normed, query):
    query[...] = (dot(normed[...], weight[...]) * QUERY_SCALE).astype(BF16)


def attend_backward(source, query, upstream, grad_query, grad_source, add):
    heads = [head(part) for part in range(source.shape[-1] // HEAD_DIM)]
    length = query.shape[0]
    if length % 128 == 0:
        sides = [jnp.concatenate([query[:, cols], upstream[:, cols]], axis=0) for cols in heads]
        both = [dot_nt(source[:, cols], side) for cols, side in zip(heads, sides)]
        raised = [jnp.exp(value[:, :length]) for value in both]
        grads = [value[:, length:] for value in both]
    else:
        raised = [jnp.exp(dot_nt(source[:, cols], query[:, cols])) for cols in heads]
        grads = [dot_nt(source[:, cols], upstream[:, cols]) for cols in heads]
    probs = [value / jnp.sum(value, axis=0, keepdims=True) for value in raised]
    scores = [
        (share * (grad - jnp.sum(grad * share, axis=0, keepdims=True))).astype(BF16) for share, grad in zip(probs, grads)
    ]
    for part, cols in enumerate(heads):
        low = probs[part].astype(BF16)
        grad_query[:, cols] = (dot_tn(scores[part], source[:, cols]) * QUERY_SCALE).astype(BF16)
        if length % 128 == 0:
            total = dot(jnp.concatenate([scores[part], low], axis=1), sides[part])
        else:
            total = dot(scores[part], query[:, cols]) + dot(low, upstream[:, cols])
        grad_source[:, cols] = grad_source[:, cols] + total if add else total


def grad_normed(weight, grad_query, scaled):
    for part in range(grad_query.shape[1] // HEAD_DIM):
        cols = head(part)
        scaled[:, cols] = dot_nt(weight[cols, :], grad_query[...]).T


def input_backward(x, gain, grad_source, upstream, scaled, out):
    hidden = x[...].astype(F32)
    scales = row_scale(hidden)
    grad = scaled[...] if grad_source is None else scaled[...] + grad_source[...]
    grad = gain * grad
    mean = jnp.mean(grad * hidden, axis=-1, keepdims=True)
    factor = scales * scales * scales * mean
    out[...] = (upstream[...].astype(F32) + scales * grad - hidden * factor).astype(BF16)


def dec_input_backward(weight, x, gain, grad_query, upstream, scaled, out):
    grad_normed(weight, grad_query, scaled)
    input_backward(x, gain, None, upstream, scaled, out)


def gain_row(x, grad_source):
    hidden = x[...].astype(F32)
    return jnp.sum(grad_source[...] * hidden * row_scale(hidden), axis=0, keepdims=True)


def by_core(core, low, high, own, other):
    for mine in (0, 1):

        @pl.when(core == mine)
        def _():
            own[...] = high[...] if mine else low[...]
            other[...] = low[...] if mine else high[...]


def load_kernel(own, other, gate, pair, sems):
    copies = [pltpu.make_async_copy(part, pair.at[slot], sems.at[slot]) for slot, part in enumerate((own, other))]
    for copy in copies:
        copy.start()
    for copy in copies:
        copy.wait()


def load_call(own, other, gate):
    pair = pl.pallas_call(
        load_kernel,
        name="load_weights",
        cost_estimate=takes(4),
        out_shape=pltpu.VMEM((2,) + own.shape, BF16),
        in_specs=[ANY] * 3,
        out_specs=VMEM,
        scratch_shapes=[pltpu.SemaphoreType.DMA((2,))],
        compiler_params=PARAMS,
    )(streamed(own), streamed(other), gate)
    return pinned(pair)


def streamed(value):
    return pltpu.with_memory_space_constraint(value, pltpu.HBM)


def pinned(value):
    return pltpu.with_memory_space_constraint(value, pltpu.VMEM)


def both_sequences(x, normed, query, out):
    count, length, width = x.shape
    for sequence in range(count):
        rows = pl.ds(sequence * length, length)
        attend_forward(x.at[sequence], query.at[rows], normed.at[rows], out.at[sequence])


def both_normal(x, gain, normed):
    count, length, width = x.shape
    for sequence in range(count):
        normed[sequence * length : (sequence + 1) * length] = normal(x.at[sequence], gain[...])


def first_kernel(turn, flags, x_any, weight_any, gain, *refs):
    out, x, weight, normed, query, x_sem, sems = refs[-7:]

    @pl.when(jnp.logical_and(flags[0] == turn, flags[1] == 0))
    def _():
        parts = range(x.shape[-1] // HEAD_DIM)
        rows = pltpu.make_async_copy(x_any, x, x_sem)
        rows.start()
        copies = [
            pltpu.make_async_copy(weight_any.at[:, head(part)], weight.at[:, head(part)], sems.at[part]) for part in parts
        ]
        for copy in copies:
            copy.start()
        rows.wait()
        both_normal(x, gain, normed)
        middle = len(parts) // 2
        for half in (parts[:middle], parts[middle:]):
            for part in half:
                copies[part].wait()
            for part in half:
                query[:, head(part)] = (dot(normed[...], weight[:, head(part)]) * QUERY_SCALE).astype(BF16)
        both_sequences(x, normed, query, out)

def first_call(turn, flags, x, weight, gain, *gates):
    count, length, width = x.shape
    return pl.pallas_call(
        functools.partial(first_kernel, turn),
        name="enc_first_lower" if turn == 0 else "enc_first_upper",
        cost_estimate=takes(6),
        out_shape=jax.ShapeDtypeStruct(x.shape, BF16),
        in_specs=[SMEM, ANY, ANY, VMEM] + [ANY] * len(gates),
        out_specs=VMEM,
        scratch_shapes=[pltpu.VMEM(x.shape, BF16), pltpu.VMEM((width, width), BF16)]
        + [pltpu.VMEM((count * length, width), BF16)] * 2
        + [pltpu.SemaphoreType.DMA, pltpu.SemaphoreType.DMA((width // HEAD_DIM,))],
        compiler_params=PARAMS,
    )(flags, x, streamed(weight), gain, *gates)


def enc_forward_kernel(
    flags, x_any, recv0, recv1, pair, gains, mem_gain, mem, n_own, n_other, saved, sem
):
    core, upper = flags[0], flags[1]
    x0, x1, x2, n0, n1, q0, q1 = [saved.at[place] for place in range(7)]

    @pl.when(upper == 0)
    def _():
        pltpu.make_async_copy(x_any.at[core], x0, sem).start()

    for mine, received in enumerate((recv0, recv1)):

        @pl.when(jnp.logical_and(upper == 1, core == mine))
        def _():
            pltpu.make_async_copy(received, x0, sem).start()

    pltpu.make_async_copy(recv0, x0, sem).wait()
    n0[...] = normal(x0, gains[0:1])
    queries_of(pair.at[core], n0, q0)
    attend_forward(x0, q0, n0, x1)
    n1[...] = normal(x1, gains[1:2])
    queries_of(pair.at[1 - core], n1, q1)
    attend_forward(x1, q1, n1, x2)
    mem[...] = normal(x2, mem_gain[...])
    by_core(core, n0, n1, n_own, n_other)


def enc_forward_call(flags, x, recv0, recv1, pair, gains, mem_gain):
    row = jax.ShapeDtypeStruct(recv0.shape, BF16)
    return pl.pallas_call(
        enc_forward_kernel,
        name="enc_forward",
        cost_estimate=takes(5.3),
        out_shape=[row] * 3 + [jax.ShapeDtypeStruct((7,) + recv0.shape, BF16)],
        in_specs=[SMEM, ANY, ANY, ANY] + [VMEM] * 3,
        out_specs=[VMEM] * 4,
        scratch_shapes=[pltpu.SemaphoreType.DMA],
        compiler_params=PARAMS,
    )(flags, streamed(x), recv0, recv1, pair, gains, mem_gain)


def dec_query_kernel(flags, x_any, pair, gains, ahead, sem, y0):
    core, upper = flags[0], flags[1]
    n0, q0 = ahead.at[0], ahead.at[1]

    @pl.when(upper == 0)
    def _():
        rows = pltpu.make_async_copy(x_any.at[core], y0, sem)
        rows.start()
        rows.wait()
        n0[...] = normal(y0, gains[0:1])
        queries_of(pair.at[core], n0, q0)


def dec_query_call(flags, x, pair, gains):
    return pl.pallas_call(
        dec_query_kernel,
        name="dec_query",
        cost_estimate=takes(2.4),
        out_shape=jax.ShapeDtypeStruct((2,) + x.shape[1:], BF16),
        in_specs=[SMEM, ANY, VMEM, VMEM],
        out_specs=VMEM,
        scratch_shapes=[pltpu.SemaphoreType.DMA, pltpu.VMEM(x.shape[1:], BF16)],
        compiler_params=PARAMS,
    )(flags, x, pair, gains)


def dec_forward_kernel(flags, x_any, memory, ahead, pair, gains, y2, saved, sem, y0):
    core, upper = flags[0], flags[1]
    q0 = ahead.at[1]
    y1, n1, q1 = [saved.at[place] for place in range(3)]

    @pl.when(upper == 0)
    def _():
        rows = pltpu.make_async_copy(x_any.at[core], y0, sem)
        rows.start()
        rows.wait()
        attend_forward(y0, q0, memory, y1)
        n1[...] = normal(y1, gains[1:2])
        queries_of(pair.at[1 - core], n1, q1)
        attend_forward(y1, q1, memory, y2)


def dec_forward_call(flags, x, memory, ahead, pair, gains):
    row = jax.ShapeDtypeStruct(x.shape[1:], BF16)
    return pl.pallas_call(
        dec_forward_kernel,
        name="dec_forward",
        cost_estimate=takes(3.3),
        out_shape=[row, jax.ShapeDtypeStruct((3,) + x.shape[1:], BF16)],
        in_specs=[SMEM, ANY] + [VMEM] * 4,
        out_specs=[VMEM] * 2,
        scratch_shapes=[pltpu.SemaphoreType.DMA, pltpu.VMEM(x.shape[1:], BF16)],
        compiler_params=PARAMS,
    )(flags, x, memory, ahead, pair, gains)


def dec_turn_kernel(
    flags, y2, memory, upstream, pair, gains, out, grad_source, pays, n0, n1, y3, u3, q0, q1, dq0, dq1, scaled
):
    core, upper = flags[0], flags[1]

    @pl.when(upper == 1)
    def _():
        length = y2.shape[0]
        n0[...] = normal(y2, gains[0:1])
        queries_of(pair.at[core], n0, q0)
        attend_forward(y2, q0, memory, y3)
        n1[...] = normal(y3, gains[1:2])
        queries_of(pair.at[1 - core], n1, q1)
        attend_backward(memory, q1, upstream, dq1, grad_source, False)
        dec_input_backward(pair.at[1 - core], y3, gains[1:2], dq1, upstream, scaled, u3)
        attend_backward(memory, q0, u3, dq0, grad_source, True)
        dec_input_backward(pair.at[core], y2, gains[0:1], dq0, u3, scaled, out)
        for payload, normed, grad in ((pays.at[0], n0, dq0), (pays.at[1], n1, dq1)):
            payload[0:length] = normed[...]
            payload[length:] = grad[...]


def dec_turn_call(flags, y2, memory, upstream, pair, gains):
    length, width = y2.shape
    row = jax.ShapeDtypeStruct((length, width), BF16)
    payload = jax.ShapeDtypeStruct((2, 2 * length, width), BF16)
    held = pltpu.VMEM((length, width), BF16)
    return pl.pallas_call(
        dec_turn_kernel,
        name="dec_turn",
        cost_estimate=takes(11),
        out_shape=[row, jax.ShapeDtypeStruct(memory.shape, F32), payload],
        in_specs=[SMEM] + [VMEM] * 5,
        out_specs=[VMEM] * 3,
        scratch_shapes=[held] * 8 + [pltpu.VMEM((length, width), F32)],
        compiler_params=PARAMS,
    )(flags, y2, memory, upstream, pair, gains)


def dec_backward_kernel(
    flags, upstream, memory, ahead, saved, pair, gains, done, source_low, out_own, out_other, u1, dq0, dq1, grad_source, scaled, pay0, pay1
):
    core, upper = flags[0], flags[1]
    n0, q0 = ahead.at[0], ahead.at[1]
    y1, n1, q1 = [saved.at[place] for place in range(3)]

    @pl.when(upper == 0)
    def _():
        length = y1.shape[0]
        attend_backward(memory, q1, upstream, dq1, grad_source, False)
        dec_input_backward(pair.at[1 - core], y1, gains[1:2], dq1, upstream, scaled, u1)
        attend_backward(memory, q0, u1, dq0, grad_source, True)
        source_low[...] = grad_source[...].astype(BF16)
        for payload, normed, grad in ((pay0, n0, dq0), (pay1, n1, dq1)):
            payload[0:length] = normed[...]
            payload[length:] = grad[...]
        by_core(core, pay0, pay1, out_own, out_other)

    @pl.when(upper == 1)
    def _():
        by_core(core, done.at[0], done.at[1], out_own, out_other)


def dec_backward_call(flags, upstream, memory, ahead, saved, pair, gains, done):
    length, width = upstream.shape
    payload = jax.ShapeDtypeStruct((2 * length, width), BF16)
    held = pltpu.VMEM((length, width), BF16)
    return pl.pallas_call(
        dec_backward_kernel,
        name="dec_backward",
        cost_estimate=takes(5.5),
        out_shape=[jax.ShapeDtypeStruct(memory.shape, BF16), payload, payload],
        in_specs=[SMEM] + [VMEM] * 7,
        out_specs=[VMEM] * 3,
        scratch_shapes=[held] * 3
        + [pltpu.VMEM(memory.shape, F32), pltpu.VMEM((length, width), F32)]
        + [pltpu.VMEM(payload.shape, BF16)] * 2,
        compiler_params=PARAMS,
    )(flags, upstream, memory, ahead, saved, pair, gains, done)


def put_payload(core, payload, grad_query, x, grad_source):
    length, width = grad_query.shape
    payload[0:length] = grad_query[...]
    place = lax.broadcasted_iota(jnp.int32, (EXTRA_ROWS, width), 0)
    payload[length:] = jnp.where(place == core, gain_row(x, grad_source), 0.0).astype(BF16)


def enc_backward_first_kernel(
    flags, source_mine, source_recv, mem_gain, pair, gains, saved, out, pay0, pay1, u2, u1, grad_query, grad_source, scaled
):
    x0, x1, x2, n0, n1, q0, q1 = [saved.at[place] for place in range(7)]
    core, upper = flags[0], flags[1]

    @pl.when(upper == 1)
    def _():
        hidden = x2[...].astype(F32)
        scales = row_scale(hidden)
        grad = mem_gain[...] * (source_mine[...] + source_recv[...].astype(F32))
        mean = jnp.mean(grad * hidden, axis=-1, keepdims=True)
        u2[...] = (scales * grad - hidden * (scales * scales * scales * mean)).astype(BF16)
        attend_backward(n1, q1, u2, grad_query, grad_source, False)
        put_payload(core, pay1, grad_query, x1, grad_source)
        grad_normed(pair.at[1 - core], grad_query, scaled)
        input_backward(x1, gains[1:2], grad_source, u2, scaled, u1)
        attend_backward(n0, q0, u1, grad_query, grad_source, False)
        put_payload(core, pay0, grad_query, x0, grad_source)
        grad_normed(pair.at[core], grad_query, scaled)
        input_backward(x0, gains[0:1], grad_source, u1, scaled, out)


def enc_backward_first_call(flags, source_mine, source_recv, mem_gain, pair, gains, saved):
    length, width = saved.shape[1:]
    row = jax.ShapeDtypeStruct((length, width), BF16)
    payload = jax.ShapeDtypeStruct((length + EXTRA_ROWS, width), BF16)
    return pl.pallas_call(
        enc_backward_first_kernel,
        name="enc_backward_first",
        cost_estimate=takes(10),
        out_shape=[row, payload, payload],
        in_specs=[SMEM] + [VMEM] * 3 + [VMEM] * 3,
        out_specs=[VMEM] * 3,
        scratch_shapes=[pltpu.VMEM((length, width), BF16)] * 3
        + [pltpu.VMEM((length, width), F32)] * 2,
        compiler_params=PARAMS,
    )(flags, source_mine, source_recv, mem_gain, pair, gains, saved)


def enc_backward_last_kernel(
    flags, upstream, done0, done1, pair, gains, saved, gate, later_gate, out_own, out_other, pay0, pay1, u1, grad_query, grad_source, scaled
):
    x0, x1, _, n0, n1, q0, q1 = [saved.at[place] for place in range(7)]
    core, upper = flags[0], flags[1]

    @pl.when(upper == 0)
    def _():
        attend_backward(n1, q1, upstream, grad_query, grad_source, False)
        put_payload(core, pay1, grad_query, x1, grad_source)
        grad_normed(pair.at[1 - core], grad_query, scaled)
        input_backward(x1, gains[1:2], grad_source, upstream, scaled, u1)
        attend_backward(n0, q0, u1, grad_query, grad_source, False)
        put_payload(core, pay0, grad_query, x0, grad_source)
        by_core(core, pay0, pay1, out_own, out_other)

    @pl.when(upper == 1)
    def _():
        by_core(core, done0, done1, out_own, out_other)


def enc_backward_last_call(flags, upstream, done0, done1, pair, gains, saved, *gates):
    length, width = upstream.shape
    payload = jax.ShapeDtypeStruct((length + EXTRA_ROWS, width), BF16)
    return pl.pallas_call(
        enc_backward_last_kernel,
        name="enc_backward_last",
        cost_estimate=takes(7),
        out_shape=[payload, payload],
        in_specs=[SMEM] + [VMEM] * 3 + [VMEM] * 3 + [ANY] * 2,
        out_specs=[VMEM] * 2,
        scratch_shapes=[pltpu.VMEM(payload.shape, BF16)] * 2
        + [pltpu.VMEM((length, width), BF16)] * 2
        + [pltpu.VMEM((length, width), F32)] * 2,
        compiler_params=PARAMS,
    )(flags, upstream, done0, done1, pair, gains, saved, *gates)


def features(place, index, block):
    row = lax.broadcasted_iota(jnp.int32, (block, 1), 0)
    half = block // 2
    return jnp.where(row < half, place[index * 2] + row, place[index * 2 + 1] + row - half)


def ones_at(place, index, block, width):
    lanes = lax.broadcasted_iota(jnp.int32, (block, width), 1)
    return jnp.where(lanes == features(place, index, block), 1.0, 0.0).astype(BF16)


def choose_kernel(place, *refs):
    pieces, out, (ones,) = refs[:4], refs[5], refs[6:]
    rows, width = pieces[0].shape
    block = out.shape[0] // 4
    for index in range(4):
        ones[index * block : (index + 1) * block] = ones_at(place, index, block, width)
    for index in range(4):
        out[:, index * rows : (index + 1) * rows] = dot_nt(ones[...], pieces[index][...]).astype(BF16)


def choose_call(place, pieces, gate):
    rows, width = pieces[0].shape
    return pl.pallas_call(
        choose_kernel,
        name="choose_enc",
        cost_estimate=takes(4.3),
        out_shape=jax.ShapeDtypeStruct((width // 4, 4 * rows), BF16),
        in_specs=[SMEM] + [VMEM] * 4 + [ANY],
        out_specs=VMEM,
        scratch_shapes=[pltpu.VMEM((width // 4, width), BF16)],
        compiler_params=PARAMS,
    )(place, *pieces, gate)


def dec_product_kernel(place, *refs):
    pieces, outs, (normed, grads) = refs[:4], refs[4:6], refs[6:]
    length = pieces[0].shape[0] // 4
    for index in range(8):
        start = index % 2 * 2 * length
        normed[index * length : (index + 1) * length] = pieces[index // 2][start : start + length]
        grads[index * length : (index + 1) * length] = pieces[index // 2][start + length : start + 2 * length]
    half = outs[0].shape[0] // 4
    for index in range(4):
        columns = dot_nt(ones_at(place, index, 2 * half, normed.shape[1]), normed[...]).astype(BF16)
        product = dot(columns, grads[...]).astype(BF16)
        for side in range(2):
            outs[side][index * half : (index + 1) * half] = product[side * half : (side + 1) * half]


def dec_product_call(place, pieces):
    rows, width = pieces[0].shape
    return pl.pallas_call(
        dec_product_kernel,
        name="product_dec",
        cost_estimate=takes(4.4),
        out_shape=[jax.ShapeDtypeStruct((width // 8, width), BF16)] * 2,
        in_specs=[SMEM] + [VMEM] * 4,
        out_specs=[VMEM] * 2,
        scratch_shapes=[pltpu.VMEM((2 * rows, width), BF16)] * 2,
        compiler_params=PARAMS,
    )(place, *pieces)


def enc_product_kernel(place, slices, *refs):
    pieces, outs, (held,) = refs[:4], refs[4:8], refs[8:]
    length, width = slices.shape[1] // 8, pieces[0].shape[1]
    block = slices.shape[0] // 4
    extra = jnp.zeros((EXTRA_ROWS, width), F32)
    for index in range(4):
        held[2 * index * length : 2 * (index + 1) * length] = pieces[index][0 : 2 * length]
        extra = extra + pieces[index][2 * length :].astype(F32)
    extra = jnp.sum(extra, axis=0, keepdims=True)
    for index in range(4):
        outs[index][:, 0:width] = dot(slices[index * block : (index + 1) * block], held[...]).astype(BF16)
        lanes = lax.broadcasted_iota(jnp.int32, (block, width), 1)
        column = jnp.sum(jnp.where(lanes == features(place, index, block), extra, 0.0), axis=-1, keepdims=True)
        outs[index][:, width:] = jnp.broadcast_to(column, (block, GAIN_LANES)).astype(BF16)


def enc_product_call(place, slices, pieces):
    width = pieces[0].shape[1]
    return pl.pallas_call(
        enc_product_kernel,
        name="product_enc",
        cost_estimate=takes(3.5),
        out_shape=[jax.ShapeDtypeStruct((slices.shape[0] // 4, width + GAIN_LANES), BF16)] * 4,
        in_specs=[SMEM] + [VMEM] * 5,
        out_specs=[VMEM] * 4,
        scratch_shapes=[pltpu.VMEM((slices.shape[1], width), BF16)],
        compiler_params=PARAMS,
    )(place, slices, *pieces)


def finish_kernel(low, recv, weight, gain, rows, gain_out):
    width = weight.shape[1]
    total = low[...].astype(F32)
    for part in recv:
        total = total + part[...].astype(F32)
    rows[...] = total[:, :width]
    column = jnp.sum(weight[...].astype(F32) * total[:, :width], axis=-1, keepdims=True) / gain[...]
    if low.shape[1] > width:
        column = column + total[:, width : width + 1]
    gain_out[...] = column


def finish_call(low, recv, weight, gain):
    count, width = weight.shape

    def kernel(low, *refs):
        finish_kernel(low, refs[: len(recv)], *refs[len(recv) :])

    return pl.pallas_call(
        kernel,
        name="finish_enc" if low.shape[1] > width else "finish_dec",
        out_shape=[jax.ShapeDtypeStruct((count, width), F32), jax.ShapeDtypeStruct((count, 1), F32)],
        in_specs=[VMEM] * (3 + len(recv)),
        out_specs=[VMEM] * 2,
        compiler_params=PARAMS,
    )(low, *recv, weight, gain)


def device(pipe, high, deep, across):
    return pipe * 32 + (high % 2) * 16 + (deep % 4) * 4 + across % 4


def all_places():
    return [(pipe, high, deep, across) for pipe in range(4) for high in range(2) for deep in range(4) for across in range(4)]


def moved(place, along_x, step):
    pipe, high, deep, across = place
    return device(pipe, high, deep, across + step) if along_x else device(pipe, high, deep + step, across)


def gather_perm(step):
    return [(device(*place), moved(place, place[0] % 2 == 0, step)) for place in all_places()]


def reduce_perm(step):
    return [(device(*place), moved(place, place[0] % 2 == 1, step)) for place in all_places()]


HALF_PERM = [(device(*place), device(place[0], place[1] + 1, place[2], place[3])) for place in all_places()]
ASIDE_PERM = [(device(*place), device(place[0] ^ 1, place[1], place[2], place[3] + 1)) for place in all_places()]
SWAP_PERM = [(device(*place), device(place[0] ^ 1, *place[1:])) for place in all_places()]
UP_PERM = [
    (device(pipe, high, deep, across), device(pipe + 2, high + pipe, deep, across))
    for pipe, high, deep, across in all_places()
    if pipe < 2
]
DOWN_PERM = [(target, source) for source, target in UP_PERM]
FIRST_PERM = [(device(*place), device(place[0] + 1, *place[1:])) for place in all_places() if place[0] % 2 == 0]
OUT_PERMS = [
    [(device(1, high, deep, across), device(2 + core, high + core, deep, across)) for _, high, deep, across in all_places()[:32]]
    for core in range(2)
]


def send(value, perm):
    return lax.ppermute(value, ("pipe", "dp"), perm)


def gather(mine, other, extra=0):
    other = send(other, SWAP_PERM)
    if extra:
        rows = mine.shape[0] - extra
        whole = jnp.concatenate([mine[:rows], other[:rows], mine[rows:] + other[rows:]], axis=0)
    else:
        whole = jnp.concatenate([mine, other], axis=0)
    return [whole] + [send(whole, gather_perm(step)) for step in (1, 2, 3)]


def per_device(enc_in, dec_in, out_grad, enc_weight, dec_weight, enc_gain, dec_gain, mem_gain):
    pipe = lax.axis_index("pipe")
    spot = lax.axis_index("dp")
    core, upper = pipe % 2, pipe // 2
    high, deep, across = spot // 16, (spot // 4) % 4, spot % 4
    even = core == 0
    near, far = jnp.where(even, across, deep), jnp.where(even, deep, across)
    flags = jnp.stack([core, upper]).astype(jnp.int32)
    width = enc_weight.shape[1]
    mem_gain = mem_gain[None]

    def place_of(step, half):
        group, third = jnp.where(even, (far + step) % 4, near), jnp.where(even, near, (far + step) % 4)
        return ((high + half) % 2 * 16 + group * 4 + third) * (width // 32)

    place = jnp.stack([place_of(step, half) for step in range(4) for half in range(2)]).astype(jnp.int32)

    enc_own, dec_own = enc_weight[0], dec_weight[0]
    gains = jnp.concatenate([enc_gain, dec_gain], axis=0)
    gains_other = send(gains, ASIDE_PERM)
    pair = jnp.where(even, jnp.stack([gains, gains_other]), jnp.stack([gains_other, gains]))
    enc_gains, dec_gains = pair[:, 0], pair[:, 1]

    enc_other = send(enc_own, SWAP_PERM)
    x1 = send(first_call(0, flags, streamed(enc_in), enc_own, enc_gain), FIRST_PERM)
    x2 = first_call(1, flags, x1, enc_own, enc_gain, gains_other)
    received = [send(x2[sequence], OUT_PERMS[sequence]) for sequence in range(2)]
    enc_pair = load_call(enc_own, enc_other, x2)
    memory, n_own, n_other, saved = enc_forward_call(flags, enc_in, *received, enc_pair, enc_gains, mem_gain)
    memory_recv = send(memory, DOWN_PERM)
    normed_pieces = gather(n_own, n_other)
    upstream = send(jnp.where(even, out_grad[0], out_grad[1]), UP_PERM)
    dec_other = send(dec_own, SWAP_PERM)
    dec_pair = load_call(dec_own, dec_other, memory)
    ahead = dec_query_call(flags, dec_in, dec_pair, dec_gains)

    y2, dec_saved = dec_forward_call(flags, dec_in, memory_recv, ahead, dec_pair, dec_gains)
    dec_pair = load_call(dec_own, dec_other, dec_saved)
    u2, source_mine, dec_done = dec_turn_call(flags, send(y2, UP_PERM), memory, upstream, dec_pair, dec_gains)
    dec_pair = load_call(dec_own, dec_other, dec_done)
    source_low, dec_own_pay, dec_other_pay = dec_backward_call(
        flags, send(u2, DOWN_PERM), memory_recv, ahead, dec_saved, dec_pair, dec_gains, dec_done
    )
    dec_pieces = gather(dec_own_pay, dec_other_pay)
    enc_pair = load_call(enc_own, enc_other, source_low)

    u_low, done0, done1 = enc_backward_first_call(
        flags, source_mine, send(source_low, UP_PERM), mem_gain, enc_pair, enc_gains, saved
    )
    dec_blocks = dec_product_call(place, dec_pieces)
    slices = choose_call(place, normed_pieces, u_low)
    own_pay, other_pay = enc_backward_last_call(
        flags, send(u_low, DOWN_PERM), done0, done1, enc_pair, enc_gains, saved, dec_blocks[0], slices
    )

    count = width // 32

    def rows_of(weight, gain):
        start = spot * count
        return (
            lax.dynamic_slice_in_dim(weight, start, count, 0),
            lax.dynamic_slice_in_dim(gain[0], start, count, 0)[:, None],
        )

    dec_sum = (dec_blocks[0].astype(F32) + send(dec_blocks[1], HALF_PERM).astype(F32)).astype(BF16)
    dec_parts = [dec_sum[step * count : (step + 1) * count] for step in range(4)]
    dec_recv = [send(dec_parts[step], reduce_perm(step)) for step in (1, 2, 3)]

    enc_blocks = enc_product_call(place, slices, gather(own_pay, other_pay, EXTRA_ROWS))
    enc_sum = enc_blocks[0].astype(F32)
    for step in (1, 2, 3):
        enc_sum = enc_sum + send(enc_blocks[step], reduce_perm(step)).astype(F32)
    enc_recv = send(enc_sum[count:].astype(BF16), HALF_PERM)

    dec_rows, dec_column = finish_call(dec_parts[0], dec_recv, *rows_of(dec_own, dec_gain))
    enc_rows, enc_column = finish_call(enc_sum[:count], [enc_recv], *rows_of(enc_own, enc_gain))
    return enc_rows[None], dec_rows[None], enc_column[None, :, 0], dec_column[None, :, 0]


def solution(mesh):
    placed = (
        P("dp", None, None),
        P("dp", None, None),
        P("dp", None, None),
        P("pipe", None, None),
        P("pipe", None, None),
        P("pipe", None),
        P("pipe", None),
        P(),
    )
    return jax.shard_map(
        per_device,
        mesh=mesh,
        in_specs=placed,
        out_specs=(P("pipe", "dp", None), P("pipe", "dp", None), P("pipe", "dp"), P("pipe", "dp")),
        check_vma=False,
    )
```

```python
import functools

import jax
import jax.numpy as jnp
from jax import lax
from jax.experimental import pallas as pl
from jax.experimental.pallas import tpu as pltpu
from jax.sharding import PartitionSpec as P

HEAD_DIM = 256
EPSILON = 1e-06
QUERY_SCALE = 0.0625
EXTRA_ROWS = 16
GAIN_LANES = 128

BF16 = jnp.bfloat16
F32 = jnp.float32
def takes(microseconds):
    return pl.CostEstimate(flops=int(microseconds * 10**9), bytes_accessed=0, transcendentals=0)


ANY = pl.BlockSpec(memory_space=pl.ANY)
SMEM = pl.BlockSpec(memory_space=pltpu.SMEM)
VMEM = pl.BlockSpec(memory_space=pltpu.VMEM)
HBM = pl.BlockSpec(memory_space=pltpu.HBM)
PARAMS = pltpu.CompilerParams(vmem_limit_bytes=14 * 2**20)


def dot(left, right):
    return jnp.dot(left, right, preferred_element_type=F32)


def dot_nt(left, right):
    return lax.dot_general(left, right, (((1,), (1,)), ((), ())), preferred_element_type=F32)


def dot_tn(left, right):
    return lax.dot_general(left, right, (((0,), (0,)), ((), ())), preferred_element_type=F32)


def row_scale(values):
    return lax.rsqrt(jnp.mean(values * values, axis=-1, keepdims=True) + EPSILON)


def head(index):
    return slice(index * HEAD_DIM, (index + 1) * HEAD_DIM)


def normal(x, gain):
    hidden = x[...].astype(F32)
    return (hidden * row_scale(hidden) * gain).astype(BF16)


def attend_forward(x, query, source, out):
    heads = [head(part) for part in range(x.shape[-1] // HEAD_DIM)]
    raised = [jnp.exp(dot_nt(query[:, cols], source[:, cols])) for cols in heads]
    low = [(value / jnp.sum(value, axis=-1, keepdims=True)).astype(BF16) for value in raised]
    for cols, shares in zip(heads, low):
        out[:, cols] = (x[:, cols].astype(F32) + dot(shares, source[:, cols])).astype(BF16)


def queries_of(weight, normed, query):
    query[...] = (dot(normed[...], weight[...]) * QUERY_SCALE).astype(BF16)


def attend_backward(source, query, upstream, grad_query, grad_source, add):
    heads = [head(part) for part in range(source.shape[-1] // HEAD_DIM)]
    length = query.shape[0]
    if length % 128 == 0:
        sides = [jnp.concatenate([query[:, cols], upstream[:, cols]], axis=0) for cols in heads]
        both = [dot_nt(source[:, cols], side) for cols, side in zip(heads, sides)]
        raised = [jnp.exp(value[:, :length]) for value in both]
        grads = [value[:, length:] for value in both]
    else:
        raised = [jnp.exp(dot_nt(source[:, cols], query[:, cols])) for cols in heads]
        grads = [dot_nt(source[:, cols], upstream[:, cols]) for cols in heads]
    probs = [value / jnp.sum(value, axis=0, keepdims=True) for value in raised]
    scores = [
        (share * (grad - jnp.sum(grad * share, axis=0, keepdims=True))).astype(BF16) for share, grad in zip(probs, grads)
    ]
    for part, cols in enumerate(heads):
        low = probs[part].astype(BF16)
        grad_query[:, cols] = (dot_tn(scores[part], source[:, cols]) * QUERY_SCALE).astype(BF16)
        if length % 128 == 0:
            total = dot(jnp.concatenate([scores[part], low], axis=1), sides[part])
        else:
            total = dot(scores[part], query[:, cols]) + dot(low, upstream[:, cols])
        grad_source[:, cols] = grad_source[:, cols] + total if add else total


def grad_normed(weight, grad_query, scaled):
    for part in range(grad_query.shape[1] // HEAD_DIM):
        cols = head(part)
        scaled[:, cols] = dot_nt(weight[cols, :], grad_query[...]).T


def input_backward(x, gain, grad_source, upstream, scaled, out):
    hidden = x[...].astype(F32)
    scales = row_scale(hidden)
    grad = scaled[...] if grad_source is None else scaled[...] + grad_source[...]
    grad = gain * grad
    mean = jnp.mean(grad * hidden, axis=-1, keepdims=True)
    factor = scales * scales * scales * mean
    out[...] = (upstream[...].astype(F32) + scales * grad - hidden * factor).astype(BF16)


def dec_input_backward(weight, x, gain, grad_query, upstream, scaled, out):
    grad_normed(weight, grad_query, scaled)
    input_backward(x, gain, None, upstream, scaled, out)


def gain_row(x, grad_source):
    hidden = x[...].astype(F32)
    return jnp.sum(grad_source[...] * hidden * row_scale(hidden), axis=0, keepdims=True)


def by_core(core, low, high, own, other):
    for mine in (0, 1):

        @pl.when(core == mine)
        def _():
            own[...] = high[...] if mine else low[...]
            other[...] = low[...] if mine else high[...]


def load_kernel(role, flags, own, other, gate, pair, sems):
    def body():
        copies = [pltpu.make_async_copy(part, pair.at[slot], sems.at[slot]) for slot, part in enumerate((own, other))]
        for copy in copies:
            copy.start()
        for copy in copies:
            copy.wait()

    if role is None:
        body()
    else:
        pl.when(flags[1] == role)(body)


def load_call(role, flags, own, other, gate):
    pair = pl.pallas_call(
        functools.partial(load_kernel, role),
        name="load_weights",
        cost_estimate=takes(4),
        out_shape=pltpu.VMEM((2,) + own.shape, BF16),
        in_specs=[SMEM] + [ANY] * 3,
        out_specs=VMEM,
        scratch_shapes=[pltpu.SemaphoreType.DMA((2,))],
        compiler_params=PARAMS,
    )(flags, streamed(own), streamed(other), gate)
    return pinned(pair)


def streamed(value):
    return pltpu.with_memory_space_constraint(value, pltpu.HBM)


def pinned(value):
    return pltpu.with_memory_space_constraint(value, pltpu.VMEM)


def both_sequences(x, normed, query, out):
    count, length, width = x.shape
    for sequence in range(count):
        rows = pl.ds(sequence * length, length)
        attend_forward(x.at[sequence], query.at[rows], normed.at[rows], out.at[sequence])


def both_normal(x, gain, normed):
    count, length, width = x.shape
    for sequence in range(count):
        normed[sequence * length : (sequence + 1) * length] = normal(x.at[sequence], gain[...])


def first_kernel(turn, flags, x_any, weight_any, gain, *refs):
    out, x, weight, normed, query, x_sem, sems = refs[-7:]

    @pl.when(jnp.logical_and(flags[0] == turn, flags[1] == 0))
    def _():
        parts = range(x.shape[-1] // HEAD_DIM)
        rows = pltpu.make_async_copy(x_any, x, x_sem)
        rows.start()
        copies = [
            pltpu.make_async_copy(weight_any.at[:, head(part)], weight.at[:, head(part)], sems.at[part]) for part in parts
        ]
        for copy in copies:
            copy.start()
        rows.wait()
        both_normal(x, gain, normed)
        middle = len(parts) // 2
        for half in (parts[:middle], parts[middle:]):
            for part in half:
                copies[part].wait()
            for part in half:
                query[:, head(part)] = (dot(normed[...], weight[:, head(part)]) * QUERY_SCALE).astype(BF16)
        both_sequences(x, normed, query, out)

def first_call(turn, flags, x, weight, gain, *gates):
    count, length, width = x.shape
    return pl.pallas_call(
        functools.partial(first_kernel, turn),
        name="enc_first_lower" if turn == 0 else "enc_first_upper",
        cost_estimate=takes(6),
        out_shape=jax.ShapeDtypeStruct(x.shape, BF16),
        in_specs=[SMEM, ANY, ANY, VMEM] + [ANY] * len(gates),
        out_specs=VMEM,
        scratch_shapes=[pltpu.VMEM(x.shape, BF16), pltpu.VMEM((width, width), BF16)]
        + [pltpu.VMEM((count * length, width), BF16)] * 2
        + [pltpu.SemaphoreType.DMA, pltpu.SemaphoreType.DMA((width // HEAD_DIM,))],
        compiler_params=PARAMS,
    )(flags, x, streamed(weight), gain, *gates)


def enc_forward_kernel(
    flags, x_any, recv0, recv1, pair, gains, mem_gain, mem, n_own, n_other, saved, sem
):
    core, upper = flags[0], flags[1]
    x0, x1, x2, n0, n1, q0, q1 = [saved.at[place] for place in range(7)]

    @pl.when(upper == 0)
    def _():
        pltpu.make_async_copy(x_any.at[core], x0, sem).start()

    for mine, received in enumerate((recv0, recv1)):

        @pl.when(jnp.logical_and(upper == 1, core == mine))
        def _():
            pltpu.make_async_copy(received, x0, sem).start()

    pltpu.make_async_copy(recv0, x0, sem).wait()
    n0[...] = normal(x0, gains[0:1])
    queries_of(pair.at[core], n0, q0)
    attend_forward(x0, q0, n0, x1)
    n1[...] = normal(x1, gains[1:2])
    queries_of(pair.at[1 - core], n1, q1)
    attend_forward(x1, q1, n1, x2)
    mem[...] = normal(x2, mem_gain[...])
    by_core(core, n0, n1, n_own, n_other)


def enc_forward_call(flags, x, recv0, recv1, pair, gains, mem_gain):
    row = jax.ShapeDtypeStruct(recv0.shape, BF16)
    return pl.pallas_call(
        enc_forward_kernel,
        name="enc_forward",
        cost_estimate=takes(5.3),
        out_shape=[row] * 3 + [jax.ShapeDtypeStruct((7,) + recv0.shape, BF16)],
        in_specs=[SMEM, ANY, ANY, ANY] + [VMEM] * 3,
        out_specs=[VMEM] * 4,
        scratch_shapes=[pltpu.SemaphoreType.DMA],
        compiler_params=PARAMS,
    )(flags, streamed(x), recv0, recv1, pair, gains, mem_gain)


def dec_query_kernel(flags, x_any, pair, gains, ahead, sem, y0):
    core, upper = flags[0], flags[1]
    n0, q0 = ahead.at[0], ahead.at[1]

    @pl.when(upper == 0)
    def _():
        rows = pltpu.make_async_copy(x_any.at[core], y0, sem)
        rows.start()
        rows.wait()
        n0[...] = normal(y0, gains[0:1])
        queries_of(pair.at[core], n0, q0)


def dec_query_call(flags, x, pair, gains):
    return pl.pallas_call(
        dec_query_kernel,
        name="dec_query",
        cost_estimate=takes(2.4),
        out_shape=jax.ShapeDtypeStruct((2,) + x.shape[1:], BF16),
        in_specs=[SMEM, ANY, VMEM, VMEM],
        out_specs=VMEM,
        scratch_shapes=[pltpu.SemaphoreType.DMA, pltpu.VMEM(x.shape[1:], BF16)],
        compiler_params=PARAMS,
    )(flags, x, pair, gains)


def dec_forward_kernel(flags, x_any, memory, ahead, pair, gains, y2, saved, sem, y0):
    core, upper = flags[0], flags[1]
    q0 = ahead.at[1]
    y1, n1, q1 = [saved.at[place] for place in range(3)]

    @pl.when(upper == 0)
    def _():
        rows = pltpu.make_async_copy(x_any.at[core], y0, sem)
        rows.start()
        rows.wait()
        attend_forward(y0, q0, memory, y1)
        n1[...] = normal(y1, gains[1:2])
        queries_of(pair.at[1 - core], n1, q1)
        attend_forward(y1, q1, memory, y2)


def dec_forward_call(flags, x, memory, ahead, pair, gains):
    row = jax.ShapeDtypeStruct(x.shape[1:], BF16)
    return pl.pallas_call(
        dec_forward_kernel,
        name="dec_forward",
        cost_estimate=takes(3.3),
        out_shape=[row, jax.ShapeDtypeStruct((3,) + x.shape[1:], BF16)],
        in_specs=[SMEM, ANY] + [VMEM] * 4,
        out_specs=[VMEM] * 2,
        scratch_shapes=[pltpu.SemaphoreType.DMA, pltpu.VMEM(x.shape[1:], BF16)],
        compiler_params=PARAMS,
    )(flags, x, memory, ahead, pair, gains)


def dec_turn_kernel(
    flags, y2, memory, upstream, pair, gains, out, grad_source, pays, n0, n1, y3, u3, q0, q1, dq0, dq1, scaled
):
    core, upper = flags[0], flags[1]

    @pl.when(upper == 1)
    def _():
        length = y2.shape[0]
        n0[...] = normal(y2, gains[0:1])
        queries_of(pair.at[core], n0, q0)
        attend_forward(y2, q0, memory, y3)
        n1[...] = normal(y3, gains[1:2])
        queries_of(pair.at[1 - core], n1, q1)
        attend_backward(memory, q1, upstream, dq1, grad_source, False)
        dec_input_backward(pair.at[1 - core], y3, gains[1:2], dq1, upstream, scaled, u3)
        attend_backward(memory, q0, u3, dq0, grad_source, True)
        dec_input_backward(pair.at[core], y2, gains[0:1], dq0, u3, scaled, out)
        for payload, normed, grad in ((pays.at[0], n0, dq0), (pays.at[1], n1, dq1)):
            payload[0:length] = normed[...]
            payload[length:] = grad[...]


def dec_turn_call(flags, y2, memory, upstream, pair, gains):
    length, width = y2.shape
    row = jax.ShapeDtypeStruct((length, width), BF16)
    payload = jax.ShapeDtypeStruct((2, 2 * length, width), BF16)
    held = pltpu.VMEM((length, width), BF16)
    return pl.pallas_call(
        dec_turn_kernel,
        name="dec_turn",
        cost_estimate=takes(11),
        out_shape=[row, jax.ShapeDtypeStruct(memory.shape, F32), payload],
        in_specs=[SMEM] + [VMEM] * 5,
        out_specs=[VMEM] * 3,
        scratch_shapes=[held] * 8 + [pltpu.VMEM((length, width), F32)],
        compiler_params=PARAMS,
    )(flags, y2, memory, upstream, pair, gains)


def dec_backward_kernel(
    flags, upstream, memory, ahead, saved, pair, gains, done, source_low, out_own, out_other, u1, dq0, dq1, grad_source, scaled, pay0, pay1
):
    core, upper = flags[0], flags[1]
    n0, q0 = ahead.at[0], ahead.at[1]
    y1, n1, q1 = [saved.at[place] for place in range(3)]

    @pl.when(upper == 0)
    def _():
        length = y1.shape[0]
        attend_backward(memory, q1, upstream, dq1, grad_source, False)
        dec_input_backward(pair.at[1 - core], y1, gains[1:2], dq1, upstream, scaled, u1)
        attend_backward(memory, q0, u1, dq0, grad_source, True)
        source_low[...] = grad_source[...].astype(BF16)
        for payload, normed, grad in ((pay0, n0, dq0), (pay1, n1, dq1)):
            payload[0:length] = normed[...]
            payload[length:] = grad[...]
        by_core(core, pay0, pay1, out_own, out_other)

    @pl.when(upper == 1)
    def _():
        by_core(core, done.at[0], done.at[1], out_own, out_other)


def dec_backward_call(flags, upstream, memory, ahead, saved, pair, gains, done):
    length, width = upstream.shape
    payload = jax.ShapeDtypeStruct((2 * length, width), BF16)
    held = pltpu.VMEM((length, width), BF16)
    return pl.pallas_call(
        dec_backward_kernel,
        name="dec_backward",
        cost_estimate=takes(5.5),
        out_shape=[jax.ShapeDtypeStruct(memory.shape, BF16), payload, payload],
        in_specs=[SMEM] + [VMEM] * 7,
        out_specs=[VMEM] * 3,
        scratch_shapes=[held] * 3
        + [pltpu.VMEM(memory.shape, F32), pltpu.VMEM((length, width), F32)]
        + [pltpu.VMEM(payload.shape, BF16)] * 2,
        compiler_params=PARAMS,
    )(flags, upstream, memory, ahead, saved, pair, gains, done)


def put_payload(core, payload, grad_query, x, grad_source):
    length, width = grad_query.shape
    payload[0:length] = grad_query[...]
    place = lax.broadcasted_iota(jnp.int32, (EXTRA_ROWS, width), 0)
    payload[length:] = jnp.where(place == core, gain_row(x, grad_source), 0.0).astype(BF16)


def enc_backward_first_kernel(
    flags, source_mine, source_recv, mem_gain, pair, gains, saved, out, pay0, pay1, u2, u1, grad_query, grad_source, scaled
):
    x0, x1, x2, n0, n1, q0, q1 = [saved.at[place] for place in range(7)]
    core, upper = flags[0], flags[1]

    @pl.when(upper == 1)
    def _():
        hidden = x2[...].astype(F32)
        scales = row_scale(hidden)
        grad = mem_gain[...] * (source_mine[...] + source_recv[...].astype(F32))
        mean = jnp.mean(grad * hidden, axis=-1, keepdims=True)
        u2[...] = (scales * grad - hidden * (scales * scales * scales * mean)).astype(BF16)
        attend_backward(n1, q1, u2, grad_query, grad_source, False)
        put_payload(core, pay1, grad_query, x1, grad_source)
        grad_normed(pair.at[1 - core], grad_query, scaled)
        input_backward(x1, gains[1:2], grad_source, u2, scaled, u1)
        attend_backward(n0, q0, u1, grad_query, grad_source, False)
        put_payload(core, pay0, grad_query, x0, grad_source)
        grad_normed(pair.at[core], grad_query, scaled)
        input_backward(x0, gains[0:1], grad_source, u1, scaled, out)


def enc_backward_first_call(flags, source_mine, source_recv, mem_gain, pair, gains, saved):
    length, width = saved.shape[1:]
    row = jax.ShapeDtypeStruct((length, width), BF16)
    payload = jax.ShapeDtypeStruct((length + EXTRA_ROWS, width), BF16)
    return pl.pallas_call(
        enc_backward_first_kernel,
        name="enc_backward_first",
        cost_estimate=takes(10),
        out_shape=[row, payload, payload],
        in_specs=[SMEM] + [VMEM] * 3 + [VMEM] * 3,
        out_specs=[VMEM] * 3,
        scratch_shapes=[pltpu.VMEM((length, width), BF16)] * 3
        + [pltpu.VMEM((length, width), F32)] * 2,
        compiler_params=PARAMS,
    )(flags, source_mine, source_recv, mem_gain, pair, gains, saved)


def enc_backward_last_kernel(
    flags, upstream, done0, done1, pair, gains, saved, gate, later_gate, out_own, out_other, pay0, pay1, u1, grad_query, grad_source, scaled
):
    x0, x1, _, n0, n1, q0, q1 = [saved.at[place] for place in range(7)]
    core, upper = flags[0], flags[1]

    @pl.when(upper == 0)
    def _():
        attend_backward(n1, q1, upstream, grad_query, grad_source, False)
        put_payload(core, pay1, grad_query, x1, grad_source)
        grad_normed(pair.at[1 - core], grad_query, scaled)
        input_backward(x1, gains[1:2], grad_source, upstream, scaled, u1)
        attend_backward(n0, q0, u1, grad_query, grad_source, False)
        put_payload(core, pay0, grad_query, x0, grad_source)
        by_core(core, pay0, pay1, out_own, out_other)

    @pl.when(upper == 1)
    def _():
        by_core(core, done0, done1, out_own, out_other)


def enc_backward_last_call(flags, upstream, done0, done1, pair, gains, saved, *gates):
    length, width = upstream.shape
    payload = jax.ShapeDtypeStruct((length + EXTRA_ROWS, width), BF16)
    return pl.pallas_call(
        enc_backward_last_kernel,
        name="enc_backward_last",
        cost_estimate=takes(7),
        out_shape=[payload, payload],
        in_specs=[SMEM] + [VMEM] * 3 + [VMEM] * 3 + [ANY] * 2,
        out_specs=[VMEM] * 2,
        scratch_shapes=[pltpu.VMEM(payload.shape, BF16)] * 2
        + [pltpu.VMEM((length, width), BF16)] * 2
        + [pltpu.VMEM((length, width), F32)] * 2,
        compiler_params=PARAMS,
    )(flags, upstream, done0, done1, pair, gains, saved, *gates)


def features(place, index, block):
    row = lax.broadcasted_iota(jnp.int32, (block, 1), 0)
    half = block // 2
    return jnp.where(row < half, place[index * 2] + row, place[index * 2 + 1] + row - half)


def ones_at(place, index, block, width):
    lanes = lax.broadcasted_iota(jnp.int32, (block, width), 1)
    return jnp.where(lanes == features(place, index, block), 1.0, 0.0).astype(BF16)


def choose_kernel(place, *refs):
    pieces, out, (ones,) = refs[:4], refs[5], refs[6:]
    rows, width = pieces[0].shape
    block = out.shape[0] // 4
    for index in range(4):
        ones[index * block : (index + 1) * block] = ones_at(place, index, block, width)
    for index in range(4):
        out[:, index * rows : (index + 1) * rows] = dot_nt(ones[...], pieces[index][...]).astype(BF16)


def choose_call(place, pieces, gate):
    rows, width = pieces[0].shape
    return pl.pallas_call(
        choose_kernel,
        name="choose_enc",
        cost_estimate=takes(4.3),
        out_shape=jax.ShapeDtypeStruct((width // 4, 4 * rows), BF16),
        in_specs=[SMEM] + [VMEM] * 4 + [ANY],
        out_specs=VMEM,
        scratch_shapes=[pltpu.VMEM((width // 4, width), BF16)],
        compiler_params=PARAMS,
    )(place, *pieces, gate)


def dec_product_kernel(place, *refs):
    pieces, outs, (normed, grads) = refs[:4], refs[5:7], refs[7:]
    length = pieces[0].shape[0] // 4
    for index in range(8):
        start = index % 2 * 2 * length
        normed[index * length : (index + 1) * length] = pieces[index // 2][start : start + length]
        grads[index * length : (index + 1) * length] = pieces[index // 2][start + length : start + 2 * length]
    half = outs[0].shape[0] // 4
    for index in range(4):
        columns = dot_nt(ones_at(place, index, 2 * half, normed.shape[1]), normed[...]).astype(BF16)
        product = dot(columns, grads[...]).astype(BF16)
        for side in range(2):
            outs[side][index * half : (index + 1) * half] = product[side * half : (side + 1) * half]


def dec_product_call(place, pieces, gate):
    rows, width = pieces[0].shape
    return pl.pallas_call(
        dec_product_kernel,
        name="product_dec",
        cost_estimate=takes(4.4),
        out_shape=[jax.ShapeDtypeStruct((width // 8, width), BF16)] * 2,
        in_specs=[SMEM] + [VMEM] * 4 + [ANY],
        out_specs=[VMEM] * 2,
        scratch_shapes=[pltpu.VMEM((2 * rows, width), BF16)] * 2,
        compiler_params=PARAMS,
    )(place, *pieces, gate)


def enc_product_kernel(place, slices_any, *refs):
    pieces, outs, (held, slices, sem) = refs[:4], refs[4:8], refs[8:]
    copy = pltpu.make_async_copy(slices_any, slices, sem)
    copy.start()
    length, width = slices.shape[1] // 8, pieces[0].shape[1]
    block = slices.shape[0] // 4
    extra = jnp.zeros((EXTRA_ROWS, width), F32)
    for index in range(4):
        held[2 * index * length : 2 * (index + 1) * length] = pieces[index][0 : 2 * length]
        extra = extra + pieces[index][2 * length :].astype(F32)
    extra = jnp.sum(extra, axis=0, keepdims=True)
    copy.wait()
    for index in range(4):
        outs[index][:, 0:width] = dot(slices[index * block : (index + 1) * block], held[...]).astype(BF16)
        lanes = lax.broadcasted_iota(jnp.int32, (block, width), 1)
        column = jnp.sum(jnp.where(lanes == features(place, index, block), extra, 0.0), axis=-1, keepdims=True)
        outs[index][:, width:] = jnp.broadcast_to(column, (block, GAIN_LANES)).astype(BF16)


def enc_product_call(place, slices, pieces):
    width = pieces[0].shape[1]
    return pl.pallas_call(
        enc_product_kernel,
        name="product_enc",
        cost_estimate=takes(3.5),
        out_shape=[jax.ShapeDtypeStruct((slices.shape[0] // 4, width + GAIN_LANES), BF16)] * 4,
        in_specs=[SMEM, ANY] + [VMEM] * 4,
        out_specs=[VMEM] * 4,
        scratch_shapes=[pltpu.VMEM((slices.shape[1], width), BF16), pltpu.VMEM(slices.shape, BF16), pltpu.SemaphoreType.DMA],
        compiler_params=PARAMS,
    )(place, streamed(slices), *pieces)


def finish_kernel(low, recv, weight, gain, rows, gain_out):
    count, width = weight.shape
    total = low[...].astype(F32)
    for part in recv:
        total = total + part[...].astype(F32)
    rows[...] = total[:, :width]
    column = jnp.sum(weight[...].astype(F32) * total[:, :width], axis=-1, keepdims=True) / gain[...]
    if low.shape[1] > width:
        column = column + total[:, width : width + 1]
    diagonal = lax.broadcasted_iota(jnp.int32, (count, count), 0) == lax.broadcasted_iota(
        jnp.int32, (count, count), 1
    )
    gain_out[...] = jnp.sum(jnp.where(diagonal, column, 0.0), axis=0, keepdims=True)


def finish_call(low, recv, weight, gain):
    count, width = weight.shape

    def kernel(low, *refs):
        finish_kernel(low, refs[: len(recv)], *refs[len(recv) :])

    return pl.pallas_call(
        kernel,
        name="finish_enc" if low.shape[1] > width else "finish_dec",
        out_shape=[jax.ShapeDtypeStruct((count, width), F32), jax.ShapeDtypeStruct((1, count), F32)],
        in_specs=[VMEM] * (3 + len(recv)),
        out_specs=[VMEM] * 2,
        compiler_params=PARAMS,
    )(low, *recv, weight, gain)


def device(pipe, high, deep, across):
    return pipe * 32 + (high % 2) * 16 + (deep % 4) * 4 + across % 4


def all_places():
    return [(pipe, high, deep, across) for pipe in range(4) for high in range(2) for deep in range(4) for across in range(4)]


def moved(place, along_x, step):
    pipe, high, deep, across = place
    return device(pipe, high, deep, across + step) if along_x else device(pipe, high, deep + step, across)


def gather_perm(step):
    return [(device(*place), moved(place, place[0] % 2 == 0, step)) for place in all_places()]


def reduce_perm(step):
    return [(device(*place), moved(place, place[0] % 2 == 1, step)) for place in all_places()]


HALF_PERM = [(device(*place), device(place[0], place[1] + 1, place[2], place[3])) for place in all_places()]
ASIDE_PERM = [(device(*place), device(place[0] ^ 1, place[1], place[2], place[3] + 1)) for place in all_places()]
SWAP_PERM = [(device(*place), device(place[0] ^ 1, *place[1:])) for place in all_places()]
UP_PERM = [
    (device(pipe, high, deep, across), device(pipe + 2, high + pipe, deep, across))
    for pipe, high, deep, across in all_places()
    if pipe < 2
]
DOWN_PERM = [(target, source) for source, target in UP_PERM]
FIRST_PERM = [(device(*place), device(place[0] + 1, *place[1:])) for place in all_places() if place[0] % 2 == 0]
OUT_PERMS = [
    [(device(1, high, deep, across), device(2 + core, high + core, deep, across)) for _, high, deep, across in all_places()[:32]]
    for core in range(2)
]


def send(value, perm):
    return lax.ppermute(value, ("pipe", "dp"), perm)


def gather(mine, other, extra=0):
    other = send(other, SWAP_PERM)
    if extra:
        rows = mine.shape[0] - extra
        whole = jnp.concatenate([mine[:rows], other[:rows], mine[rows:] + other[rows:]], axis=0)
    else:
        whole = jnp.concatenate([mine, other], axis=0)
    return [whole] + [send(whole, gather_perm(step)) for step in (1, 2, 3)]


def per_device(enc_in, dec_in, out_grad, enc_weight, dec_weight, enc_gain, dec_gain, mem_gain):
    pipe = lax.axis_index("pipe")
    spot = lax.axis_index("dp")
    core, upper = pipe % 2, pipe // 2
    high, deep, across = spot // 16, (spot // 4) % 4, spot % 4
    even = core == 0
    near, far = jnp.where(even, across, deep), jnp.where(even, deep, across)
    flags = jnp.stack([core, upper]).astype(jnp.int32)
    width = enc_weight.shape[1]
    mem_gain = mem_gain[None]

    def place_of(step, half):
        group, third = jnp.where(even, (far + step) % 4, near), jnp.where(even, near, (far + step) % 4)
        return ((high + half) % 2 * 16 + group * 4 + third) * (width // 32)

    place = jnp.stack([place_of(step, half) for step in range(4) for half in range(2)]).astype(jnp.int32)

    enc_own, dec_own = enc_weight[0], dec_weight[0]
    gains = jnp.concatenate([enc_gain, dec_gain], axis=0)
    gains_other = send(gains, ASIDE_PERM)
    pair = jnp.where(even, jnp.stack([gains, gains_other]), jnp.stack([gains_other, gains]))
    enc_gains, dec_gains = pair[:, 0], pair[:, 1]

    enc_other = send(enc_own, SWAP_PERM)
    x1 = send(first_call(0, flags, streamed(enc_in), enc_own, enc_gain), FIRST_PERM)
    x2 = first_call(1, flags, x1, enc_own, enc_gain, gains_other)
    received = [send(x2[sequence], OUT_PERMS[sequence]) for sequence in range(2)]
    enc_pair = load_call(None, flags, enc_own, enc_other, x2)
    memory, n_own, n_other, saved = enc_forward_call(flags, enc_in, *received, enc_pair, enc_gains, mem_gain)
    memory_recv = send(memory, DOWN_PERM)
    normed_pieces = gather(n_own, n_other)
    upstream = send(jnp.where(even, out_grad[0], out_grad[1]), UP_PERM)
    dec_other = send(dec_own, SWAP_PERM)
    dec_pair = load_call(0, flags, dec_own, dec_other, memory)
    ahead = dec_query_call(flags, dec_in, dec_pair, dec_gains)

    y2, dec_saved = dec_forward_call(flags, dec_in, memory_recv, ahead, dec_pair, dec_gains)
    dec_pair = load_call(1, flags, dec_own, dec_other, dec_saved)
    u2, source_mine, dec_done = dec_turn_call(flags, send(y2, UP_PERM), memory, upstream, dec_pair, dec_gains)
    dec_pair = load_call(0, flags, dec_own, dec_other, dec_done)
    source_low, dec_own_pay, dec_other_pay = dec_backward_call(
        flags, send(u2, DOWN_PERM), memory_recv, ahead, dec_saved, dec_pair, dec_gains, dec_done
    )
    dec_pieces = gather(dec_own_pay, dec_other_pay)
    enc_pair = load_call(None, flags, enc_own, enc_other, source_low)

    u_low, done0, done1 = enc_backward_first_call(
        flags, source_mine, send(source_low, UP_PERM), mem_gain, enc_pair, enc_gains, saved
    )
    dec_blocks = dec_product_call(place, dec_pieces, dec_own_pay)
    slices = choose_call(place, normed_pieces, u_low)
    own_pay, other_pay = enc_backward_last_call(
        flags, send(u_low, DOWN_PERM), done0, done1, enc_pair, enc_gains, saved, dec_blocks[0], slices
    )

    count = width // 32

    def rows_of(weight, gain):
        start = spot * count
        return (
            lax.dynamic_slice_in_dim(weight, start, count, 0),
            lax.dynamic_slice_in_dim(gain[0], start, count, 0)[:, None],
        )

    dec_sum = (dec_blocks[0].astype(F32) + send(dec_blocks[1], HALF_PERM).astype(F32)).astype(BF16)
    dec_parts = [dec_sum[step * count : (step + 1) * count] for step in range(4)]
    dec_recv = [send(dec_parts[step], reduce_perm(step)) for step in (1, 2, 3)]

    enc_blocks = enc_product_call(place, slices, gather(own_pay, other_pay, EXTRA_ROWS))
    enc_sum = enc_blocks[0].astype(F32)
    for step in (1, 2, 3):
        enc_sum = enc_sum + send(enc_blocks[step], reduce_perm(step)).astype(F32)
    enc_recv = send(enc_sum[count:].astype(BF16), HALF_PERM)

    dec_rows, dec_column = finish_call(dec_parts[0], dec_recv, *rows_of(dec_own, dec_gain))
    enc_rows, enc_column = finish_call(enc_sum[:count], [enc_recv], *rows_of(enc_own, enc_gain))
    return enc_rows[None], dec_rows[None], enc_column, dec_column


def solution(mesh):
    placed = (
        P("dp", None, None),
        P("dp", None, None),
        P("dp", None, None),
        P("pipe", None, None),
        P("pipe", None, None),
        P("pipe", None),
        P("pipe", None),
        P(),
    )
    return jax.shard_map(
        per_device,
        mesh=mesh,
        in_specs=placed,
        out_specs=(P("pipe", "dp", None), P("pipe", "dp", None), P("pipe", "dp"), P("pipe", "dp")),
        check_vma=False,
    )
```

```python
import functools

import jax
import jax.numpy as jnp
from jax import lax
from jax.experimental import pallas as pl
from jax.experimental.pallas import tpu as pltpu
from jax.sharding import PartitionSpec as P

HEAD_DIM = 256
EPSILON = 1e-06
QUERY_SCALE = 0.0625
EXTRA_ROWS = 16
GAIN_LANES = 128

BF16 = jnp.bfloat16
F32 = jnp.float32
def takes(microseconds):
    return pl.CostEstimate(flops=int(microseconds * 10**9), bytes_accessed=0, transcendentals=0)


ANY = pl.BlockSpec(memory_space=pl.ANY)
SMEM = pl.BlockSpec(memory_space=pltpu.SMEM)
VMEM = pl.BlockSpec(memory_space=pltpu.VMEM)
HBM = pl.BlockSpec(memory_space=pltpu.HBM)
PARAMS = pltpu.CompilerParams(vmem_limit_bytes=14 * 2**20)


def dot(left, right):
    return jnp.dot(left, right, preferred_element_type=F32)


def dot_nt(left, right):
    return lax.dot_general(left, right, (((1,), (1,)), ((), ())), preferred_element_type=F32)


def dot_tn(left, right):
    return lax.dot_general(left, right, (((0,), (0,)), ((), ())), preferred_element_type=F32)


def row_scale(values):
    return lax.rsqrt(jnp.mean(values * values, axis=-1, keepdims=True) + EPSILON)


def head(index):
    return slice(index * HEAD_DIM, (index + 1) * HEAD_DIM)


def normal(x, gain):
    hidden = x[...].astype(F32)
    return (hidden * row_scale(hidden) * gain).astype(BF16)


def attend_forward(x, query, source, out):
    heads = [head(part) for part in range(x.shape[-1] // HEAD_DIM)]
    raised = [jnp.exp(dot_nt(query[:, cols], source[:, cols])) for cols in heads]
    low = [(value / jnp.sum(value, axis=-1, keepdims=True)).astype(BF16) for value in raised]
    for cols, shares in zip(heads, low):
        out[:, cols] = (x[:, cols].astype(F32) + dot(shares, source[:, cols])).astype(BF16)


def queries_of(weight, normed, query):
    query[...] = (dot(normed[...], weight[...]) * QUERY_SCALE).astype(BF16)


def attend_backward(source, query, upstream, grad_query, grad_source, add):
    heads = [head(part) for part in range(source.shape[-1] // HEAD_DIM)]
    length = query.shape[0]
    if length % 128 == 0:
        sides = [jnp.concatenate([query[:, cols], upstream[:, cols]], axis=0) for cols in heads]
        both = [dot_nt(source[:, cols], side) for cols, side in zip(heads, sides)]
        raised = [jnp.exp(value[:, :length]) for value in both]
        grads = [value[:, length:] for value in both]
    else:
        raised = [jnp.exp(dot_nt(source[:, cols], query[:, cols])) for cols in heads]
        grads = [dot_nt(source[:, cols], upstream[:, cols]) for cols in heads]
    probs = [value / jnp.sum(value, axis=0, keepdims=True) for value in raised]
    scores = [
        (share * (grad - jnp.sum(grad * share, axis=0, keepdims=True))).astype(BF16) for share, grad in zip(probs, grads)
    ]
    for part, cols in enumerate(heads):
        low = probs[part].astype(BF16)
        grad_query[:, cols] = (dot_tn(scores[part], source[:, cols]) * QUERY_SCALE).astype(BF16)
        if length % 128 == 0:
            total = dot(jnp.concatenate([scores[part], low], axis=1), sides[part])
        else:
            total = dot(scores[part], query[:, cols]) + dot(low, upstream[:, cols])
        grad_source[:, cols] = grad_source[:, cols] + total if add else total


def grad_normed(weight, grad_query, scaled):
    for part in range(grad_query.shape[1] // HEAD_DIM):
        cols = head(part)
        scaled[:, cols] = dot_nt(weight[cols, :], grad_query[...]).T


def input_backward(x, gain, grad_source, upstream, scaled, out):
    hidden = x[...].astype(F32)
    scales = row_scale(hidden)
    grad = scaled[...] if grad_source is None else scaled[...] + grad_source[...]
    grad = gain * grad
    mean = jnp.mean(grad * hidden, axis=-1, keepdims=True)
    factor = scales * scales * scales * mean
    out[...] = (upstream[...].astype(F32) + scales * grad - hidden * factor).astype(BF16)


def dec_input_backward(weight, x, gain, grad_query, upstream, scaled, out):
    grad_normed(weight, grad_query, scaled)
    input_backward(x, gain, None, upstream, scaled, out)


def gain_row(x, grad_source):
    hidden = x[...].astype(F32)
    return jnp.sum(grad_source[...] * hidden * row_scale(hidden), axis=0, keepdims=True)


def by_core(core, low, high, own, other):
    for mine in (0, 1):

        @pl.when(core == mine)
        def _():
            own[...] = high[...] if mine else low[...]
            other[...] = low[...] if mine else high[...]


def load_kernel(role, flags, own, other, *refs):
    pair, sems = refs[-2:]

    def body():
        copies = [pltpu.make_async_copy(part, pair.at[slot], sems.at[slot]) for slot, part in enumerate((own, other))]
        for copy in copies:
            copy.start()
        for copy in copies:
            copy.wait()

    if role is None:
        body()
    else:
        pl.when(flags[1] == role)(body)


def load_call(role, flags, own, other, *gates):
    pair = pl.pallas_call(
        functools.partial(load_kernel, role),
        name="load_weights",
        cost_estimate=takes(4),
        out_shape=pltpu.VMEM((2,) + own.shape, BF16),
        in_specs=[SMEM] + [ANY] * (2 + len(gates)),
        out_specs=VMEM,
        scratch_shapes=[pltpu.SemaphoreType.DMA((2,))],
        compiler_params=PARAMS,
    )(flags, streamed(own), streamed(other), *gates)
    return pinned(pair)


def streamed(value):
    return pltpu.with_memory_space_constraint(value, pltpu.HBM)


def pinned(value):
    return pltpu.with_memory_space_constraint(value, pltpu.VMEM)


def both_sequences(x, normed, query, out):
    count, length, width = x.shape
    for sequence in range(count):
        rows = pl.ds(sequence * length, length)
        attend_forward(x.at[sequence], query.at[rows], normed.at[rows], out.at[sequence])


def both_normal(x, gain, normed):
    count, length, width = x.shape
    for sequence in range(count):
        normed[sequence * length : (sequence + 1) * length] = normal(x.at[sequence], gain[...])


def first_kernel(turn, flags, x_any, weight_any, gain, *refs):
    out, x, weight, normed, query, x_sem, sems = refs[-7:]

    @pl.when(jnp.logical_and(flags[0] == turn, flags[1] == 0))
    def _():
        parts = range(x.shape[-1] // HEAD_DIM)
        rows = pltpu.make_async_copy(x_any, x, x_sem)
        rows.start()
        copies = [
            pltpu.make_async_copy(weight_any.at[:, head(part)], weight.at[:, head(part)], sems.at[part]) for part in parts
        ]
        for copy in copies:
            copy.start()
        rows.wait()
        both_normal(x, gain, normed)
        middle = len(parts) // 2
        for half in (parts[:middle], parts[middle:]):
            for part in half:
                copies[part].wait()
            for part in half:
                query[:, head(part)] = (dot(normed[...], weight[:, head(part)]) * QUERY_SCALE).astype(BF16)
        both_sequences(x, normed, query, out)

def first_call(turn, flags, x, weight, gain, *gates):
    count, length, width = x.shape
    return pl.pallas_call(
        functools.partial(first_kernel, turn),
        name="enc_first_lower" if turn == 0 else "enc_first_upper",
        cost_estimate=takes(6),
        out_shape=jax.ShapeDtypeStruct(x.shape, BF16),
        in_specs=[SMEM, ANY, ANY, VMEM] + [ANY] * len(gates),
        out_specs=VMEM,
        scratch_shapes=[pltpu.VMEM(x.shape, BF16), pltpu.VMEM((width, width), BF16)]
        + [pltpu.VMEM((count * length, width), BF16)] * 2
        + [pltpu.SemaphoreType.DMA, pltpu.SemaphoreType.DMA((width // HEAD_DIM,))],
        compiler_params=PARAMS,
    )(flags, x, streamed(weight), gain, *gates)


def enc_forward_kernel(
    flags, x_any, recv0, recv1, pair, gains, mem_gain, mem, n_own, n_other, saved, sem
):
    core, upper = flags[0], flags[1]
    x0, x1, x2, n0, n1, q0, q1 = [saved.at[place] for place in range(7)]

    @pl.when(upper == 0)
    def _():
        pltpu.make_async_copy(x_any.at[core], x0, sem).start()

    for mine, received in enumerate((recv0, recv1)):

        @pl.when(jnp.logical_and(upper == 1, core == mine))
        def _():
            pltpu.make_async_copy(received, x0, sem).start()

    pltpu.make_async_copy(recv0, x0, sem).wait()
    n0[...] = normal(x0, gains[0:1])
    queries_of(pair.at[core], n0, q0)
    attend_forward(x0, q0, n0, x1)
    n1[...] = normal(x1, gains[1:2])
    queries_of(pair.at[1 - core], n1, q1)
    attend_forward(x1, q1, n1, x2)
    mem[...] = normal(x2, mem_gain[...])
    by_core(core, n0, n1, n_own, n_other)


def enc_forward_call(flags, x, recv0, recv1, pair, gains, mem_gain):
    row = jax.ShapeDtypeStruct(recv0.shape, BF16)
    return pl.pallas_call(
        enc_forward_kernel,
        name="enc_forward",
        cost_estimate=takes(5.3),
        out_shape=[row] * 3 + [jax.ShapeDtypeStruct((7,) + recv0.shape, BF16)],
        in_specs=[SMEM, ANY, ANY, ANY] + [VMEM] * 3,
        out_specs=[VMEM] * 4,
        scratch_shapes=[pltpu.SemaphoreType.DMA],
        compiler_params=PARAMS,
    )(flags, streamed(x), recv0, recv1, pair, gains, mem_gain)


def dec_query_kernel(flags, x_any, pair, gains, ahead, sem, y0):
    core, upper = flags[0], flags[1]
    n0, q0 = ahead.at[0], ahead.at[1]

    @pl.when(upper == 0)
    def _():
        rows = pltpu.make_async_copy(x_any.at[core], y0, sem)
        rows.start()
        rows.wait()
        n0[...] = normal(y0, gains[0:1])
        queries_of(pair.at[core], n0, q0)


def dec_query_call(flags, x, pair, gains):
    return pl.pallas_call(
        dec_query_kernel,
        name="dec_query",
        cost_estimate=takes(2.4),
        out_shape=jax.ShapeDtypeStruct((2,) + x.shape[1:], BF16),
        in_specs=[SMEM, ANY, VMEM, VMEM],
        out_specs=VMEM,
        scratch_shapes=[pltpu.SemaphoreType.DMA, pltpu.VMEM(x.shape[1:], BF16)],
        compiler_params=PARAMS,
    )(flags, x, pair, gains)


def dec_forward_kernel(flags, x_any, memory, ahead, pair, gains, y2, saved, sem, y0):
    core, upper = flags[0], flags[1]
    q0 = ahead.at[1]
    y1, n1, q1 = [saved.at[place] for place in range(3)]

    @pl.when(upper == 0)
    def _():
        rows = pltpu.make_async_copy(x_any.at[core], y0, sem)
        rows.start()
        rows.wait()
        attend_forward(y0, q0, memory, y1)
        n1[...] = normal(y1, gains[1:2])
        queries_of(pair.at[1 - core], n1, q1)
        attend_forward(y1, q1, memory, y2)


def dec_forward_call(flags, x, memory, ahead, pair, gains):
    row = jax.ShapeDtypeStruct(x.shape[1:], BF16)
    return pl.pallas_call(
        dec_forward_kernel,
        name="dec_forward",
        cost_estimate=takes(3.3),
        out_shape=[row, jax.ShapeDtypeStruct((3,) + x.shape[1:], BF16)],
        in_specs=[SMEM, ANY] + [VMEM] * 4,
        out_specs=[VMEM] * 2,
        scratch_shapes=[pltpu.SemaphoreType.DMA, pltpu.VMEM(x.shape[1:], BF16)],
        compiler_params=PARAMS,
    )(flags, x, memory, ahead, pair, gains)


def dec_turn_kernel(
    flags, y2, memory, upstream, pair, gains, out, grad_source, pays, n0, n1, y3, u3, q0, q1, dq0, dq1, scaled
):
    core, upper = flags[0], flags[1]

    @pl.when(upper == 1)
    def _():
        length = y2.shape[0]
        n0[...] = normal(y2, gains[0:1])
        queries_of(pair.at[core], n0, q0)
        attend_forward(y2, q0, memory, y3)
        n1[...] = normal(y3, gains[1:2])
        queries_of(pair.at[1 - core], n1, q1)
        attend_backward(memory, q1, upstream, dq1, grad_source, False)
        dec_input_backward(pair.at[1 - core], y3, gains[1:2], dq1, upstream, scaled, u3)
        attend_backward(memory, q0, u3, dq0, grad_source, True)
        dec_input_backward(pair.at[core], y2, gains[0:1], dq0, u3, scaled, out)
        for payload, normed, grad in ((pays.at[0], n0, dq0), (pays.at[1], n1, dq1)):
            payload[0:length] = normed[...]
            payload[length:] = grad[...]


def dec_turn_call(flags, y2, memory, upstream, pair, gains):
    length, width = y2.shape
    row = jax.ShapeDtypeStruct((length, width), BF16)
    payload = jax.ShapeDtypeStruct((2, 2 * length, width), BF16)
    held = pltpu.VMEM((length, width), BF16)
    return pl.pallas_call(
        dec_turn_kernel,
        name="dec_turn",
        cost_estimate=takes(11),
        out_shape=[row, jax.ShapeDtypeStruct(memory.shape, F32), payload],
        in_specs=[SMEM] + [VMEM] * 5,
        out_specs=[VMEM] * 3,
        scratch_shapes=[held] * 8 + [pltpu.VMEM((length, width), F32)],
        compiler_params=PARAMS,
    )(flags, y2, memory, upstream, pair, gains)


def dec_backward_kernel(
    flags, upstream, memory, ahead, saved, pair, gains, done, source_low, out_own, out_other, u1, dq0, dq1, grad_source, scaled, pay0, pay1
):
    core, upper = flags[0], flags[1]
    n0, q0 = ahead.at[0], ahead.at[1]
    y1, n1, q1 = [saved.at[place] for place in range(3)]

    @pl.when(upper == 0)
    def _():
        length = y1.shape[0]
        attend_backward(memory, q1, upstream, dq1, grad_source, False)
        dec_input_backward(pair.at[1 - core], y1, gains[1:2], dq1, upstream, scaled, u1)
        attend_backward(memory, q0, u1, dq0, grad_source, True)
        source_low[...] = grad_source[...].astype(BF16)
        for payload, normed, grad in ((pay0, n0, dq0), (pay1, n1, dq1)):
            payload[0:length] = normed[...]
            payload[length:] = grad[...]
        by_core(core, pay0, pay1, out_own, out_other)

    @pl.when(upper == 1)
    def _():
        by_core(core, done.at[0], done.at[1], out_own, out_other)


def dec_backward_call(flags, upstream, memory, ahead, saved, pair, gains, done):
    length, width = upstream.shape
    payload = jax.ShapeDtypeStruct((2 * length, width), BF16)
    held = pltpu.VMEM((length, width), BF16)
    return pl.pallas_call(
        dec_backward_kernel,
        name="dec_backward",
        cost_estimate=takes(5.5),
        out_shape=[jax.ShapeDtypeStruct(memory.shape, BF16), payload, payload],
        in_specs=[SMEM] + [VMEM] * 7,
        out_specs=[VMEM] * 3,
        scratch_shapes=[held] * 3
        + [pltpu.VMEM(memory.shape, F32), pltpu.VMEM((length, width), F32)]
        + [pltpu.VMEM(payload.shape, BF16)] * 2,
        compiler_params=PARAMS,
    )(flags, upstream, memory, ahead, saved, pair, gains, done)


def put_payload(core, payload, grad_query, x, grad_source):
    length, width = grad_query.shape
    payload[0:length] = grad_query[...]
    place = lax.broadcasted_iota(jnp.int32, (EXTRA_ROWS, width), 0)
    payload[length:] = jnp.where(place == core, gain_row(x, grad_source), 0.0).astype(BF16)


def enc_backward_first_kernel(
    flags, source_mine, source_recv, mem_gain, pair, gains, saved, out, pay0, pay1, u2, u1, grad_query, grad_source, scaled
):
    x0, x1, x2, n0, n1, q0, q1 = [saved.at[place] for place in range(7)]
    core, upper = flags[0], flags[1]

    @pl.when(upper == 1)
    def _():
        hidden = x2[...].astype(F32)
        scales = row_scale(hidden)
        grad = mem_gain[...] * (source_mine[...] + source_recv[...].astype(F32))
        mean = jnp.mean(grad * hidden, axis=-1, keepdims=True)
        u2[...] = (scales * grad - hidden * (scales * scales * scales * mean)).astype(BF16)
        attend_backward(n1, q1, u2, grad_query, grad_source, False)
        put_payload(core, pay1, grad_query, x1, grad_source)
        grad_normed(pair.at[1 - core], grad_query, scaled)
        input_backward(x1, gains[1:2], grad_source, u2, scaled, u1)
        attend_backward(n0, q0, u1, grad_query, grad_source, False)
        put_payload(core, pay0, grad_query, x0, grad_source)
        grad_normed(pair.at[core], grad_query, scaled)
        input_backward(x0, gains[0:1], grad_source, u1, scaled, out)


def enc_backward_first_call(flags, source_mine, source_recv, mem_gain, pair, gains, saved):
    length, width = saved.shape[1:]
    row = jax.ShapeDtypeStruct((length, width), BF16)
    payload = jax.ShapeDtypeStruct((length + EXTRA_ROWS, width), BF16)
    return pl.pallas_call(
        enc_backward_first_kernel,
        name="enc_backward_first",
        cost_estimate=takes(10),
        out_shape=[row, payload, payload],
        in_specs=[SMEM] + [VMEM] * 3 + [VMEM] * 3,
        out_specs=[VMEM] * 3,
        scratch_shapes=[pltpu.VMEM((length, width), BF16)] * 3
        + [pltpu.VMEM((length, width), F32)] * 2,
        compiler_params=PARAMS,
    )(flags, source_mine, source_recv, mem_gain, pair, gains, saved)


def enc_backward_last_kernel(
    flags, upstream, done0, done1, pair, gains, saved, gate, out_own, out_other, pay0, pay1, u1, grad_query, grad_source, scaled
):
    x0, x1, _, n0, n1, q0, q1 = [saved.at[place] for place in range(7)]
    core, upper = flags[0], flags[1]

    @pl.when(upper == 0)
    def _():
        attend_backward(n1, q1, upstream, grad_query, grad_source, False)
        put_payload(core, pay1, grad_query, x1, grad_source)
        grad_normed(pair.at[1 - core], grad_query, scaled)
        input_backward(x1, gains[1:2], grad_source, upstream, scaled, u1)
        attend_backward(n0, q0, u1, grad_query, grad_source, False)
        put_payload(core, pay0, grad_query, x0, grad_source)
        by_core(core, pay0, pay1, out_own, out_other)

    @pl.when(upper == 1)
    def _():
        by_core(core, done0, done1, out_own, out_other)


def enc_backward_last_call(flags, upstream, done0, done1, pair, gains, saved, *gates):
    length, width = upstream.shape
    payload = jax.ShapeDtypeStruct((length + EXTRA_ROWS, width), BF16)
    return pl.pallas_call(
        enc_backward_last_kernel,
        name="enc_backward_last",
        cost_estimate=takes(7),
        out_shape=[payload, payload],
        in_specs=[SMEM] + [VMEM] * 3 + [VMEM] * 3 + [ANY],
        out_specs=[VMEM] * 2,
        scratch_shapes=[pltpu.VMEM(payload.shape, BF16)] * 2
        + [pltpu.VMEM((length, width), BF16)] * 2
        + [pltpu.VMEM((length, width), F32)] * 2,
        compiler_params=PARAMS,
    )(flags, upstream, done0, done1, pair, gains, saved, *gates)


def features(place, index, block):
    row = lax.broadcasted_iota(jnp.int32, (block, 1), 0)
    half = block // 2
    return jnp.where(row < half, place[index * 2] + row, place[index * 2 + 1] + row - half)


def ones_at(place, index, block, width):
    lanes = lax.broadcasted_iota(jnp.int32, (block, width), 1)
    return jnp.where(lanes == features(place, index, block), 1.0, 0.0).astype(BF16)


def choose_kernel(place, *refs):
    pieces, out, (ones,) = refs[:4], refs[5], refs[6:]
    rows, width = pieces[0].shape
    block = out.shape[0] // 4
    for index in range(4):
        ones[index * block : (index + 1) * block] = ones_at(place, index, block, width)
    for index in range(4):
        out[:, index * rows : (index + 1) * rows] = dot_nt(ones[...], pieces[index][...]).astype(BF16)


def choose_call(place, pieces, gate):
    rows, width = pieces[0].shape
    return pl.pallas_call(
        choose_kernel,
        name="choose_enc",
        cost_estimate=takes(4.3),
        out_shape=jax.ShapeDtypeStruct((width // 4, 4 * rows), BF16),
        in_specs=[SMEM] + [VMEM] * 4 + [ANY],
        out_specs=VMEM,
        scratch_shapes=[pltpu.VMEM((width // 4, width), BF16)],
        compiler_params=PARAMS,
    )(place, *pieces, gate)


def dec_product_kernel(place, *refs):
    pieces, outs, (normed, grads) = refs[:4], refs[5:7], refs[7:]
    length = pieces[0].shape[0] // 4
    for index in range(8):
        start = index % 2 * 2 * length
        normed[index * length : (index + 1) * length] = pieces[index // 2][start : start + length]
        grads[index * length : (index + 1) * length] = pieces[index // 2][start + length : start + 2 * length]
    half = outs[0].shape[0] // 4
    for index in range(4):
        columns = dot_nt(ones_at(place, index, 2 * half, normed.shape[1]), normed[...]).astype(BF16)
        product = dot(columns, grads[...]).astype(BF16)
        for side in range(2):
            outs[side][index * half : (index + 1) * half] = product[side * half : (side + 1) * half]


def dec_product_call(place, pieces, gate):
    rows, width = pieces[0].shape
    return pl.pallas_call(
        dec_product_kernel,
        name="product_dec",
        cost_estimate=takes(4.4),
        out_shape=[jax.ShapeDtypeStruct((width // 8, width), BF16)] * 2,
        in_specs=[SMEM] + [VMEM] * 4 + [ANY],
        out_specs=[VMEM] * 2,
        scratch_shapes=[pltpu.VMEM((2 * rows, width), BF16)] * 2,
        compiler_params=PARAMS,
    )(place, *pieces, gate)


def enc_product_kernel(place, slices_any, *refs):
    pieces, outs, (slices, sem) = refs[:4], refs[4:8], refs[8:]
    copy = pltpu.make_async_copy(slices_any, slices, sem)
    copy.start()
    length, width = slices.shape[1] // 8, pieces[0].shape[1]
    block = slices.shape[0] // 4
    extra = jnp.zeros((EXTRA_ROWS, width), F32)
    for index in range(4):
        extra = extra + pieces[index][2 * length :].astype(F32)
    extra = jnp.sum(extra, axis=0, keepdims=True)
    copy.wait()
    for index in range(4):
        rows = slice(index * block, (index + 1) * block)
        total = dot(slices[rows, 0 : 2 * length], pieces[0][0 : 2 * length])
        for place_of_piece in range(1, 4):
            depth = slice(2 * place_of_piece * length, 2 * (place_of_piece + 1) * length)
            total = total + dot(slices[rows, depth], pieces[place_of_piece][0 : 2 * length])
        outs[index][:, 0:width] = total.astype(BF16)
        lanes = lax.broadcasted_iota(jnp.int32, (block, width), 1)
        column = jnp.sum(jnp.where(lanes == features(place, index, block), extra, 0.0), axis=-1, keepdims=True)
        outs[index][:, width:] = jnp.broadcast_to(column, (block, GAIN_LANES)).astype(BF16)


def enc_product_call(place, slices, pieces):
    width = pieces[0].shape[1]
    return pl.pallas_call(
        enc_product_kernel,
        name="product_enc",
        cost_estimate=takes(3.5),
        out_shape=[jax.ShapeDtypeStruct((slices.shape[0] // 4, width + GAIN_LANES), BF16)] * 4,
        in_specs=[SMEM, ANY] + [VMEM] * 4,
        out_specs=[VMEM] * 4,
        scratch_shapes=[pltpu.VMEM(slices.shape, BF16), pltpu.SemaphoreType.DMA],
        compiler_params=PARAMS,
    )(place, streamed(slices), *pieces)


def finish_kernel(low, recv, weight, gain, rows, gain_out):
    count, width = weight.shape
    total = low[...].astype(F32)
    for part in recv:
        total = total + part[...].astype(F32)
    rows[...] = total[:, :width]
    column = jnp.sum(weight[...].astype(F32) * total[:, :width], axis=-1, keepdims=True) / gain[...]
    if low.shape[1] > width:
        column = column + total[:, width : width + 1]
    diagonal = lax.broadcasted_iota(jnp.int32, (count, count), 0) == lax.broadcasted_iota(
        jnp.int32, (count, count), 1
    )
    gain_out[...] = jnp.sum(jnp.where(diagonal, column, 0.0), axis=0, keepdims=True)


def finish_call(low, recv, weight, gain):
    count, width = weight.shape

    def kernel(low, *refs):
        finish_kernel(low, refs[: len(recv)], *refs[len(recv) :])

    return pl.pallas_call(
        kernel,
        name="finish_enc" if low.shape[1] > width else "finish_dec",
        out_shape=[jax.ShapeDtypeStruct((count, width), F32), jax.ShapeDtypeStruct((1, count), F32)],
        in_specs=[VMEM] * (3 + len(recv)),
        out_specs=[VMEM] * 2,
        compiler_params=PARAMS,
    )(low, *recv, weight, gain)


def device(pipe, high, deep, across):
    return pipe * 32 + (high % 2) * 16 + (deep % 4) * 4 + across % 4


def all_places():
    return [(pipe, high, deep, across) for pipe in range(4) for high in range(2) for deep in range(4) for across in range(4)]


def moved(place, along_x, step):
    pipe, high, deep, across = place
    return device(pipe, high, deep, across + step) if along_x else device(pipe, high, deep + step, across)


def gather_perm(step):
    return [(device(*place), moved(place, place[0] % 2 == 0, step)) for place in all_places()]


def reduce_perm(step):
    return [(device(*place), moved(place, place[0] % 2 == 1, step)) for place in all_places()]


HALF_PERM = [(device(*place), device(place[0], place[1] + 1, place[2], place[3])) for place in all_places()]
ASIDE_PERM = [(device(*place), device(place[0] ^ 1, place[1], place[2], place[3] + 1)) for place in all_places()]
SWAP_PERM = [(device(*place), device(place[0] ^ 1, *place[1:])) for place in all_places()]
UP_PERM = [
    (device(pipe, high, deep, across), device(pipe + 2, high + pipe, deep, across))
    for pipe, high, deep, across in all_places()
    if pipe < 2
]
DOWN_PERM = [(target, source) for source, target in UP_PERM]
FIRST_PERM = [(device(*place), device(place[0] + 1, *place[1:])) for place in all_places() if place[0] % 2 == 0]
OUT_PERMS = [
    [(device(1, high, deep, across), device(2 + core, high + core, deep, across)) for _, high, deep, across in all_places()[:32]]
    for core in range(2)
]


def send(value, perm):
    return lax.ppermute(value, ("pipe", "dp"), perm)


def gather(mine, other, extra=0):
    other = send(other, SWAP_PERM)
    if extra:
        rows = mine.shape[0] - extra
        whole = jnp.concatenate([mine[:rows], other[:rows], mine[rows:] + other[rows:]], axis=0)
    else:
        whole = jnp.concatenate([mine, other], axis=0)
    return [whole] + [send(whole, gather_perm(step)) for step in (1, 2, 3)]


def per_device(enc_in, dec_in, out_grad, enc_weight, dec_weight, enc_gain, dec_gain, mem_gain):
    pipe = lax.axis_index("pipe")
    spot = lax.axis_index("dp")
    core, upper = pipe % 2, pipe // 2
    high, deep, across = spot // 16, (spot // 4) % 4, spot % 4
    even = core == 0
    near, far = jnp.where(even, across, deep), jnp.where(even, deep, across)
    flags = jnp.stack([core, upper]).astype(jnp.int32)
    width = enc_weight.shape[1]
    mem_gain = mem_gain[None]

    def place_of(step, half):
        group, third = jnp.where(even, (far + step) % 4, near), jnp.where(even, near, (far + step) % 4)
        return ((high + half) % 2 * 16 + group * 4 + third) * (width // 32)

    place = jnp.stack([place_of(step, half) for step in range(4) for half in range(2)]).astype(jnp.int32)

    enc_own, dec_own = enc_weight[0], dec_weight[0]
    gains = jnp.concatenate([enc_gain, dec_gain], axis=0)
    gains_other = send(gains, ASIDE_PERM)
    pair = jnp.where(even, jnp.stack([gains, gains_other]), jnp.stack([gains_other, gains]))
    enc_gains, dec_gains = pair[:, 0], pair[:, 1]

    enc_other = send(enc_own, SWAP_PERM)
    x1 = send(first_call(0, flags, streamed(enc_in), enc_own, enc_gain), FIRST_PERM)
    x2 = first_call(1, flags, x1, enc_own, enc_gain, gains_other)
    received = [send(x2[sequence], OUT_PERMS[sequence]) for sequence in range(2)]
    enc_pair = load_call(None, flags, enc_own, enc_other, x2)
    memory, n_own, n_other, saved = enc_forward_call(flags, enc_in, *received, enc_pair, enc_gains, mem_gain)
    memory_recv = send(memory, DOWN_PERM)
    normed_pieces = gather(n_own, n_other)
    upstream = send(jnp.where(even, out_grad[0], out_grad[1]), UP_PERM)
    dec_other = send(dec_own, SWAP_PERM)
    dec_pair = load_call(0, flags, dec_own, dec_other, memory)
    ahead = dec_query_call(flags, dec_in, dec_pair, dec_gains)

    y2, dec_saved = dec_forward_call(flags, dec_in, memory_recv, ahead, dec_pair, dec_gains)
    dec_pair = load_call(1, flags, dec_own, dec_other, dec_saved)
    u2, source_mine, dec_done = dec_turn_call(flags, send(y2, UP_PERM), memory, upstream, dec_pair, dec_gains)
    dec_pair = load_call(0, flags, dec_own, dec_other, dec_done)
    source_low, dec_own_pay, dec_other_pay = dec_backward_call(
        flags, send(u2, DOWN_PERM), memory_recv, ahead, dec_saved, dec_pair, dec_gains, dec_done
    )
    dec_pieces = gather(dec_own_pay, dec_other_pay)
    slices = choose_call(place, [streamed(piece) for piece in normed_pieces], dec_other_pay)
    enc_pair = load_call(1, flags, enc_own, enc_other, slices)

    u_low, done0, done1 = enc_backward_first_call(
        flags, source_mine, send(source_low, UP_PERM), mem_gain, enc_pair, enc_gains, saved
    )
    dec_blocks = dec_product_call(place, dec_pieces, dec_own_pay)
    enc_pair = load_call(0, flags, enc_own, enc_other, u_low)
    own_pay, other_pay = enc_backward_last_call(
        flags, send(u_low, DOWN_PERM), done0, done1, enc_pair, enc_gains, saved, dec_blocks[0]
    )

    count = width // 32

    def rows_of(weight, gain):
        start = spot * count
        return (
            lax.dynamic_slice_in_dim(weight, start, count, 0),
            lax.dynamic_slice_in_dim(gain[0], start, count, 0)[:, None],
        )

    dec_sum = (dec_blocks[0].astype(F32) + send(dec_blocks[1], HALF_PERM).astype(F32)).astype(BF16)
    dec_parts = [dec_sum[step * count : (step + 1) * count] for step in range(4)]
    dec_recv = [send(dec_parts[step], reduce_perm(step)) for step in (1, 2, 3)]

    enc_blocks = enc_product_call(place, slices, gather(own_pay, other_pay, EXTRA_ROWS))
    enc_sum = enc_blocks[0].astype(F32)
    for step in (1, 2, 3):
        enc_sum = enc_sum + send(enc_blocks[step], reduce_perm(step)).astype(F32)
    enc_recv = send(enc_sum[count:].astype(BF16), HALF_PERM)

    dec_rows, dec_column = finish_call(dec_parts[0], dec_recv, *rows_of(dec_own, dec_gain))
    enc_rows, enc_column = finish_call(enc_sum[:count], [enc_recv], *rows_of(enc_own, enc_gain))
    return enc_rows[None], dec_rows[None], enc_column, dec_column


def solution(mesh):
    placed = (
        P("dp", None, None),
        P("dp", None, None),
        P("dp", None, None),
        P("pipe", None, None),
        P("pipe", None, None),
        P("pipe", None),
        P("pipe", None),
        P(),
    )
    return jax.shard_map(
        per_device,
        mesh=mesh,
        in_specs=placed,
        out_specs=(P("pipe", "dp", None), P("pipe", "dp", None), P("pipe", "dp"), P("pipe", "dp")),
        check_vma=False,
    )
```

```python
import functools

import jax
import jax.numpy as jnp
from jax import lax
from jax.experimental import pallas as pl
from jax.experimental.pallas import tpu as pltpu
from jax.sharding import PartitionSpec as P

HEAD_DIM = 256
EPSILON = 1e-06
QUERY_SCALE = 0.0625
EXTRA_ROWS = 16
GAIN_LANES = 128

BF16 = jnp.bfloat16
F32 = jnp.float32
def takes(microseconds):
    return pl.CostEstimate(flops=int(microseconds * 10**9), bytes_accessed=0, transcendentals=0)


ANY = pl.BlockSpec(memory_space=pl.ANY)
SMEM = pl.BlockSpec(memory_space=pltpu.SMEM)
VMEM = pl.BlockSpec(memory_space=pltpu.VMEM)
HBM = pl.BlockSpec(memory_space=pltpu.HBM)
PARAMS = pltpu.CompilerParams(vmem_limit_bytes=14 * 2**20)


def dot(left, right):
    return jnp.dot(left, right, preferred_element_type=F32)


def dot_nt(left, right):
    return lax.dot_general(left, right, (((1,), (1,)), ((), ())), preferred_element_type=F32)


def dot_tn(left, right):
    return lax.dot_general(left, right, (((0,), (0,)), ((), ())), preferred_element_type=F32)


def row_scale(values):
    return lax.rsqrt(jnp.mean(values * values, axis=-1, keepdims=True) + EPSILON)


def head(index):
    return slice(index * HEAD_DIM, (index + 1) * HEAD_DIM)


def normal(x, gain):
    hidden = x[...].astype(F32)
    return (hidden * row_scale(hidden) * gain).astype(BF16)


def attend_forward(x, query, source, out):
    heads = [head(part) for part in range(x.shape[-1] // HEAD_DIM)]
    raised = [jnp.exp(dot_nt(query[:, cols], source[:, cols])) for cols in heads]
    low = [(value / jnp.sum(value, axis=-1, keepdims=True)).astype(BF16) for value in raised]
    for cols, shares in zip(heads, low):
        out[:, cols] = (x[:, cols].astype(F32) + dot(shares, source[:, cols])).astype(BF16)


def queries_of(weight, normed, query):
    query[...] = (dot(normed[...], weight[...]) * QUERY_SCALE).astype(BF16)


def attend_backward(source, query, upstream, grad_query, grad_source, add):
    heads = [head(part) for part in range(source.shape[-1] // HEAD_DIM)]
    length = query.shape[0]
    if length % 128 == 0:
        sides = [jnp.concatenate([query[:, cols], upstream[:, cols]], axis=0) for cols in heads]
        both = [dot_nt(source[:, cols], side) for cols, side in zip(heads, sides)]
        raised = [jnp.exp(value[:, :length]) for value in both]
        grads = [value[:, length:] for value in both]
    else:
        raised = [jnp.exp(dot_nt(source[:, cols], query[:, cols])) for cols in heads]
        grads = [dot_nt(source[:, cols], upstream[:, cols]) for cols in heads]
    probs = [value / jnp.sum(value, axis=0, keepdims=True) for value in raised]
    scores = [
        (share * (grad - jnp.sum(grad * share, axis=0, keepdims=True))).astype(BF16) for share, grad in zip(probs, grads)
    ]
    for part, cols in enumerate(heads):
        low = probs[part].astype(BF16)
        grad_query[:, cols] = (dot_tn(scores[part], source[:, cols]) * QUERY_SCALE).astype(BF16)
        if length % 128 == 0:
            total = dot(jnp.concatenate([scores[part], low], axis=1), sides[part])
        else:
            total = dot(scores[part], query[:, cols]) + dot(low, upstream[:, cols])
        grad_source[:, cols] = grad_source[:, cols] + total if add else total


def grad_normed(weight, grad_query, scaled):
    for part in range(grad_query.shape[1] // HEAD_DIM):
        cols = head(part)
        scaled[:, cols] = dot_nt(weight[cols, :], grad_query[...]).T


def input_backward(x, gain, grad_source, upstream, scaled, out):
    hidden = x[...].astype(F32)
    scales = row_scale(hidden)
    grad = scaled[...] if grad_source is None else scaled[...] + grad_source[...]
    grad = gain * grad
    mean = jnp.mean(grad * hidden, axis=-1, keepdims=True)
    factor = scales * scales * scales * mean
    out[...] = (upstream[...].astype(F32) + scales * grad - hidden * factor).astype(BF16)


def dec_input_backward(weight, x, gain, grad_query, upstream, scaled, out):
    grad_normed(weight, grad_query, scaled)
    input_backward(x, gain, None, upstream, scaled, out)


def gain_row(x, grad_source):
    hidden = x[...].astype(F32)
    return jnp.sum(grad_source[...] * hidden * row_scale(hidden), axis=0, keepdims=True)


def by_core(core, low, high, own, other):
    for mine in (0, 1):

        @pl.when(core == mine)
        def _():
            own[...] = high[...] if mine else low[...]
            other[...] = low[...] if mine else high[...]


def load_kernel(role, flags, own, other, gate, pair, sems):
    def body():
        copies = [pltpu.make_async_copy(part, pair.at[slot], sems.at[slot]) for slot, part in enumerate((own, other))]
        for copy in copies:
            copy.start()
        for copy in copies:
            copy.wait()

    if role is None:
        body()
    else:
        pl.when(flags[1] == role)(body)


def load_call(role, flags, own, other, gate):
    pair = pl.pallas_call(
        functools.partial(load_kernel, role),
        name="load_weights",
        cost_estimate=takes(4),
        out_shape=pltpu.VMEM((2,) + own.shape, BF16),
        in_specs=[SMEM] + [ANY] * 3,
        out_specs=VMEM,
        scratch_shapes=[pltpu.SemaphoreType.DMA((2,))],
        compiler_params=PARAMS,
    )(flags, streamed(own), streamed(other), gate)
    return pinned(pair)


def streamed(value):
    return pltpu.with_memory_space_constraint(value, pltpu.HBM)


def pinned(value):
    return pltpu.with_memory_space_constraint(value, pltpu.VMEM)


def both_sequences(x, normed, query, out):
    count, length, width = x.shape
    for sequence in range(count):
        rows = pl.ds(sequence * length, length)
        attend_forward(x.at[sequence], query.at[rows], normed.at[rows], out.at[sequence])


def both_normal(x, gain, normed):
    count, length, width = x.shape
    for sequence in range(count):
        normed[sequence * length : (sequence + 1) * length] = normal(x.at[sequence], gain[...])


def first_kernel(turn, flags, x_any, weight_any, gain, *refs):
    out, x, weight, normed, query, x_sem, sems = refs[-7:]

    @pl.when(jnp.logical_and(flags[0] == turn, flags[1] == 0))
    def _():
        parts = range(x.shape[-1] // HEAD_DIM)
        rows = pltpu.make_async_copy(x_any, x, x_sem)
        rows.start()
        copies = [
            pltpu.make_async_copy(weight_any.at[:, head(part)], weight.at[:, head(part)], sems.at[part]) for part in parts
        ]
        for copy in copies:
            copy.start()
        rows.wait()
        both_normal(x, gain, normed)
        middle = len(parts) // 2
        for half in (parts[:middle], parts[middle:]):
            for part in half:
                copies[part].wait()
            for part in half:
                query[:, head(part)] = (dot(normed[...], weight[:, head(part)]) * QUERY_SCALE).astype(BF16)
        both_sequences(x, normed, query, out)

def first_call(turn, flags, x, weight, gain, *gates):
    count, length, width = x.shape
    return pl.pallas_call(
        functools.partial(first_kernel, turn),
        name="enc_first_lower" if turn == 0 else "enc_first_upper",
        cost_estimate=takes(6),
        out_shape=jax.ShapeDtypeStruct(x.shape, BF16),
        in_specs=[SMEM, ANY, ANY, VMEM] + [ANY] * len(gates),
        out_specs=VMEM,
        scratch_shapes=[pltpu.VMEM(x.shape, BF16), pltpu.VMEM((width, width), BF16)]
        + [pltpu.VMEM((count * length, width), BF16)] * 2
        + [pltpu.SemaphoreType.DMA, pltpu.SemaphoreType.DMA((width // HEAD_DIM,))],
        compiler_params=PARAMS,
    )(flags, x, streamed(weight), gain, *gates)


def enc_forward_kernel(
    flags, x_any, recv0, recv1, pair, gains, mem_gain, mem, n_own, n_other, saved, sem
):
    core, upper = flags[0], flags[1]
    x0, x1, x2, n0, n1, q0, q1 = [saved.at[place] for place in range(7)]

    @pl.when(upper == 0)
    def _():
        pltpu.make_async_copy(x_any.at[core], x0, sem).start()

    for mine, received in enumerate((recv0, recv1)):

        @pl.when(jnp.logical_and(upper == 1, core == mine))
        def _():
            pltpu.make_async_copy(received, x0, sem).start()

    pltpu.make_async_copy(recv0, x0, sem).wait()
    n0[...] = normal(x0, gains[0:1])
    queries_of(pair.at[core], n0, q0)
    attend_forward(x0, q0, n0, x1)
    n1[...] = normal(x1, gains[1:2])
    queries_of(pair.at[1 - core], n1, q1)
    attend_forward(x1, q1, n1, x2)
    mem[...] = normal(x2, mem_gain[...])
    by_core(core, n0, n1, n_own, n_other)


def enc_forward_call(flags, x, recv0, recv1, pair, gains, mem_gain):
    row = jax.ShapeDtypeStruct(recv0.shape, BF16)
    return pl.pallas_call(
        enc_forward_kernel,
        name="enc_forward",
        cost_estimate=takes(5.3),
        out_shape=[row] * 3 + [jax.ShapeDtypeStruct((7,) + recv0.shape, BF16)],
        in_specs=[SMEM, ANY, ANY, ANY] + [VMEM] * 3,
        out_specs=[VMEM] * 4,
        scratch_shapes=[pltpu.SemaphoreType.DMA],
        compiler_params=PARAMS,
    )(flags, streamed(x), recv0, recv1, pair, gains, mem_gain)


def dec_query_kernel(flags, x_any, pair, gains, ahead, sem, y0):
    core, upper = flags[0], flags[1]
    n0, q0 = ahead.at[0], ahead.at[1]

    @pl.when(upper == 0)
    def _():
        rows = pltpu.make_async_copy(x_any.at[core], y0, sem)
        rows.start()
        rows.wait()
        n0[...] = normal(y0, gains[0:1])
        queries_of(pair.at[core], n0, q0)


def dec_query_call(flags, x, pair, gains):
    return pl.pallas_call(
        dec_query_kernel,
        name="dec_query",
        cost_estimate=takes(2.4),
        out_shape=jax.ShapeDtypeStruct((2,) + x.shape[1:], BF16),
        in_specs=[SMEM, ANY, VMEM, VMEM],
        out_specs=VMEM,
        scratch_shapes=[pltpu.SemaphoreType.DMA, pltpu.VMEM(x.shape[1:], BF16)],
        compiler_params=PARAMS,
    )(flags, x, pair, gains)


def dec_forward_kernel(flags, x_any, memory, ahead, pair, gains, y2, saved, sem, y0):
    core, upper = flags[0], flags[1]
    q0 = ahead.at[1]
    y1, n1, q1 = [saved.at[place] for place in range(3)]

    @pl.when(upper == 0)
    def _():
        rows = pltpu.make_async_copy(x_any.at[core], y0, sem)
        rows.start()
        rows.wait()
        attend_forward(y0, q0, memory, y1)
        n1[...] = normal(y1, gains[1:2])
        queries_of(pair.at[1 - core], n1, q1)
        attend_forward(y1, q1, memory, y2)


def dec_forward_call(flags, x, memory, ahead, pair, gains):
    row = jax.ShapeDtypeStruct(x.shape[1:], BF16)
    return pl.pallas_call(
        dec_forward_kernel,
        name="dec_forward",
        cost_estimate=takes(3.3),
        out_shape=[row, jax.ShapeDtypeStruct((3,) + x.shape[1:], BF16)],
        in_specs=[SMEM, ANY] + [VMEM] * 4,
        out_specs=[VMEM] * 2,
        scratch_shapes=[pltpu.SemaphoreType.DMA, pltpu.VMEM(x.shape[1:], BF16)],
        compiler_params=PARAMS,
    )(flags, x, memory, ahead, pair, gains)


def dec_turn_kernel(
    flags, y2, memory, upstream, pair, gains, out, grad_source, pays, n0, n1, y3, u3, q0, q1, dq0, dq1, scaled
):
    core, upper = flags[0], flags[1]

    @pl.when(upper == 1)
    def _():
        length = y2.shape[0]
        n0[...] = normal(y2, gains[0:1])
        queries_of(pair.at[core], n0, q0)
        attend_forward(y2, q0, memory, y3)
        n1[...] = normal(y3, gains[1:2])
        queries_of(pair.at[1 - core], n1, q1)
        attend_backward(memory, q1, upstream, dq1, grad_source, False)
        dec_input_backward(pair.at[1 - core], y3, gains[1:2], dq1, upstream, scaled, u3)
        attend_backward(memory, q0, u3, dq0, grad_source, True)
        dec_input_backward(pair.at[core], y2, gains[0:1], dq0, u3, scaled, out)
        for payload, normed, grad in ((pays.at[0], n0, dq0), (pays.at[1], n1, dq1)):
            payload[0:length] = normed[...]
            payload[length:] = grad[...]


def dec_turn_call(flags, y2, memory, upstream, pair, gains):
    length, width = y2.shape
    row = jax.ShapeDtypeStruct((length, width), BF16)
    payload = jax.ShapeDtypeStruct((2, 2 * length, width), BF16)
    held = pltpu.VMEM((length, width), BF16)
    return pl.pallas_call(
        dec_turn_kernel,
        name="dec_turn",
        cost_estimate=takes(11),
        out_shape=[row, jax.ShapeDtypeStruct(memory.shape, F32), payload],
        in_specs=[SMEM] + [VMEM] * 5,
        out_specs=[VMEM] * 3,
        scratch_shapes=[held] * 8 + [pltpu.VMEM((length, width), F32)],
        compiler_params=PARAMS,
    )(flags, y2, memory, upstream, pair, gains)


def dec_backward_kernel(
    flags, upstream, memory, ahead, saved, pair, gains, done, source_low, out_own, out_other, u1, dq0, dq1, grad_source, scaled, pay0, pay1
):
    core, upper = flags[0], flags[1]
    n0, q0 = ahead.at[0], ahead.at[1]
    y1, n1, q1 = [saved.at[place] for place in range(3)]

    @pl.when(upper == 0)
    def _():
        length = y1.shape[0]
        attend_backward(memory, q1, upstream, dq1, grad_source, False)
        dec_input_backward(pair.at[1 - core], y1, gains[1:2], dq1, upstream, scaled, u1)
        attend_backward(memory, q0, u1, dq0, grad_source, True)
        source_low[...] = grad_source[...].astype(BF16)
        for payload, normed, grad in ((pay0, n0, dq0), (pay1, n1, dq1)):
            payload[0:length] = normed[...]
            payload[length:] = grad[...]
        by_core(core, pay0, pay1, out_own, out_other)

    @pl.when(upper == 1)
    def _():
        by_core(core, done.at[0], done.at[1], out_own, out_other)


def dec_backward_call(flags, upstream, memory, ahead, saved, pair, gains, done):
    length, width = upstream.shape
    payload = jax.ShapeDtypeStruct((2 * length, width), BF16)
    held = pltpu.VMEM((length, width), BF16)
    return pl.pallas_call(
        dec_backward_kernel,
        name="dec_backward",
        cost_estimate=takes(5.5),
        out_shape=[jax.ShapeDtypeStruct(memory.shape, BF16), payload, payload],
        in_specs=[SMEM] + [VMEM] * 7,
        out_specs=[VMEM] * 3,
        scratch_shapes=[held] * 3
        + [pltpu.VMEM(memory.shape, F32), pltpu.VMEM((length, width), F32)]
        + [pltpu.VMEM(payload.shape, BF16)] * 2,
        compiler_params=PARAMS,
    )(flags, upstream, memory, ahead, saved, pair, gains, done)


def put_payload(core, payload, grad_query, x, grad_source):
    length, width = grad_query.shape
    payload[0:length] = grad_query[...]
    place = lax.broadcasted_iota(jnp.int32, (EXTRA_ROWS, width), 0)
    payload[length:] = jnp.where(place == core, gain_row(x, grad_source), 0.0).astype(BF16)


def enc_backward_first_kernel(
    flags, source_mine, source_recv, mem_gain, pair, gains, saved, out, pay0, pay1, u2, u1, grad_query, grad_source, scaled
):
    x0, x1, x2, n0, n1, q0, q1 = [saved.at[place] for place in range(7)]
    core, upper = flags[0], flags[1]

    @pl.when(upper == 1)
    def _():
        hidden = x2[...].astype(F32)
        scales = row_scale(hidden)
        grad = mem_gain[...] * (source_mine[...] + source_recv[...].astype(F32))
        mean = jnp.mean(grad * hidden, axis=-1, keepdims=True)
        u2[...] = (scales * grad - hidden * (scales * scales * scales * mean)).astype(BF16)
        attend_backward(n1, q1, u2, grad_query, grad_source, False)
        put_payload(core, pay1, grad_query, x1, grad_source)
        grad_normed(pair.at[1 - core], grad_query, scaled)
        input_backward(x1, gains[1:2], grad_source, u2, scaled, u1)
        attend_backward(n0, q0, u1, grad_query, grad_source, False)
        put_payload(core, pay0, grad_query, x0, grad_source)
        grad_normed(pair.at[core], grad_query, scaled)
        input_backward(x0, gains[0:1], grad_source, u1, scaled, out)


def enc_backward_first_call(flags, source_mine, source_recv, mem_gain, pair, gains, saved):
    length, width = saved.shape[1:]
    row = jax.ShapeDtypeStruct((length, width), BF16)
    payload = jax.ShapeDtypeStruct((length + EXTRA_ROWS, width), BF16)
    return pl.pallas_call(
        enc_backward_first_kernel,
        name="enc_backward_first",
        cost_estimate=takes(10),
        out_shape=[row, payload, payload],
        in_specs=[SMEM] + [VMEM] * 3 + [VMEM] * 3,
        out_specs=[VMEM] * 3,
        scratch_shapes=[pltpu.VMEM((length, width), BF16)] * 3
        + [pltpu.VMEM((length, width), F32)] * 2,
        compiler_params=PARAMS,
    )(flags, source_mine, source_recv, mem_gain, pair, gains, saved)


def enc_backward_last_kernel(
    flags, upstream, done0, done1, pair, gains, saved, gate, later_gate, out_own, out_other, pay0, pay1, u1, grad_query, grad_source, scaled
):
    x0, x1, _, n0, n1, q0, q1 = [saved.at[place] for place in range(7)]
    core, upper = flags[0], flags[1]

    @pl.when(upper == 0)
    def _():
        attend_backward(n1, q1, upstream, grad_query, grad_source, False)
        put_payload(core, pay1, grad_query, x1, grad_source)
        grad_normed(pair.at[1 - core], grad_query, scaled)
        input_backward(x1, gains[1:2], grad_source, upstream, scaled, u1)
        attend_backward(n0, q0, u1, grad_query, grad_source, False)
        put_payload(core, pay0, grad_query, x0, grad_source)
        by_core(core, pay0, pay1, out_own, out_other)

    @pl.when(upper == 1)
    def _():
        by_core(core, done0, done1, out_own, out_other)


def enc_backward_last_call(flags, upstream, done0, done1, pair, gains, saved, *gates):
    length, width = upstream.shape
    payload = jax.ShapeDtypeStruct((length + EXTRA_ROWS, width), BF16)
    return pl.pallas_call(
        enc_backward_last_kernel,
        name="enc_backward_last",
        cost_estimate=takes(7),
        out_shape=[payload, payload],
        in_specs=[SMEM] + [VMEM] * 3 + [VMEM] * 3 + [ANY] * 2,
        out_specs=[VMEM] * 2,
        scratch_shapes=[pltpu.VMEM(payload.shape, BF16)] * 2
        + [pltpu.VMEM((length, width), BF16)] * 2
        + [pltpu.VMEM((length, width), F32)] * 2,
        compiler_params=PARAMS,
    )(flags, upstream, done0, done1, pair, gains, saved, *gates)


def features(place, index, block):
    row = lax.broadcasted_iota(jnp.int32, (block, 1), 0)
    half = block // 2
    return jnp.where(row < half, place[index * 2] + row, place[index * 2 + 1] + row - half)


def ones_at(place, index, block, width):
    lanes = lax.broadcasted_iota(jnp.int32, (block, width), 1)
    return jnp.where(lanes == features(place, index, block), 1.0, 0.0).astype(BF16)


def choose_kernel(place, *refs):
    pieces, out, (ones,) = refs[:4], refs[5], refs[6:]
    rows, width = pieces[0].shape
    block = out.shape[0] // 4
    for index in range(4):
        ones[index * block : (index + 1) * block] = ones_at(place, index, block, width)
    for index in range(4):
        out[:, index * rows : (index + 1) * rows] = dot_nt(ones[...], pieces[index][...]).astype(BF16)


def choose_call(place, pieces, gate):
    rows, width = pieces[0].shape
    return pl.pallas_call(
        choose_kernel,
        name="choose_enc",
        cost_estimate=takes(4.3),
        out_shape=jax.ShapeDtypeStruct((width // 4, 4 * rows), BF16),
        in_specs=[SMEM] + [VMEM] * 4 + [ANY],
        out_specs=VMEM,
        scratch_shapes=[pltpu.VMEM((width // 4, width), BF16)],
        compiler_params=PARAMS,
    )(place, *pieces, gate)


def dec_product_kernel(place, *refs):
    pieces, outs, (normed, grads) = refs[:4], refs[5:7], refs[7:]
    length = pieces[0].shape[0] // 4
    for index in range(8):
        start = index % 2 * 2 * length
        normed[index * length : (index + 1) * length] = pieces[index // 2][start : start + length]
        grads[index * length : (index + 1) * length] = pieces[index // 2][start + length : start + 2 * length]
    half = outs[0].shape[0] // 4
    for index in range(4):
        columns = dot_nt(ones_at(place, index, 2 * half, normed.shape[1]), normed[...]).astype(BF16)
        product = dot(columns, grads[...]).astype(BF16)
        for side in range(2):
            outs[side][index * half : (index + 1) * half] = product[side * half : (side + 1) * half]


def dec_product_call(place, pieces, gate):
    rows, width = pieces[0].shape
    return pl.pallas_call(
        dec_product_kernel,
        name="product_dec",
        cost_estimate=takes(4.4),
        out_shape=[jax.ShapeDtypeStruct((width // 8, width), BF16)] * 2,
        in_specs=[SMEM] + [VMEM] * 4 + [ANY],
        out_specs=[VMEM] * 2,
        scratch_shapes=[pltpu.VMEM((2 * rows, width), BF16)] * 2,
        compiler_params=PARAMS,
    )(place, *pieces, gate)


def enc_product_kernel(place, slices_any, *refs):
    pieces, outs, (held, slices, sem) = refs[:4], refs[4:8], refs[8:]
    copy = pltpu.make_async_copy(slices_any, slices, sem)
    copy.start()
    length, width = slices.shape[1] // 8, pieces[0].shape[1]
    block = slices.shape[0] // 4
    extra = jnp.zeros((EXTRA_ROWS, width), F32)
    for index in range(4):
        held[2 * index * length : 2 * (index + 1) * length] = pieces[index][0 : 2 * length]
        extra = extra + pieces[index][2 * length :].astype(F32)
    extra = jnp.sum(extra, axis=0, keepdims=True)
    copy.wait()
    for index in range(4):
        outs[index][:, 0:width] = dot(slices[index * block : (index + 1) * block], held[...]).astype(BF16)
        lanes = lax.broadcasted_iota(jnp.int32, (block, width), 1)
        column = jnp.sum(jnp.where(lanes == features(place, index, block), extra, 0.0), axis=-1, keepdims=True)
        outs[index][:, width:] = jnp.broadcast_to(column, (block, GAIN_LANES)).astype(BF16)


def enc_product_call(place, slices, pieces):
    width = pieces[0].shape[1]
    return pl.pallas_call(
        enc_product_kernel,
        name="product_enc",
        cost_estimate=takes(3.5),
        out_shape=[jax.ShapeDtypeStruct((slices.shape[0] // 4, width + GAIN_LANES), BF16)] * 4,
        in_specs=[SMEM, ANY] + [VMEM] * 4,
        out_specs=[VMEM] * 4,
        scratch_shapes=[pltpu.VMEM((slices.shape[1], width), BF16), pltpu.VMEM(slices.shape, BF16), pltpu.SemaphoreType.DMA],
        compiler_params=PARAMS,
    )(place, streamed(slices), *pieces)


def finish_kernel(low, recv, weight, gain, rows, gain_out):
    count, width = weight.shape
    total = low[...].astype(F32)
    for part in recv:
        total = total + part[...].astype(F32)
    rows[...] = total[:, :width]
    column = jnp.sum(weight[...].astype(F32) * total[:, :width], axis=-1, keepdims=True) / gain[...]
    if low.shape[1] > width:
        column = column + total[:, width : width + 1]
    diagonal = lax.broadcasted_iota(jnp.int32, (count, count), 0) == lax.broadcasted_iota(
        jnp.int32, (count, count), 1
    )
    gain_out[...] = jnp.sum(jnp.where(diagonal, column, 0.0), axis=0, keepdims=True)


def finish_call(low, recv, weight, gain):
    count, width = weight.shape

    def kernel(low, *refs):
        finish_kernel(low, refs[: len(recv)], *refs[len(recv) :])

    return pl.pallas_call(
        kernel,
        name="finish_enc" if low.shape[1] > width else "finish_dec",
        out_shape=[jax.ShapeDtypeStruct((count, width), F32), jax.ShapeDtypeStruct((1, count), F32)],
        in_specs=[VMEM] * (3 + len(recv)),
        out_specs=[VMEM] * 2,
        compiler_params=PARAMS,
    )(low, *recv, weight, gain)


def device(pipe, high, deep, across):
    return pipe * 32 + (high % 2) * 16 + (deep % 4) * 4 + across % 4


def all_places():
    return [(pipe, high, deep, across) for pipe in range(4) for high in range(2) for deep in range(4) for across in range(4)]


def moved(place, along_x, step):
    pipe, high, deep, across = place
    return device(pipe, high, deep, across + step) if along_x else device(pipe, high, deep + step, across)


def gather_perm(step):
    return [(device(*place), moved(place, place[0] % 2 == 0, step)) for place in all_places()]


def reduce_perm(step):
    return [(device(*place), moved(place, place[0] % 2 == 1, step)) for place in all_places()]


HALF_PERM = [(device(*place), device(place[0], place[1] + 1, place[2], place[3])) for place in all_places()]
ASIDE_PERM = [(device(*place), device(place[0] ^ 1, place[1], place[2], place[3] + 1)) for place in all_places()]
SWAP_PERM = [(device(*place), device(place[0] ^ 1, *place[1:])) for place in all_places()]
UP_PERM = [
    (device(pipe, high, deep, across), device(pipe + 2, high + pipe, deep, across))
    for pipe, high, deep, across in all_places()
    if pipe < 2
]
DOWN_PERM = [(target, source) for source, target in UP_PERM]
FIRST_PERM = [(device(*place), device(place[0] + 1, *place[1:])) for place in all_places() if place[0] % 2 == 0]
OUT_PERMS = [
    [(device(1, high, deep, across), device(2 + core, high + core, deep, across)) for _, high, deep, across in all_places()[:32]]
    for core in range(2)
]


def send(value, perm):
    return lax.ppermute(value, ("pipe", "dp"), perm)


def gather(mine, other, extra=0):
    other = send(other, SWAP_PERM)
    if extra:
        rows = mine.shape[0] - extra
        whole = jnp.concatenate([mine[:rows], other[:rows], mine[rows:] + other[rows:]], axis=0)
    else:
        whole = jnp.concatenate([mine, other], axis=0)
    return [whole] + [send(whole, gather_perm(step)) for step in (2, 1, 3)]


def per_device(enc_in, dec_in, out_grad, enc_weight, dec_weight, enc_gain, dec_gain, mem_gain):
    pipe = lax.axis_index("pipe")
    spot = lax.axis_index("dp")
    core, upper = pipe % 2, pipe // 2
    high, deep, across = spot // 16, (spot // 4) % 4, spot % 4
    even = core == 0
    near, far = jnp.where(even, across, deep), jnp.where(even, deep, across)
    flags = jnp.stack([core, upper]).astype(jnp.int32)
    width = enc_weight.shape[1]
    mem_gain = mem_gain[None]

    def place_of(step, half):
        group, third = jnp.where(even, (far + step) % 4, near), jnp.where(even, near, (far + step) % 4)
        return ((high + half) % 2 * 16 + group * 4 + third) * (width // 32)

    place = jnp.stack([place_of(step, half) for step in range(4) for half in range(2)]).astype(jnp.int32)

    enc_own, dec_own = enc_weight[0], dec_weight[0]
    gains = jnp.concatenate([enc_gain, dec_gain], axis=0)
    gains_other = send(gains, ASIDE_PERM)
    pair = jnp.where(even, jnp.stack([gains, gains_other]), jnp.stack([gains_other, gains]))
    enc_gains, dec_gains = pair[:, 0], pair[:, 1]

    enc_other = send(enc_own, SWAP_PERM)
    x1 = send(first_call(0, flags, streamed(enc_in), enc_own, enc_gain), FIRST_PERM)
    x2 = first_call(1, flags, x1, enc_own, enc_gain, gains_other)
    received = [send(x2[sequence], OUT_PERMS[sequence]) for sequence in range(2)]
    enc_pair = load_call(None, flags, enc_own, enc_other, x2)
    memory, n_own, n_other, saved = enc_forward_call(flags, enc_in, *received, enc_pair, enc_gains, mem_gain)
    memory_recv = send(memory, DOWN_PERM)
    normed_pieces = gather(n_own, n_other)
    upstream = send(jnp.where(even, out_grad[0], out_grad[1]), UP_PERM)
    dec_other = send(dec_own, SWAP_PERM)
    dec_pair = load_call(0, flags, dec_own, dec_other, memory)
    ahead = dec_query_call(flags, dec_in, dec_pair, dec_gains)

    y2, dec_saved = dec_forward_call(flags, dec_in, memory_recv, ahead, dec_pair, dec_gains)
    dec_pair = load_call(1, flags, dec_own, dec_other, dec_saved)
    u2, source_mine, dec_done = dec_turn_call(flags, send(y2, UP_PERM), memory, upstream, dec_pair, dec_gains)
    dec_pair = load_call(0, flags, dec_own, dec_other, dec_done)
    source_low, dec_own_pay, dec_other_pay = dec_backward_call(
        flags, send(u2, DOWN_PERM), memory_recv, ahead, dec_saved, dec_pair, dec_gains, dec_done
    )
    dec_pieces = gather(dec_own_pay, dec_other_pay)
    enc_pair = load_call(None, flags, enc_own, enc_other, source_low)

    u_low, done0, done1 = enc_backward_first_call(
        flags, source_mine, send(source_low, UP_PERM), mem_gain, enc_pair, enc_gains, saved
    )
    dec_blocks = dec_product_call(place, dec_pieces, dec_own_pay)
    slices = choose_call(place, normed_pieces, u_low)
    own_pay, other_pay = enc_backward_last_call(
        flags, send(u_low, DOWN_PERM), done0, done1, enc_pair, enc_gains, saved, dec_blocks[0], slices
    )

    count = width // 32

    def rows_of(weight, gain):
        start = spot * count
        return (
            lax.dynamic_slice_in_dim(weight, start, count, 0),
            lax.dynamic_slice_in_dim(gain[0], start, count, 0)[:, None],
        )

    dec_sum = (dec_blocks[0].astype(F32) + send(dec_blocks[1], HALF_PERM).astype(F32)).astype(BF16)
    dec_parts = [dec_sum[step * count : (step + 1) * count] for step in range(4)]
    dec_recv = [send(dec_parts[step], reduce_perm(step)) for step in (1, 2, 3)]

    enc_blocks = enc_product_call(place, slices, gather(own_pay, other_pay, EXTRA_ROWS))
    enc_sum = enc_blocks[0].astype(F32)
    for step in (1, 2, 3):
        enc_sum = enc_sum + send(enc_blocks[step], reduce_perm(step)).astype(F32)
    enc_recv = send(enc_sum[count:].astype(BF16), HALF_PERM)

    dec_rows, dec_column = finish_call(dec_parts[0], dec_recv, *rows_of(dec_own, dec_gain))
    enc_rows, enc_column = finish_call(enc_sum[:count], [enc_recv], *rows_of(enc_own, enc_gain))
    return enc_rows[None], dec_rows[None], enc_column, dec_column


def solution(mesh):
    placed = (
        P("dp", None, None),
        P("dp", None, None),
        P("dp", None, None),
        P("pipe", None, None),
        P("pipe", None, None),
        P("pipe", None),
        P("pipe", None),
        P(),
    )
    return jax.shard_map(
        per_device,
        mesh=mesh,
        in_specs=placed,
        out_specs=(P("pipe", "dp", None), P("pipe", "dp", None), P("pipe", "dp"), P("pipe", "dp")),
        check_vma=False,
    )
```

```python
import functools

import jax
import jax.numpy as jnp
from jax import lax
from jax.experimental import pallas as pl
from jax.experimental.pallas import tpu as pltpu
from jax.sharding import PartitionSpec as P

HEAD_DIM = 256
EPSILON = 1e-06
QUERY_SCALE = 0.0625
EXTRA_ROWS = 16
GAIN_LANES = 128

BF16 = jnp.bfloat16
F32 = jnp.float32
def takes(microseconds):
    return pl.CostEstimate(flops=int(microseconds * 10**9), bytes_accessed=0, transcendentals=0)


ANY = pl.BlockSpec(memory_space=pl.ANY)
SMEM = pl.BlockSpec(memory_space=pltpu.SMEM)
VMEM = pl.BlockSpec(memory_space=pltpu.VMEM)
HBM = pl.BlockSpec(memory_space=pltpu.HBM)
PARAMS = pltpu.CompilerParams(vmem_limit_bytes=14 * 2**20)


def dot(left, right):
    return jnp.dot(left, right, preferred_element_type=F32)


def dot_nt(left, right):
    return lax.dot_general(left, right, (((1,), (1,)), ((), ())), preferred_element_type=F32)


def dot_tn(left, right):
    return lax.dot_general(left, right, (((0,), (0,)), ((), ())), preferred_element_type=F32)


def row_scale(values):
    return lax.rsqrt(jnp.mean(values * values, axis=-1, keepdims=True) + EPSILON)


def head(index):
    return slice(index * HEAD_DIM, (index + 1) * HEAD_DIM)


def normal(x, gain):
    hidden = x[...].astype(F32)
    return (hidden * row_scale(hidden) * gain).astype(BF16)


def attend_forward(x, query, source, out):
    heads = [head(part) for part in range(x.shape[-1] // HEAD_DIM)]
    raised = [jnp.exp(dot_nt(query[:, cols], source[:, cols])) for cols in heads]
    low = [(value / jnp.sum(value, axis=-1, keepdims=True)).astype(BF16) for value in raised]
    for cols, shares in zip(heads, low):
        out[:, cols] = (x[:, cols].astype(F32) + dot(shares, source[:, cols])).astype(BF16)


def queries_of(weight, normed, query):
    query[...] = (dot(normed[...], weight[...]) * QUERY_SCALE).astype(BF16)


def attend_backward(source, query, upstream, grad_query, grad_source, add):
    heads = [head(part) for part in range(source.shape[-1] // HEAD_DIM)]
    length = query.shape[0]
    if length % 128 == 0:
        sides = [jnp.concatenate([query[:, cols], upstream[:, cols]], axis=0) for cols in heads]
        both = [dot_nt(source[:, cols], side) for cols, side in zip(heads, sides)]
        raised = [jnp.exp(value[:, :length]) for value in both]
        grads = [value[:, length:] for value in both]
    else:
        raised = [jnp.exp(dot_nt(source[:, cols], query[:, cols])) for cols in heads]
        grads = [dot_nt(source[:, cols], upstream[:, cols]) for cols in heads]
    probs = [value / jnp.sum(value, axis=0, keepdims=True) for value in raised]
    scores = [
        (share * (grad - jnp.sum(grad * share, axis=0, keepdims=True))).astype(BF16) for share, grad in zip(probs, grads)
    ]
    for part, cols in enumerate(heads):
        low = probs[part].astype(BF16)
        grad_query[:, cols] = (dot_tn(scores[part], source[:, cols]) * QUERY_SCALE).astype(BF16)
        if length % 128 == 0:
            total = dot(jnp.concatenate([scores[part], low], axis=1), sides[part])
        else:
            total = dot(scores[part], query[:, cols]) + dot(low, upstream[:, cols])
        grad_source[:, cols] = grad_source[:, cols] + total if add else total


def grad_normed(weight, grad_query, scaled):
    for part in range(grad_query.shape[1] // HEAD_DIM):
        cols = head(part)
        scaled[:, cols] = dot_nt(weight[cols, :], grad_query[...]).T


def input_backward(x, gain, grad_source, upstream, scaled, out):
    hidden = x[...].astype(F32)
    scales = row_scale(hidden)
    grad = scaled[...] if grad_source is None else scaled[...] + grad_source[...]
    grad = gain * grad
    mean = jnp.mean(grad * hidden, axis=-1, keepdims=True)
    factor = scales * scales * scales * mean
    out[...] = (upstream[...].astype(F32) + scales * grad - hidden * factor).astype(BF16)


def dec_input_backward(weight, x, gain, grad_query, upstream, scaled, out):
    grad_normed(weight, grad_query, scaled)
    input_backward(x, gain, None, upstream, scaled, out)


def gain_row(x, grad_source):
    hidden = x[...].astype(F32)
    return jnp.sum(grad_source[...] * hidden * row_scale(hidden), axis=0, keepdims=True)


def by_core(core, low, high, own, other):
    for mine in (0, 1):

        @pl.when(core == mine)
        def _():
            own[...] = high[...] if mine else low[...]
            other[...] = low[...] if mine else high[...]


def load_kernel(role, flags, own, other, gate, pair, sems):
    def body():
        copies = [pltpu.make_async_copy(part, pair.at[slot], sems.at[slot]) for slot, part in enumerate((own, other))]
        for copy in copies:
            copy.start()
        for copy in copies:
            copy.wait()

    if role is None:
        body()
    else:
        pl.when(flags[1] == role)(body)


def load_call(role, flags, own, other, gate):
    pair = pl.pallas_call(
        functools.partial(load_kernel, role),
        name="load_weights",
        cost_estimate=takes(4),
        out_shape=pltpu.VMEM((2,) + own.shape, BF16),
        in_specs=[SMEM] + [ANY] * 3,
        out_specs=VMEM,
        scratch_shapes=[pltpu.SemaphoreType.DMA((2,))],
        compiler_params=PARAMS,
    )(flags, streamed(own), streamed(other), gate)
    return pinned(pair)


def streamed(value):
    return pltpu.with_memory_space_constraint(value, pltpu.HBM)


def pinned(value):
    return pltpu.with_memory_space_constraint(value, pltpu.VMEM)


def both_sequences(x, normed, query, out):
    count, length, width = x.shape
    for sequence in range(count):
        rows = pl.ds(sequence * length, length)
        attend_forward(x.at[sequence], query.at[rows], normed.at[rows], out.at[sequence])


def both_normal(x, gain, normed):
    count, length, width = x.shape
    for sequence in range(count):
        normed[sequence * length : (sequence + 1) * length] = normal(x.at[sequence], gain[...])


def first_kernel(turn, flags, x_any, weight_any, gain, *refs):
    out, x, weight, normed, query, x_sem, sems = refs[-7:]

    @pl.when(jnp.logical_and(flags[0] == turn, flags[1] == 0))
    def _():
        parts = range(x.shape[-1] // HEAD_DIM)
        rows = pltpu.make_async_copy(x_any, x, x_sem)
        rows.start()
        copies = [
            pltpu.make_async_copy(weight_any.at[:, head(part)], weight.at[:, head(part)], sems.at[part]) for part in parts
        ]
        for copy in copies:
            copy.start()
        rows.wait()
        both_normal(x, gain, normed)
        middle = len(parts) // 2
        for half in (parts[:middle], parts[middle:]):
            for part in half:
                copies[part].wait()
            for part in half:
                query[:, head(part)] = (dot(normed[...], weight[:, head(part)]) * QUERY_SCALE).astype(BF16)
        both_sequences(x, normed, query, out)

def first_call(turn, flags, x, weight, gain, *gates):
    count, length, width = x.shape
    return pl.pallas_call(
        functools.partial(first_kernel, turn),
        name="enc_first_lower" if turn == 0 else "enc_first_upper",
        cost_estimate=takes(6),
        out_shape=jax.ShapeDtypeStruct(x.shape, BF16),
        in_specs=[SMEM, ANY, ANY, VMEM] + [ANY] * len(gates),
        out_specs=VMEM,
        scratch_shapes=[pltpu.VMEM(x.shape, BF16), pltpu.VMEM((width, width), BF16)]
        + [pltpu.VMEM((count * length, width), BF16)] * 2
        + [pltpu.SemaphoreType.DMA, pltpu.SemaphoreType.DMA((width // HEAD_DIM,))],
        compiler_params=PARAMS,
    )(flags, x, streamed(weight), gain, *gates)


def enc_forward_kernel(
    flags, x_any, recv0, recv1, pair, gains, mem_gain, mem, n_own, n_other, saved, sem
):
    core, upper = flags[0], flags[1]
    x0, x1, x2, n0, n1, q0, q1 = [saved.at[place] for place in range(7)]

    @pl.when(upper == 0)
    def _():
        pltpu.make_async_copy(x_any.at[core], x0, sem).start()

    for mine, received in enumerate((recv0, recv1)):

        @pl.when(jnp.logical_and(upper == 1, core == mine))
        def _():
            pltpu.make_async_copy(received, x0, sem).start()

    pltpu.make_async_copy(recv0, x0, sem).wait()
    n0[...] = normal(x0, gains[0:1])
    queries_of(pair.at[core], n0, q0)
    attend_forward(x0, q0, n0, x1)
    n1[...] = normal(x1, gains[1:2])
    queries_of(pair.at[1 - core], n1, q1)
    attend_forward(x1, q1, n1, x2)
    mem[...] = normal(x2, mem_gain[...])
    by_core(core, n0, n1, n_own, n_other)


def enc_forward_call(flags, x, recv0, recv1, pair, gains, mem_gain):
    row = jax.ShapeDtypeStruct(recv0.shape, BF16)
    return pl.pallas_call(
        enc_forward_kernel,
        name="enc_forward",
        cost_estimate=takes(5.3),
        out_shape=[row] * 3 + [jax.ShapeDtypeStruct((7,) + recv0.shape, BF16)],
        in_specs=[SMEM, ANY, ANY, ANY] + [VMEM] * 3,
        out_specs=[VMEM] * 4,
        scratch_shapes=[pltpu.SemaphoreType.DMA],
        compiler_params=PARAMS,
    )(flags, streamed(x), recv0, recv1, pair, gains, mem_gain)


def dec_query_kernel(flags, x_any, pair, gains, ahead, sem, y0):
    core, upper = flags[0], flags[1]
    n0, q0 = ahead.at[0], ahead.at[1]

    @pl.when(upper == 0)
    def _():
        rows = pltpu.make_async_copy(x_any.at[core], y0, sem)
        rows.start()
        rows.wait()
        n0[...] = normal(y0, gains[0:1])
        queries_of(pair.at[core], n0, q0)


def dec_query_call(flags, x, pair, gains):
    return pl.pallas_call(
        dec_query_kernel,
        name="dec_query",
        cost_estimate=takes(2.4),
        out_shape=jax.ShapeDtypeStruct((2,) + x.shape[1:], BF16),
        in_specs=[SMEM, ANY, VMEM, VMEM],
        out_specs=VMEM,
        scratch_shapes=[pltpu.SemaphoreType.DMA, pltpu.VMEM(x.shape[1:], BF16)],
        compiler_params=PARAMS,
    )(flags, x, pair, gains)


def dec_forward_kernel(flags, x_any, memory, ahead, pair, gains, y2, saved, sem, y0):
    core, upper = flags[0], flags[1]
    q0 = ahead.at[1]
    y1, n1, q1 = [saved.at[place] for place in range(3)]

    @pl.when(upper == 0)
    def _():
        rows = pltpu.make_async_copy(x_any.at[core], y0, sem)
        rows.start()
        rows.wait()
        attend_forward(y0, q0, memory, y1)
        n1[...] = normal(y1, gains[1:2])
        queries_of(pair.at[1 - core], n1, q1)
        attend_forward(y1, q1, memory, y2)


def dec_forward_call(flags, x, memory, ahead, pair, gains):
    row = jax.ShapeDtypeStruct(x.shape[1:], BF16)
    return pl.pallas_call(
        dec_forward_kernel,
        name="dec_forward",
        cost_estimate=takes(3.3),
        out_shape=[row, jax.ShapeDtypeStruct((3,) + x.shape[1:], BF16)],
        in_specs=[SMEM, ANY] + [VMEM] * 4,
        out_specs=[VMEM] * 2,
        scratch_shapes=[pltpu.SemaphoreType.DMA, pltpu.VMEM(x.shape[1:], BF16)],
        compiler_params=PARAMS,
    )(flags, x, memory, ahead, pair, gains)


def dec_turn_kernel(
    flags, y2, memory, upstream, pair, gains, out, grad_source, pays, n0, n1, y3, u3, q0, q1, dq0, dq1, scaled
):
    core, upper = flags[0], flags[1]

    @pl.when(upper == 1)
    def _():
        length = y2.shape[0]
        n0[...] = normal(y2, gains[0:1])
        queries_of(pair.at[core], n0, q0)
        attend_forward(y2, q0, memory, y3)
        n1[...] = normal(y3, gains[1:2])
        queries_of(pair.at[1 - core], n1, q1)
        attend_backward(memory, q1, upstream, dq1, grad_source, False)
        dec_input_backward(pair.at[1 - core], y3, gains[1:2], dq1, upstream, scaled, u3)
        attend_backward(memory, q0, u3, dq0, grad_source, True)
        dec_input_backward(pair.at[core], y2, gains[0:1], dq0, u3, scaled, out)
        for payload, normed, grad in ((pays.at[0], n0, dq0), (pays.at[1], n1, dq1)):
            payload[0:length] = normed[...]
            payload[length:] = grad[...]


def dec_turn_call(flags, y2, memory, upstream, pair, gains):
    length, width = y2.shape
    row = jax.ShapeDtypeStruct((length, width), BF16)
    payload = jax.ShapeDtypeStruct((2, 2 * length, width), BF16)
    held = pltpu.VMEM((length, width), BF16)
    return pl.pallas_call(
        dec_turn_kernel,
        name="dec_turn",
        cost_estimate=takes(11),
        out_shape=[row, jax.ShapeDtypeStruct(memory.shape, F32), payload],
        in_specs=[SMEM] + [VMEM] * 5,
        out_specs=[VMEM] * 3,
        scratch_shapes=[held] * 8 + [pltpu.VMEM((length, width), F32)],
        compiler_params=PARAMS,
    )(flags, y2, memory, upstream, pair, gains)


def dec_backward_kernel(
    flags, upstream, memory, ahead, saved, pair, gains, done, source_low, out_own, out_other, u1, dq0, dq1, grad_source, scaled, pay0, pay1
):
    core, upper = flags[0], flags[1]
    n0, q0 = ahead.at[0], ahead.at[1]
    y1, n1, q1 = [saved.at[place] for place in range(3)]

    @pl.when(upper == 0)
    def _():
        length = y1.shape[0]
        attend_backward(memory, q1, upstream, dq1, grad_source, False)
        dec_input_backward(pair.at[1 - core], y1, gains[1:2], dq1, upstream, scaled, u1)
        attend_backward(memory, q0, u1, dq0, grad_source, True)
        source_low[...] = grad_source[...].astype(BF16)
        for payload, normed, grad in ((pay0, n0, dq0), (pay1, n1, dq1)):
            payload[0:length] = normed[...]
            payload[length:] = grad[...]
        by_core(core, pay0, pay1, out_own, out_other)

    @pl.when(upper == 1)
    def _():
        by_core(core, done.at[0], done.at[1], out_own, out_other)


def dec_backward_call(flags, upstream, memory, ahead, saved, pair, gains, done):
    length, width = upstream.shape
    payload = jax.ShapeDtypeStruct((2 * length, width), BF16)
    held = pltpu.VMEM((length, width), BF16)
    return pl.pallas_call(
        dec_backward_kernel,
        name="dec_backward",
        cost_estimate=takes(5.5),
        out_shape=[jax.ShapeDtypeStruct(memory.shape, BF16), payload, payload],
        in_specs=[SMEM] + [VMEM] * 7,
        out_specs=[VMEM] * 3,
        scratch_shapes=[held] * 3
        + [pltpu.VMEM(memory.shape, F32), pltpu.VMEM((length, width), F32)]
        + [pltpu.VMEM(payload.shape, BF16)] * 2,
        compiler_params=PARAMS,
    )(flags, upstream, memory, ahead, saved, pair, gains, done)


def put_payload(core, payload, grad_query, x, grad_source):
    length, width = grad_query.shape
    payload[0:length] = grad_query[...]
    place = lax.broadcasted_iota(jnp.int32, (EXTRA_ROWS, width), 0)
    payload[length:] = jnp.where(place == core, gain_row(x, grad_source), 0.0).astype(BF16)


def enc_backward_first_kernel(
    flags, source_mine, source_recv, mem_gain, pair, gains, saved, out, pay0, pay1, u2, u1, grad_query, grad_source, scaled
):
    x0, x1, x2, n0, n1, q0, q1 = [saved.at[place] for place in range(7)]
    core, upper = flags[0], flags[1]

    @pl.when(upper == 1)
    def _():
        hidden = x2[...].astype(F32)
        scales = row_scale(hidden)
        grad = mem_gain[...] * (source_mine[...] + source_recv[...].astype(F32))
        mean = jnp.mean(grad * hidden, axis=-1, keepdims=True)
        u2[...] = (scales * grad - hidden * (scales * scales * scales * mean)).astype(BF16)
        attend_backward(n1, q1, u2, grad_query, grad_source, False)
        put_payload(core, pay1, grad_query, x1, grad_source)
        grad_normed(pair.at[1 - core], grad_query, scaled)
        input_backward(x1, gains[1:2], grad_source, u2, scaled, u1)
        attend_backward(n0, q0, u1, grad_query, grad_source, False)
        put_payload(core, pay0, grad_query, x0, grad_source)
        grad_normed(pair.at[core], grad_query, scaled)
        input_backward(x0, gains[0:1], grad_source, u1, scaled, out)


def enc_backward_first_call(flags, source_mine, source_recv, mem_gain, pair, gains, saved):
    length, width = saved.shape[1:]
    row = jax.ShapeDtypeStruct((length, width), BF16)
    payload = jax.ShapeDtypeStruct((length + EXTRA_ROWS, width), BF16)
    return pl.pallas_call(
        enc_backward_first_kernel,
        name="enc_backward_first",
        cost_estimate=takes(10),
        out_shape=[row, payload, payload],
        in_specs=[SMEM] + [VMEM] * 3 + [VMEM] * 3,
        out_specs=[VMEM] * 3,
        scratch_shapes=[pltpu.VMEM((length, width), BF16)] * 3
        + [pltpu.VMEM((length, width), F32)] * 2,
        compiler_params=PARAMS,
    )(flags, source_mine, source_recv, mem_gain, pair, gains, saved)


def enc_backward_last_kernel(
    flags, upstream, done0, done1, pair, gains, saved, gate, later_gate, out_own, out_other, pay0, pay1, u1, grad_query, grad_source, scaled
):
    x0, x1, _, n0, n1, q0, q1 = [saved.at[place] for place in range(7)]
    core, upper = flags[0], flags[1]

    @pl.when(upper == 0)
    def _():
        attend_backward(n1, q1, upstream, grad_query, grad_source, False)
        put_payload(core, pay1, grad_query, x1, grad_source)
        grad_normed(pair.at[1 - core], grad_query, scaled)
        input_backward(x1, gains[1:2], grad_source, upstream, scaled, u1)
        attend_backward(n0, q0, u1, grad_query, grad_source, False)
        put_payload(core, pay0, grad_query, x0, grad_source)
        by_core(core, pay0, pay1, out_own, out_other)

    @pl.when(upper == 1)
    def _():
        by_core(core, done0, done1, out_own, out_other)


def enc_backward_last_call(flags, upstream, done0, done1, pair, gains, saved, *gates):
    length, width = upstream.shape
    payload = jax.ShapeDtypeStruct((length + EXTRA_ROWS, width), BF16)
    return pl.pallas_call(
        enc_backward_last_kernel,
        name="enc_backward_last",
        cost_estimate=takes(7),
        out_shape=[payload, payload],
        in_specs=[SMEM] + [VMEM] * 3 + [VMEM] * 3 + [ANY] * 2,
        out_specs=[VMEM] * 2,
        scratch_shapes=[pltpu.VMEM(payload.shape, BF16)] * 2
        + [pltpu.VMEM((length, width), BF16)] * 2
        + [pltpu.VMEM((length, width), F32)] * 2,
        compiler_params=PARAMS,
    )(flags, upstream, done0, done1, pair, gains, saved, *gates)


def features(place, index, block):
    row = lax.broadcasted_iota(jnp.int32, (block, 1), 0)
    half = block // 2
    return jnp.where(row < half, place[index * 2] + row, place[index * 2 + 1] + row - half)


def ones_at(place, index, block, width):
    lanes = lax.broadcasted_iota(jnp.int32, (block, width), 1)
    return jnp.where(lanes == features(place, index, block), 1.0, 0.0).astype(BF16)


def choose_kernel(place, *refs):
    pieces, out, (ones,) = refs[:4], refs[5], refs[6:]
    rows, width = pieces[0].shape
    block = out.shape[0] // 4
    for index in range(4):
        ones[index * block : (index + 1) * block] = ones_at(place, index, block, width)
    for index in range(4):
        out[:, index * rows : (index + 1) * rows] = dot_nt(ones[...], pieces[index][...]).astype(BF16)


def choose_call(place, pieces, gate):
    rows, width = pieces[0].shape
    return pl.pallas_call(
        choose_kernel,
        name="choose_enc",
        cost_estimate=takes(4.3),
        out_shape=jax.ShapeDtypeStruct((width // 4, 4 * rows), BF16),
        in_specs=[SMEM] + [VMEM] * 4 + [ANY],
        out_specs=VMEM,
        scratch_shapes=[pltpu.VMEM((width // 4, width), BF16)],
        compiler_params=PARAMS,
    )(place, *pieces, gate)


def dec_product_kernel(place, *refs):
    pieces, outs, (normed, grads) = refs[:4], refs[5:7], refs[7:]
    length = pieces[0].shape[0] // 4
    for index in range(8):
        start = index % 2 * 2 * length
        normed[index * length : (index + 1) * length] = pieces[index // 2][start : start + length]
        grads[index * length : (index + 1) * length] = pieces[index // 2][start + length : start + 2 * length]
    half = outs[0].shape[0] // 4
    for index in range(4):
        columns = dot_nt(ones_at(place, index, 2 * half, normed.shape[1]), normed[...]).astype(BF16)
        product = dot(columns, grads[...]).astype(BF16)
        for side in range(2):
            outs[side][index * half : (index + 1) * half] = product[side * half : (side + 1) * half]


def dec_product_call(place, pieces, gate):
    rows, width = pieces[0].shape
    return pl.pallas_call(
        dec_product_kernel,
        name="product_dec",
        cost_estimate=takes(4.4),
        out_shape=[jax.ShapeDtypeStruct((width // 8, width), BF16)] * 2,
        in_specs=[SMEM] + [VMEM] * 4 + [ANY],
        out_specs=[VMEM] * 2,
        scratch_shapes=[pltpu.VMEM((2 * rows, width), BF16)] * 2,
        compiler_params=PARAMS,
    )(place, *pieces, gate)


def enc_product_kernel(place, slices_any, *refs):
    pieces, outs, (held, slices, sem) = refs[:4], refs[4:8], refs[8:]
    copy = pltpu.make_async_copy(slices_any, slices, sem)
    copy.start()
    length, width = slices.shape[1] // 8, pieces[0].shape[1]
    block = slices.shape[0] // 4
    extra = jnp.zeros((EXTRA_ROWS, width), F32)
    for index in range(4):
        held[2 * index * length : 2 * (index + 1) * length] = pieces[index][0 : 2 * length]
        extra = extra + pieces[index][2 * length :].astype(F32)
    extra = jnp.sum(extra, axis=0, keepdims=True)
    copy.wait()
    for index in range(4):
        outs[index][:, 0:width] = dot(slices[index * block : (index + 1) * block], held[...]).astype(BF16)
        lanes = lax.broadcasted_iota(jnp.int32, (block, width), 1)
        column = jnp.sum(jnp.where(lanes == features(place, index, block), extra, 0.0), axis=-1, keepdims=True)
        outs[index][:, width:] = jnp.broadcast_to(column, (block, GAIN_LANES)).astype(BF16)


def enc_product_call(place, slices, pieces):
    width = pieces[0].shape[1]
    return pl.pallas_call(
        enc_product_kernel,
        name="product_enc",
        cost_estimate=takes(3.5),
        out_shape=[jax.ShapeDtypeStruct((slices.shape[0] // 4, width + GAIN_LANES), BF16)] * 4,
        in_specs=[SMEM, ANY] + [VMEM] * 4,
        out_specs=[VMEM] * 4,
        scratch_shapes=[pltpu.VMEM((slices.shape[1], width), BF16), pltpu.VMEM(slices.shape, BF16), pltpu.SemaphoreType.DMA],
        compiler_params=PARAMS,
    )(place, streamed(slices), *pieces)


def finish_kernel(low, recv, weight, gain, rows, gain_out):
    count, width = weight.shape
    total = low[...].astype(F32)
    for part in recv:
        total = total + part[...].astype(F32)
    rows[...] = total[:, :width]
    column = jnp.sum(weight[...].astype(F32) * total[:, :width], axis=-1, keepdims=True) / gain[...]
    if low.shape[1] > width:
        column = column + total[:, width : width + 1]
    diagonal = lax.broadcasted_iota(jnp.int32, (count, count), 0) == lax.broadcasted_iota(
        jnp.int32, (count, count), 1
    )
    gain_out[...] = jnp.sum(jnp.where(diagonal, column, 0.0), axis=0, keepdims=True)


def finish_call(low, recv, weight, gain):
    count, width = weight.shape

    def kernel(low, *refs):
        finish_kernel(low, refs[: len(recv)], *refs[len(recv) :])

    return pl.pallas_call(
        kernel,
        name="finish_enc" if low.shape[1] > width else "finish_dec",
        out_shape=[jax.ShapeDtypeStruct((count, width), F32), jax.ShapeDtypeStruct((1, count), F32)],
        in_specs=[VMEM] * (3 + len(recv)),
        out_specs=[VMEM] * 2,
        compiler_params=PARAMS,
    )(low, *recv, weight, gain)


def device(pipe, high, deep, across):
    return pipe * 32 + (high % 2) * 16 + (deep % 4) * 4 + across % 4


def all_places():
    return [(pipe, high, deep, across) for pipe in range(4) for high in range(2) for deep in range(4) for across in range(4)]


def moved(place, along_x, step):
    pipe, high, deep, across = place
    return device(pipe, high, deep, across + step) if along_x else device(pipe, high, deep + step, across)


def gather_perm(step):
    return [(device(*place), moved(place, place[0] % 2 == 0, step)) for place in all_places()]


def reduce_perm(step):
    return [(device(*place), moved(place, place[0] % 2 == 1, step)) for place in all_places()]


HALF_PERM = [(device(*place), device(place[0], place[1] + 1, place[2], place[3])) for place in all_places()]
ASIDE_PERM = [(device(*place), device(place[0] ^ 1, place[1], place[2], place[3] + 1)) for place in all_places()]
SWAP_PERM = [(device(*place), device(place[0] ^ 1, *place[1:])) for place in all_places()]
UP_PERM = [
    (device(pipe, high, deep, across), device(pipe + 2, high + pipe, deep, across))
    for pipe, high, deep, across in all_places()
    if pipe < 2
]
DOWN_PERM = [(target, source) for source, target in UP_PERM]
FIRST_PERM = [(device(*place), device(place[0] + 1, *place[1:])) for place in all_places() if place[0] % 2 == 0]
OUT_PERMS = [
    [(device(1, high, deep, across), device(2 + core, high + core, deep, across)) for _, high, deep, across in all_places()[:32]]
    for core in range(2)
]


def send(value, perm):
    return lax.ppermute(value, ("pipe", "dp"), perm)


def gather(mine, other, extra=0):
    other = send(other, SWAP_PERM)
    if extra:
        rows = mine.shape[0] - extra
        whole = jnp.concatenate([mine[:rows], other[:rows], mine[rows:] + other[rows:]], axis=0)
    else:
        whole = jnp.concatenate([mine, other], axis=0)
    return [whole] + [send(whole, gather_perm(step)) for step in (2, 1, 3)]


def per_device(enc_in, dec_in, out_grad, enc_weight, dec_weight, enc_gain, dec_gain, mem_gain):
    pipe = lax.axis_index("pipe")
    spot = lax.axis_index("dp")
    core, upper = pipe % 2, pipe // 2
    high, deep, across = spot // 16, (spot // 4) % 4, spot % 4
    even = core == 0
    near, far = jnp.where(even, across, deep), jnp.where(even, deep, across)
    flags = jnp.stack([core, upper]).astype(jnp.int32)
    width = enc_weight.shape[1]
    mem_gain = mem_gain[None]

    def place_of(step, half):
        group, third = jnp.where(even, (far + step) % 4, near), jnp.where(even, near, (far + step) % 4)
        return ((high + half) % 2 * 16 + group * 4 + third) * (width // 32)

    place = jnp.stack([place_of(step, half) for step in range(4) for half in range(2)]).astype(jnp.int32)

    enc_own, dec_own = enc_weight[0], dec_weight[0]
    gains = jnp.concatenate([enc_gain, dec_gain], axis=0)
    gains_other = send(gains, ASIDE_PERM)
    pair = jnp.where(even, jnp.stack([gains, gains_other]), jnp.stack([gains_other, gains]))
    enc_gains, dec_gains = pair[:, 0], pair[:, 1]

    enc_other = send(enc_own, SWAP_PERM)
    x1 = send(first_call(0, flags, streamed(enc_in), enc_own, enc_gain), FIRST_PERM)
    x2 = first_call(1, flags, x1, enc_own, enc_gain, gains_other)
    received = [send(x2[sequence], OUT_PERMS[sequence]) for sequence in range(2)]
    enc_pair = load_call(None, flags, enc_own, enc_other, x2)
    memory, n_own, n_other, saved = enc_forward_call(flags, enc_in, *received, enc_pair, enc_gains, mem_gain)
    memory_recv = send(memory, DOWN_PERM)
    normed_pieces = gather(n_own, n_other)
    upstream = send(jnp.where(even, out_grad[0], out_grad[1]), UP_PERM)
    dec_other = send(dec_own, SWAP_PERM)
    dec_pair = load_call(0, flags, dec_own, dec_other, memory)
    ahead = dec_query_call(flags, dec_in, dec_pair, dec_gains)

    y2, dec_saved = dec_forward_call(flags, dec_in, memory_recv, ahead, dec_pair, dec_gains)
    dec_pair = load_call(1, flags, dec_own, dec_other, dec_saved)
    u2, source_mine, dec_done = dec_turn_call(flags, send(y2, UP_PERM), memory, upstream, dec_pair, dec_gains)
    dec_pair = load_call(0, flags, dec_own, dec_other, dec_done)
    source_low, dec_own_pay, dec_other_pay = dec_backward_call(
        flags, send(u2, DOWN_PERM), memory_recv, ahead, dec_saved, dec_pair, dec_gains, dec_done
    )
    dec_pieces = gather(dec_own_pay, dec_other_pay)
    enc_pair = load_call(1, flags, enc_own, enc_other, source_low)

    u_low, done0, done1 = enc_backward_first_call(
        flags, source_mine, send(source_low, UP_PERM), mem_gain, enc_pair, enc_gains, saved
    )
    dec_blocks = dec_product_call(place, dec_pieces, dec_own_pay)
    slices = choose_call(place, normed_pieces, u_low)
    enc_pair = load_call(0, flags, enc_own, enc_other, slices)
    own_pay, other_pay = enc_backward_last_call(
        flags, send(u_low, DOWN_PERM), done0, done1, enc_pair, enc_gains, saved, dec_blocks[0], slices
    )

    count = width // 32

    def rows_of(weight, gain):
        start = spot * count
        return (
            lax.dynamic_slice_in_dim(weight, start, count, 0),
            lax.dynamic_slice_in_dim(gain[0], start, count, 0)[:, None],
        )

    dec_sum = (dec_blocks[0].astype(F32) + send(dec_blocks[1], HALF_PERM).astype(F32)).astype(BF16)
    dec_parts = [dec_sum[step * count : (step + 1) * count] for step in range(4)]
    dec_recv = [send(dec_parts[step], reduce_perm(step)) for step in (1, 2, 3)]

    enc_blocks = enc_product_call(place, slices, gather(own_pay, other_pay, EXTRA_ROWS))
    enc_sum = enc_blocks[0].astype(F32)
    for step in (1, 2, 3):
        enc_sum = enc_sum + send(enc_blocks[step], reduce_perm(step)).astype(F32)
    enc_recv = send(enc_sum[count:].astype(BF16), HALF_PERM)

    dec_rows, dec_column = finish_call(dec_parts[0], dec_recv, *rows_of(dec_own, dec_gain))
    enc_rows, enc_column = finish_call(enc_sum[:count], [enc_recv], *rows_of(enc_own, enc_gain))
    return enc_rows[None], dec_rows[None], enc_column, dec_column


def solution(mesh):
    placed = (
        P("dp", None, None),
        P("dp", None, None),
        P("dp", None, None),
        P("pipe", None, None),
        P("pipe", None, None),
        P("pipe", None),
        P("pipe", None),
        P(),
    )
    return jax.shard_map(
        per_device,
        mesh=mesh,
        in_specs=placed,
        out_specs=(P("pipe", "dp", None), P("pipe", "dp", None), P("pipe", "dp"), P("pipe", "dp")),
        check_vma=False,
    )
```
